32 devices in a mesh: dp: 8 (over z, y), tensor: 4 (over x, core).
Axes of the slice: x: 2, y: 2, z: 4, core: 2. Of those that a mesh axis runs over, the one named last changes fastest.
Arguments:
- tokens: bfloat16 [32, 256, 768], P(('dp', 'tensor')), may hold values from -6 to 6
- memory: bfloat16 [32, 1024, 768], P(('dp', 'tensor')), may hold values from -6 to 6
- cotangent: bfloat16 [32, 256, 768], P(('dp', 'tensor')), may hold values from -6 to 6
- lengths: int32 [32], P('dp'), may hold values from 64 to 256, as said below
- memory_mask: int32 [32, 1024], P('dp'), may hold values from 0 to 1, as said below
- token_tags: int32 [32, 256], P(('dp', 'tensor')), may hold values 0 or 1
- embedding: bfloat16 [2, 768], replicated, may hold values from -3 to 3
- gain_self: bfloat16 [768], replicated, may hold values from 0.25 to 1.75
- gain_cross: bfloat16 [768], replicated, may hold values from 0.25 to 1.75
- gain_hidden: bfloat16 [768], replicated, may hold values from 0.25 to 1.75
- self_query: bfloat16 [768, 768], P(None, 'tensor'), may hold values from -0.21875 to 0.21875
- self_key: bfloat16 [768, 768], P(None, 'tensor'), may hold values from -0.21875 to 0.21875
- self_value: bfloat16 [768, 768], P(None, 'tensor'), may hold values from -0.21875 to 0.21875
- self_output: bfloat16 [768, 768], P('tensor'), may hold values from -0.875 to 0.875
- position_bias: bfloat16 [32, 12], P(None, 'tensor'), may hold values from -4 to 4
- cross_query: bfloat16 [768, 768], P(None, 'tensor'), may hold values from -0.21875 to 0.21875
- cross_key: bfloat16 [768, 768], P(None, 'tensor'), may hold values from -0.21875 to 0.21875
- cross_value: bfloat16 [768, 768], P(None, 'tensor'), may hold values from -0.21875 to 0.21875
- cross_output: bfloat16 [768, 768], P('tensor'), may hold values from -1.25 to 1.25
- hidden_in: bfloat16 [768, 3072], P(None, 'tensor'), may hold values from -0.21875 to 0.21875
- hidden_out: bfloat16 [3072, 768], P('tensor'), may hold values from -0.15625 to 0.15625
Outputs:
- layer_out: bfloat16 [32, 256, 768], P(('dp', 'tensor'))
- grad_tokens: bfloat16 [32, 256, 768], P(('dp', 'tensor'))
- grad_memory: bfloat16 [32, 1024, 768], P(('dp', 'tensor'))
- grad_embedding: float32 [2, 768], replicated
- grad_gain_self: float32 [768], replicated
- grad_gain_cross: float32 [768], replicated
- grad_gain_hidden: float32 [768], replicated
- grad_self_query: float32 [768, 768], P(None, 'tensor')
- grad_self_key: float32 [768, 768], P(None, 'tensor')
- grad_self_value: float32 [768, 768], P(None, 'tensor')
- grad_self_output: float32 [768, 768], P('tensor')
- grad_position_bias: float32 [32, 12], P(None, 'tensor')
- grad_cross_query: float32 [768, 768], P(None, 'tensor')
- grad_cross_key: float32 [768, 768], P(None, 'tensor')
- grad_cross_value: float32 [768, 768], P(None, 'tensor')
- grad_cross_output: float32 [768, 768], P('tensor')
- grad_hidden_in: float32 [768, 3072], P(None, 'tensor')
- grad_hidden_out: float32 [3072, 768], P('tensor')
The draws below stay inside these ranges and needn't reach their ends.
Inputs may be any that keep to these rules, and one draw needn't show every extreme that they name: `lengths`: in each aligned block of 4 items one item has length 256; the others are at least 64. `memory_mask`: each row is 1 on a leading run of 256 to 1024 positions and 0 after it; in each aligned block of 4 items one row is all ones.
All inputs are finite; a program needn't handle non-finite values. No bound on the sum of `token_tags` on one device may be relied on, other than what follows from the above.
Results may differ from the reference program's by a relative error of at most 0.03.
Values may be sent and summed in bfloat16 or wider, within the bound.
A program may use at most 128 MiB of HBM per device.

```python
import math
import jax
import jax.numpy as jnp
import numpy as np
from jax import lax

D = 768
HEADS = 12
HEAD_DIM = 64
FF = 3072
BUCKETS = 32
MAX_DISTANCE = 128
DEC_LEN = 256
ENC_LEN = 1024
ITEMS_DEV = 4
ITEMS = 32


def group_lengths(key, count, group, longest, shortest):
    drawn = jax.random.randint(key, (count,), shortest, longest + 1)
    picked = jax.random.randint(jax.random.fold_in(key, 7), (count // group,), 0, group)
    full_item = jnp.arange(count) % group == jnp.repeat(picked, group)
    return jnp.where(full_item, longest, drawn).astype(jnp.int32)


def draw_lengths(key, part):
    key = jax.random.fold_in(key, 11)
    return group_lengths(key, ITEMS, ITEMS_DEV, DEC_LEN, DEC_LEN // 4)


def draw_memory_mask(key, part):
    key = jax.random.fold_in(key, 23)
    valid_count = group_lengths(key, ITEMS, ITEMS_DEV, ENC_LEN, ENC_LEN // 4)
    return (jnp.arange(ENC_LEN)[None, :] < valid_count[:, None]).astype(jnp.int32)


def with_ends(values, stream_key, smallest, high):
    spot = [jax.random.randint(jax.random.fold_in(stream_key, axis), (), 0, length) for axis, length in enumerate(values.shape)]
    main_axis = values.shape.index(max(values.shape))
    neighbour = spot[:main_axis] + [(spot[main_axis] + 1) % values.shape[main_axis]] + spot[main_axis + 1:]
    return values.at[tuple(spot)].set(smallest).at[tuple(neighbour)].set(high)


def steps_of(key, shape, cuts, low, top_value):
    factor_of, own = 1.0, jax.random.fold_in(key, 6)
    for position, parts in cuts:
        draws = jnp.exp(jax.random.uniform(jax.random.fold_in(own, position), (parts,), jnp.float32, low / len(cuts), top_value / len(cuts)))
        factor_of = factor_of * jnp.repeat(draws, shape[position] // parts).reshape([-1 if axis == position else 1 for axis in range(len(shape))])
    return factor_of


def scatter_about(rng, extent, spread, most, shards=(), kind=jnp.bfloat16):
    values = spread * jax.random.normal(rng, extent, jnp.float32)
    if shards:
        values = values * steps_of(rng, extent, shards, -0.22, 0.18)
    return jnp.clip(values, -most, most).astype(kind)


def setup_inputs(seed: int = 0) -> dict:
    seeds = jax.random.split(jax.random.key(seed), 22)
    return {
        "tokens": scatter_about(seeds[0], (ITEMS, DEC_LEN, D), 1.0, 6.0, ((0, 32),)),
        "memory": scatter_about(seeds[1], (ITEMS, ENC_LEN, D), 1.0, 6.0, ((0, 32),)),
        "cotangent": scatter_about(seeds[2], (ITEMS, DEC_LEN, D), 1.0, 6.0, ((0, 32),)),
        "lengths": draw_lengths(jax.random.fold_in(seeds[21], 71), 0),
        "memory_mask": draw_memory_mask(jax.random.fold_in(seeds[21], 71), 0),
        "token_tags": with_ends((jax.random.randint(seeds[5], (ITEMS, DEC_LEN), 0, 4) < 1).astype(jnp.int32), jax.random.fold_in(seeds[5], 1), 0, 1),
        "embedding": scatter_about(seeds[6], (2, D), 0.5, 3.0),
        "gain_self": jnp.clip(1.0 + 0.15 * jax.random.normal(seeds[7], (D,), jnp.float32), 0.25, 1.75).astype(jnp.bfloat16),
        "gain_cross": jnp.clip(1.0 + 0.15 * jax.random.normal(seeds[8], (D,), jnp.float32), 0.25, 1.75).astype(jnp.bfloat16),
        "gain_hidden": jnp.clip(1.0 + 0.15 * jax.random.normal(seeds[9], (D,), jnp.float32), 0.25, 1.75).astype(jnp.bfloat16),
        "self_query": scatter_about(seeds[10], (D, HEADS * HEAD_DIM), D ** -0.5, 0.21875, ((1, 4),)),
        "self_key": scatter_about(seeds[11], (D, HEADS * HEAD_DIM), D ** -0.5, 0.21875, ((1, 4),)),
        "self_value": scatter_about(seeds[12], (D, HEADS * HEAD_DIM), D ** -0.5, 0.21875, ((1, 4),)),
        "self_output": scatter_about(seeds[13], (HEADS * HEAD_DIM, D), (HEADS * HEAD_DIM // 16) ** -0.5, 0.875, ((0, 4),)),
        "position_bias": scatter_about(seeds[14], (BUCKETS, HEADS), 1.0, 4.0, ((1, 4),)),
        "cross_query": scatter_about(seeds[15], (D, HEADS * HEAD_DIM), D ** -0.5, 0.21875, ((1, 4),)),
        "cross_key": scatter_about(seeds[16], (D, HEADS * HEAD_DIM), D ** -0.5, 0.21875, ((1, 4),)),
        "cross_value": scatter_about(seeds[17], (D, HEADS * HEAD_DIM), D ** -0.5, 0.21875, ((1, 4),)),
        "cross_output": scatter_about(seeds[18], (HEADS * HEAD_DIM, D), (HEADS * HEAD_DIM // 32) ** -0.5, 1.25, ((0, 4),)),
        "hidden_in": scatter_about(seeds[19], (D, FF), D ** -0.5, 0.21875, ((1, 4),)),
        "hidden_out": scatter_about(seeds[20], (FF, D), (FF * 2 // 5) ** -0.5, 0.15625, ((0, 4),)),
    }


EPSILON = 1e-06
MASKED = -1000000000.0

@jax.custom_vjp
def low(v):
    return lax.optimization_barrier(v.astype(jnp.bfloat16)).astype(jnp.float32)

@jax.custom_vjp
def low_back(v):
    return v

def low_keep(v):
    return (low(v), None)

def low_pass(kept, grad):
    return (grad,)

def back_keep(v):
    return (v, None)

def back_low(kept, grad):
    return (low(grad),)
low.defvjp(low_keep, low_pass)
low_back.defvjp(back_keep, back_low)

def bucket_index(length, buckets, distance):
    exact_span = buckets // 2
    distances = np.arange(length)
    far_bucket = exact_span + np.floor(np.log(np.maximum(distances, 1) / exact_span) / math.log(distance / exact_span) * (buckets - exact_span)).astype(np.int32)
    return np.where(distances < exact_span, distances, np.minimum(far_bucket, buckets - 1)).astype(np.int32)

def product(left_side, right_side):
    return jnp.dot(left_side, right_side, precision=lax.Precision.HIGHEST)

def rms_scale(stream, gain):
    inverse = lax.rsqrt(lax.optimization_barrier(jnp.mean(stream * stream, axis=-1, keepdims=True)) + EPSILON)
    return stream * inverse * gain

def split_heads(matrix):
    return matrix.reshape(matrix.shape[0], -1, HEAD_DIM)

def gelu(value):
    return jax.nn.gelu(value, approximate=False)

def attend(query_rows, key_rows, value_rows, score_bias, allowed):
    scores = low_back(jnp.einsum('qhd,khd->hqk', query_rows, key_rows, precision=lax.Precision.HIGHEST) * 0.125 + score_bias)
    weights = low(jax.nn.softmax(jnp.where(allowed[None], scores, MASKED), axis=-1))
    mixed = jnp.einsum('hqk,khd->qhd', weights, value_rows, precision=lax.Precision.HIGHEST)
    return low(low_back(mixed.reshape(mixed.shape[0], -1)))

def item_layer(params, chosen, token_rows, memory_rows, length, memory_valid, tag_row):
    embedding, gain_self, gain_cross, gain_hidden, self_query, self_key, self_value, self_output, position_bias, cross_query, cross_key, cross_value, cross_output, hidden_in, hidden_out = params
    positions = jnp.arange(DEC_LEN)
    stream = token_rows + jnp.where((tag_row == 1)[:, None], embedding[1], embedding[0])
    normed = low(rms_scale(stream, gain_self))
    query_rows = split_heads(low(low_back(product(normed, self_query))))
    key_rows = split_heads(low(low_back(product(normed, self_key))))
    value_rows = split_heads(low(low_back(product(normed, self_value))))
    offset = jnp.clip(positions[:, None] - positions[None, :], 0, DEC_LEN - 1)
    score_bias = jnp.transpose(position_bias[chosen][offset], (2, 0, 1))
    allowed = (positions[None, :] <= positions[:, None]) & (positions[None, :] < length)
    stream = stream + low_back(product(attend(query_rows, key_rows, value_rows, score_bias, allowed), self_output))
    normed = low(rms_scale(stream, gain_cross))
    query_rows = split_heads(low(low_back(product(normed, cross_query))))
    key_rows = split_heads(low(low_back(product(memory_rows, cross_key))))
    value_rows = split_heads(low(low_back(product(memory_rows, cross_value))))
    allowed = jnp.broadcast_to((memory_valid == 1)[None, :], (DEC_LEN, ENC_LEN))
    stream = stream + low_back(product(attend(query_rows, key_rows, value_rows, 0.0, allowed), cross_output))
    normed = low(rms_scale(stream, gain_hidden))
    hidden = low(gelu(low_back(product(normed, hidden_in))))
    return stream + low_back(product(hidden, hidden_out))

def reference(tokens, memory, cotangent, lengths, memory_mask, token_tags, embedding, gain_self, gain_cross, gain_hidden, self_query, self_key, self_value, self_output, position_bias, cross_query, cross_key, cross_value, cross_output, hidden_in, hidden_out):
    chosen = jnp.asarray(bucket_index(DEC_LEN, BUCKETS, MAX_DISTANCE))
    weight_set = (embedding, gain_self, gain_cross, gain_hidden, self_query, self_key, self_value, self_output, position_bias, cross_query, cross_key, cross_value, cross_output, hidden_in, hidden_out)
    params = tuple((weight.astype(jnp.float32) for weight in weight_set))

    def layer(token_block, memory_block, param_set):

        def single(packed):
            return jax.checkpoint(item_layer)(param_set, chosen, packed[0], packed[1], packed[2], packed[3], packed[4])
        return lax.map(single, (token_block, memory_block, lengths, memory_mask, token_tags))
    layer_out, backward = jax.vjp(layer, tokens.astype(jnp.float32), memory.astype(jnp.float32), params)
    grad_tokens, grad_memory, gradients = backward(cotangent.astype(jnp.float32))
    return (layer_out.astype(jnp.bfloat16), grad_tokens.astype(jnp.bfloat16), grad_memory.astype(jnp.bfloat16), gradients[0], gradients[1], gradients[2], gradients[3], gradients[4], gradients[5], gradients[6], gradients[7], gradients[8], gradients[9], gradients[10], gradients[11], gradients[12], gradients[13], gradients[14])
```

```python
import math

import jax, jax.numpy as jnp, numpy as np
from jax import lax
from jax.experimental import pallas as pl
from jax.experimental.pallas import tpu as pltpu
from jax.sharding import PartitionSpec as P

EPSILON=1e-6
MASKED=-1e9
F32=jnp.float32; BF=jnp.bfloat16
NN=(((1,),(0,)),((),())); NT=(((1,),(1,)),((),()))
def mm(a,b,d=NN): return lax.dot_general(a,b,d,preferred_element_type=F32)
def inv_of(h): return lax.rsqrt(jnp.mean(h*h,axis=-1,keepdims=True)+EPSILON)
def norm_back(h,inv,g,r):
    s=r*g
    gg=jnp.sum(r*h*inv,axis=0,keepdims=True)
    return inv*s-h*(inv*inv*inv)*jnp.mean(s*h,axis=-1,keepdims=True),gg

def kernel(tok,mem,cot,tagc,emb,gains,mask1,mask2,btab,
           wqk,wvq,wckv,wso,wco,whin,whout,
           lo,gtok,gmem,small,diag,gqk,gvq,gckv,gso,gco,ghin,ghout,
           vqk,vvq,vckv,vso,vco,vhin,vhout,
           s0,s1,s2,gst,acc,gma,n1,n2,n1T,n2T,n3T,memT,
           qk1,vx1,q2r,kv2,kvT,mixT1,mixT2,lse,gkv,gvq2,rows,st384,st768,stout,sem,osem):
    ws=[(wqk,vqk),(wso,vso),(wvq,vvq),(wckv,vckv),(wco,vco),(whin,vhin),(whout,vhout)]
    cps=[pltpu.make_async_copy(a,b,sem.at[i]) for i,(a,b) in enumerate(ws)]
    for c in cps: c.start()
    g_self=gains[0:1,:]; g_cross=gains[1:2,:]; g_hid=gains[2:3,:]
    lane384=lax.broadcasted_iota(jnp.int32,(1,384),1)
    e0=emb[0:1,:].astype(F32); e1=emb[1:2,:].astype(F32)
    x0=tok[...].astype(F32)+jnp.where(tagc[...]>0.5,e1,e0)
    s0[...]=x0
    nn=(x0*inv_of(x0)*g_self).astype(BF)
    n1[...]=nn; n1T[...]=nn.T
    ji=lax.broadcasted_iota(jnp.int32,(256,256),0); ii=lax.broadcasted_iota(jnp.int32,(256,256),1)
    memT[...]=mem[...].T
    cps[0].wait(); cps[2].wait()
    def self_fwd(t,_):
        x=mm(n1[...],vqk[t])
        qk1[t]=jnp.where(lane384<192,x*0.125,x).astype(BF)
        v=mm(n1[...],vvq[t]).astype(BF)
        vx1[t]=v
        vT=v.T
        allowed=(ji<=ii)&(mask1[...]>0.5)
        for i in range(3):
            q=qk1[t,:,64*i:64*i+64]; k=qk1[t,:,192+64*i:256+64*i]
            b=pltpu.roll(jnp.broadcast_to(btab[t,i:i+1,:],(256,256)),0,1,stride=1,stride_axis=0)
            s=jnp.where(allowed,mm(k,q,NT)+b,MASKED)
            m=jnp.max(s,axis=0,keepdims=True)
            p=jnp.exp(s-m); l=jnp.sum(p,axis=0,keepdims=True)
            o=mm(vT[64*i:64*i+64,:],p.astype(BF))
            mixT1[t,64*i:64*i+64,:]=(o/l).astype(BF)
            lse[t,i:i+1,:]=m+jnp.log(l)
        return 0
    lax.fori_loop(0,4,self_fwd,0)
    cps[1].wait()
    s1[...]=s0[...]
    def so_fwd(t,_):
        s1[...]+=mm(mixT1[t].T,vso[t]); return 0
    lax.fori_loop(0,4,so_fwd,0)
    x1=s1[...]
    nn=(x1*inv_of(x1)*g_cross).astype(BF)
    n2[...]=nn; n2T[...]=nn.T
    cps[3].wait()
    def cross_fwd(t,_):
        q2r[t]=(mm(n2[...],vvq[t])*0.125).astype(BF)
        def proj(r,_):
            rs=pl.ds(pl.multiple_of(r*256,256),256)
            x=mm(mem[rs,:],vckv[t]).astype(BF)
            kv2[t,rs,:]=x
            return 0
        lax.fori_loop(0,4,proj,0)
        kvT[t]=kv2[t].T
        for i in range(3):
            q=q2r[t,:,192+64*i:256+64*i]
            ss=[]
            m=None
            for c in range(4):
                k=kv2[t,256*c:256*c+256,64*i:64*i+64]
                s=mm(k,q,NT)+jnp.concatenate([mask2[256*c:256*c+256,:]]*2,axis=1)
                ss.append(s)
                mc=jnp.max(s,axis=0,keepdims=True)
                m=mc if m is None else jnp.maximum(m,mc)
            l=0.;o=0.
            for c in range(4):
                p=jnp.exp(ss[c]-m)
                l=l+jnp.sum(p,axis=0,keepdims=True)
                o=o+mm(kvT[t,192+64*i:256+64*i,256*c:256*c+256],p.astype(BF))
            mixT2[t,64*i:64*i+64,:]=(o/l).astype(BF)
            lse[4+t,i:i+1,:]=m+jnp.log(l)
        return 0
    lax.fori_loop(0,4,cross_fwd,0)
    cps[4].wait()
    s2[...]=s1[...]
    def co_fwd(t,_):
        s2[...]+=mm(mixT2[t].T,vco[t]); return 0
    lax.fori_loop(0,4,co_fwd,0)
    x2=s2[...]
    nn=(x2*inv_of(x2)*g_hid).astype(BF)
    n3T[...]=nn.T
    rows[...]=nn
    acc[...]=x2
    gst[...]=jnp.zeros_like(x2)
    cps[5].wait(); cps[6].wait()
    def out_copy(t,src,dst,i): return pltpu.make_async_copy(src,dst.at[t],osem.at[i])
    def ffn(t,_):
        def part(c,_):
            cs=pl.ds(pl.multiple_of(c*256,256),256)
            v=mm(rows[...],vhin[t,:,cs])
            phi=0.5*(1.0+lax.erf(v*np.float32(1/math.sqrt(2))))
            act=(v*phi).astype(BF)
            gd=phi+v*(jnp.exp(-0.5*v*v)*np.float32(1/math.sqrt(2*math.pi)))
            acc[...]+=mm(act,vhout[t,cs,:])
            ga=mm(cot[...],vhout[t,cs,:],NT)
            gb=(gd*ga).astype(BF)
            gst[...]+=mm(gb,vhin[t,:,cs],NT)
            st768[0,:,cs]=mm(n3T[...],gb).astype(BF)
            st768[1,cs,:]=mm(act.T,cot[...]).astype(BF)
            return 0
        lax.fori_loop(0,3,part,0)
        c0=out_copy(t,st768.at[0],ghin,0); c1=out_copy(t,st768.at[1],ghout,1)
        c0.start(); c1.start(); c0.wait(); c1.wait()
        return 0
    lax.fori_loop(0,4,ffn,0)
    lo[...]=acc[...].astype(BF)
    d,gg=norm_back(x2,inv_of(x2),g_hid,gst[...])
    small[...]=jnp.zeros_like(small)
    small[4:5,:]=gg
    gst[...]=cot[...].astype(F32)+d
    rows[...]=gst[...].astype(BF)
    gma[...]=jnp.zeros_like(gma)
    acc[...]=jnp.zeros_like(x2)
    def cross_bwd(t,_):
        rw=rows[...]
        w=vco[t]
        G=mm(rw,w,NT).astype(BF)
        GT=mm(w,rw,NT).astype(BF)
        stout[...]=mm(mixT2[t],rw).astype(BF)
        c0=out_copy(t,stout,gco,0); c0.start()
        dqs=[]; dks=[];dvs=[]
        for i in range(3):
            q=q2r[t,:,192+64*i:256+64*i]
            g=G[:,64*i:64*i+64]
            r=jnp.sum(mixT2[t,64*i:64*i+64,:].astype(F32)*GT[64*i:64*i+64,:].astype(F32),axis=0,keepdims=True)
            ls=lse[4+t,i:i+1,:]
            dq=0.; dk=[];dv=[]
            for c in range(4):
                rs=slice(256*c,256*c+256)
                s=mm(kv2[t,rs,64*i:64*i+64],q,NT)+jnp.concatenate([mask2[rs,:]]*2,axis=1)
                p=jnp.exp(s-ls)
                dp=mm(kv2[t,rs,192+64*i:256+64*i],g,NT)
                gs=(p*(dp-r)).astype(BF)
                dv.append(mm(p.astype(BF),g).astype(BF))
                dk.append(mm(gs,q).astype(BF))
                dq=dq+mm(kvT[t,64*i:64*i+64,rs],gs)
            dqs.append(dq*0.125); dks.append(dk); dvs.append(dv)
        for c in range(4):
            gkv[256*c:256*c+256,:]=jnp.concatenate([x[c] for x in dks+dvs],axis=1)
        dqT=jnp.concatenate(dqs,axis=0).astype(BF)
        gvq2[t,:,192:384]=dqT.T
        def rl(r,_):
            rs=pl.ds(pl.multiple_of(r*256,256),256)
            gma[rs,:]+=mm(gkv[rs,:],vckv[t],NT)
            return 0
        lax.fori_loop(0,4,rl,0)
        def rd(r,_):
            rs=pl.ds(pl.multiple_of(r*256,256),256)
            st384[rs,:]=mm(memT[rs,:],gkv[...]).astype(BF)
            return 0
        lax.fori_loop(0,3,rd,0)
        c1=out_copy(t,st384,gckv,1); c1.start()
        acc[...]+=mm(jnp.where(lane384>=192,gvq2[t],0).astype(BF),vvq[t],NT)
        c0.wait(); c1.wait()
        return 0
    lax.fori_loop(0,4,cross_bwd,0)
    gmem[...]=gma[...].astype(BF)
    x1=s1[...]
    d,gg=norm_back(x1,inv_of(x1),g_cross,acc[...])
    small[3:4,:]=gg
    gst[...]+=d
    rows[...]=gst[...].astype(BF)
    acc[...]=jnp.zeros_like(x1)
    J=(ji+ii==255).astype(BF)
    def self_bwd(t,_):
        rw=rows[...]
        w=vso[t]
        G=mm(rw,w,NT).astype(BF)
        GT=mm(w,rw,NT).astype(BF)
        stout[...]=mm(mixT1[t],rw).astype(BF)
        c0=out_copy(t,stout,gso,0); c0.start()
        allowed=(ji<=ii)&(mask1[...]>0.5)
        kT=qk1[t].T
        dqs=[];dks=[];dvs=[]
        for i in range(3):
            q=qk1[t,:,64*i:64*i+64]; k=qk1[t,:,192+64*i:256+64*i]
            b=pltpu.roll(jnp.broadcast_to(btab[t,i:i+1,:],(256,256)),0,1,stride=1,stride_axis=0)
            g=G[:,64*i:64*i+64]
            r=jnp.sum(mixT1[t,64*i:64*i+64,:].astype(F32)*GT[64*i:64*i+64,:].astype(F32),axis=0,keepdims=True)
            s=jnp.where(allowed,mm(k,q,NT)+b,MASKED)
            p=jnp.exp(s-lse[t,i:i+1,:])
            dp=mm(vx1[t,:,64*i:64*i+64],g,NT)
            gs=(p*(dp-r)).astype(BF)
            dvs.append(mm(p.astype(BF),g).astype(BF))
            dks.append(mm(gs,q).astype(BF))
            dqs.append(mm(kT[192+64*i:256+64*i,:],gs)*0.125)
            dd=pltpu.roll(mm(J,gs),1,1,stride=1,stride_axis=0)
            diag[t,i:i+1,:]=jnp.sum(dd,axis=0,keepdims=True)
        dq=jnp.concatenate(dqs,axis=0).astype(BF).T
        gqk_t=jnp.concatenate([dq]+dks,axis=1)
        gvq_t=jnp.concatenate(dvs+[gvq2[t,:,192:384]],axis=1)
        st384[...]=mm(n1T[...],gqk_t).astype(BF)
        c1=out_copy(t,st384,gqk,1); c1.start()
        acc[...]+=mm(gqk_t,vqk[t],NT)+mm(jnp.where(lane384<192,gvq_t,0).astype(BF),vvq[t],NT)
        gkv[0:768,:]=jnp.where(lane384<192,mm(n1T[...],gvq_t),mm(n2T[...],gvq_t)).astype(BF)
        c2=out_copy(t,gkv.at[pl.ds(0,768),:],gvq,2); c2.start()
        c0.wait(); c1.wait(); c2.wait()
        return 0
    lax.fori_loop(0,4,self_bwd,0)
    x0=s0[...]
    d,gg=norm_back(x0,inv_of(x0),g_self,acc[...])
    small[2:3,:]=gg
    g0=gst[...]+d
    gtok[...]=g0.astype(BF)
    tg=tagc[...]>0.5
    small[0:1,:]=jnp.sum(jnp.where(tg,0.0,g0),axis=0,keepdims=True)
    small[1:2,:]=jnp.sum(jnp.where(tg,g0,0.0),axis=0,keepdims=True)

def compute(tok,mem,cot,tagc,emb,gains,mask1,mask2,btab,wqk,wvq,wckv,wso,wco,whin,whout):
    V=pl.BlockSpec(memory_space=pltpu.VMEM); A=pl.BlockSpec(memory_space=pl.ANY)
    S=jax.ShapeDtypeStruct
    outs=[S((256,768),BF),S((256,768),BF),S((1024,768),BF),S((8,768),F32),S((4,8,256),F32),
          S((4,768,384),BF),S((4,768,384),BF),S((4,768,384),BF),S((4,192,768),BF),S((4,192,768),BF),S((4,768,768),BF),S((4,768,768),BF)]
    vm=pltpu.VMEM
    scr=[vm((4,768,384),BF)]*3+[vm((4,192,768),BF)]*2+[vm((4,768,768),BF)]*2+\
        [vm((256,768),F32)]*5+[vm((1024,768),F32)]+[vm((256,768),BF)]*2+[vm((768,256),BF)]*3+[vm((768,1024),BF)]+\
        [vm((4,256,384),BF)]*3+[vm((4,1024,384),BF),vm((4,384,1024),BF),vm((4,192,256),BF),vm((4,192,256),BF),vm((8,8,256),F32),
         vm((1024,384),BF),vm((4,256,384),BF),vm((256,768),BF),vm((768,384),BF),vm((2,768,768),BF),vm((192,768),BF),
         pltpu.SemaphoreType.DMA((7,)),pltpu.SemaphoreType.DMA((3,))]
    return pl.pallas_call(kernel,out_shape=outs,in_specs=[V]*9+[A]*7,out_specs=[V]*5+[A]*7,scratch_shapes=scr,
        compiler_params=pltpu.CompilerParams(vmem_limit_bytes=63<<20))(tok,mem,cot,tagc,emb,gains,mask1,mask2,btab,wqk,wvq,wckv,wso,wco,whin,whout)

BUCKETS=32; MAX_DISTANCE=128
def bucket_of(length=256):
    e=BUCKETS//2
    d=np.arange(length)
    far=e+np.floor(np.log(np.maximum(d,1)/e)/math.log(MAX_DISTANCE/e)*(BUCKETS-e)).astype(np.int32)
    return np.where(d<e,d,np.minimum(far,BUCKETS-1)).astype(np.int32)

def prepare(tokens, memory, cotangent, lengths, memory_mask, token_tags, gain_self, gain_cross, gain_hidden):
    t = lax.axis_index("tensor")
    length = lax.dynamic_index_in_dim(lengths, t, 0, keepdims=False)
    mask = lax.dynamic_index_in_dim(memory_mask, t, 0, keepdims=False)
    mask1 = jnp.broadcast_to((jnp.arange(256)[:, None] < length).astype(F32), (256, 256))
    mask2 = jnp.broadcast_to(jnp.where(mask == 1, 0.0, MASKED).astype(F32)[:, None], (1024, 128))
    tagc = (token_tags == 1).astype(F32).reshape(256, 1)
    gains = jnp.pad(jnp.stack([gain_self, gain_cross, gain_hidden]).astype(F32), ((0, 5), (0, 0)))
    return tokens[0], memory[0], cotangent[0], tagc, gains, mask1, mask2


def per_device(tokens, memory, cotangent, lengths, memory_mask, token_tags, embedding, gain_self, gain_cross, gain_hidden,
               self_query, self_key, self_value, self_output, position_bias, cross_query, cross_key, cross_value,
               cross_output, hidden_in, hidden_out):
    tok, mem, cot, tagc, gains, mask1, mask2 = prepare(
        tokens, memory, cotangent, lengths, memory_mask, token_tags, gain_self, gain_cross, gain_hidden)
    chosen = bucket_of()
    onehot = (chosen[:, None] == np.arange(BUCKETS)[None, :]).astype(np.float32)
    table = jnp.dot(position_bias.T, jnp.asarray(onehot.T, BF), preferred_element_type=F32)
    table = jnp.pad(table, ((0, 5), (0, 0)))
    gather = lambda w: lax.all_gather(w, "tensor", axis=0)
    btab = gather(table)
    wqk = gather(jnp.concatenate([self_query, self_key], 1))
    wvq = gather(jnp.concatenate([self_value, cross_query], 1))
    wckv = gather(jnp.concatenate([cross_key, cross_value], 1))
    lo, gtok, gmem, small, diag, gqk, gvq, gckv, gso, gco, ghin, ghout = compute(
        tok, mem, cot, tagc, embedding, gains, mask1, mask2, btab, wqk, wvq, wckv,
        gather(self_output), gather(cross_output), gather(hidden_in), gather(hidden_out))
    small = lax.psum(small, ("dp", "tensor"))
    def total(g):
        g = lax.psum_scatter(g, "tensor", scatter_dimension=0, tiled=False)
        return lax.psum(g, "dp")
    diag = total(diag)
    pb = jnp.dot(jnp.asarray(onehot.T), diag[:3].T, precision=lax.Precision.HIGHEST)
    a, b, c, so, co, hi, ho = lax.psum(tuple(lax.psum_scatter(g, "tensor", scatter_dimension=0, tiled=False) for g in (gqk, gvq, gckv, gso, gco, ghin, ghout)), "dp")
    f = lambda x: x.astype(F32)
    return (lo[None], gtok[None], gmem[None], small[:2], small[2], small[3], small[4],
            f(a[:, :192]), f(a[:, 192:]), f(b[:, :192]), f(so), pb, f(b[:, 192:]), f(c[:, :192]), f(c[:, 192:]), f(co), f(hi), f(ho))


def solution(mesh):
    item = P(("dp", "tensor"), None, None)
    col, row, rep = P(None, "tensor"), P("tensor", None), P()
    in_specs = (item, item, item, P("dp"), P("dp", None), P(("dp", "tensor"), None), rep, rep, rep, rep,
                col, col, col, row, col, col, col, col, row, col, row)
    out_specs = (item, item, item, rep, rep, rep, rep, col, col, col, row, col, col, col, col, row, col, row)
    return jax.shard_map(per_device, mesh=mesh, in_specs=in_specs, out_specs=out_specs, check_vma=False)
```

```python
import math

import jax
import jax.numpy as jnp
import numpy as np
from jax import lax
from jax.experimental import pallas as pl
from jax.experimental.pallas import tpu as pltpu
from jax.sharding import PartitionSpec as P

EPSILON = 1e-6
MASKED = -1e9
BUCKETS = 32
MAX_DISTANCE = 128
F32 = jnp.float32
BF = jnp.bfloat16
NN = (((1,), (0,)), ((), ()))
NT = (((1,), (1,)), ((), ()))
MESH = pl.DeviceIdType.MESH
GATHERED = ("qk", "vq", "so", "ckv", "co", "hin", "hout")
LAST_OF_FEED = ("hout2", 2)
FIRST_REUSE = ("ckv", 0)
CHUNKS = ("hin0", "hout0", "hin1", "hout1", "hin2", "hout2", "co", "ckv", "so", "qk", "vq")


class Remote:
    def __init__(self, *args):
        self.args = args

    def made(self):
        src, dst, send, recv, to = self.args
        return pltpu.make_async_remote_copy(
            src_ref=src, dst_ref=dst, send_sem=send, recv_sem=recv, device_id=to, device_id_type=MESH)

    def start(self):
        self.made().start()

    def wait(self):
        self.made().wait()

    def wait_send(self):
        self.made().wait_send()

    def wait_recv(self):
        self.made().wait_recv()


def mm(a, b, d=NN):
    return lax.dot_general(a, b, d, preferred_element_type=F32)


def inverse_of(h):
    return lax.rsqrt(jnp.mean(h * h, axis=-1, keepdims=True) + EPSILON)


def norm_back(h, inv, g, r):
    s = r * g
    gain = jnp.sum(r * h * inv, axis=0, keepdims=True)
    return inv * s - h * (inv * inv * inv) * jnp.mean(s * h, axis=-1, keepdims=True), gain


def rows_of(start, size):
    return pl.ds(pl.multiple_of(start, 16), size)


def add_into(dst, parts, into=None):
    rows, width = dst.shape
    into = dst if into is None else into
    step = next(n for n in (96, 64, 48, 32, 16) if rows % n == 0 and n * width <= 96 * 768)

    def block(i, _):
        at = rows_of(i * step, step)
        total = dst[at, :].astype(F32)
        for p in parts:
            total = total + p[at, :].astype(F32)
        into[at, :] = total.astype(BF)
        return 0

    lax.fori_loop(0, rows // step, block, 0)


class Chunk:
    def __init__(self, base, row0, rows, col0, width, first, second):
        self.base, self.row0, self.rows, self.col0, self.width = base, row0, rows, col0, width
        self.first, self.second = first, second
        self.by_columns = rows == 192
        self.half = (rows, width // 2) if self.by_columns else (rows // 2, width)
        self.quarter = (self.half[0] // 2, self.half[1])
        self.eighth = (self.half[0] // 4, self.half[1])

    def part(self, shard, row, rows, col, width):
        return self.base.at[shard, rows_of(self.row0 + row, rows), pl.ds(pl.multiple_of(self.col0 + col, 128), width)]

    def whole(self, shard):
        return self.part(shard, 0, self.rows, 0, self.width)

    def place(self, y, z=None, w=None):
        if self.by_columns:
            row, rows, col, width = 0, self.rows, y * (self.width // 2), self.width // 2
        else:
            row, rows, col, width = y * (self.rows // 2), self.rows // 2, 0, self.width
        if z is not None:
            rows = rows // 2
            row = row + z * rows
        if w is not None:
            rows = rows // 2
            row = row + w * rows
        return row, rows, col, width

    def piece(self, shard, *at):
        return self.part(shard, *self.place(*at))

    def result(self, *at):
        row, rows, col, width = self.place(*at)
        return self.second.at[rows_of(row, rows), pl.ds(pl.multiple_of(col, 128), width)]


def bucket_onehot():
    bucket = bucket_of()
    n = lax.broadcasted_iota(jnp.int32, (BUCKETS, 256), 1)
    chosen = jnp.zeros((BUCKETS, 256), jnp.int32)
    for b in range(1, BUCKETS):
        chosen = chosen + jnp.where(n >= int(np.argmax(bucket >= b)), 1, 0)
    return (chosen == lax.broadcasted_iota(jnp.int32, (BUCKETS, 256), 0)).astype(BF)


def layer_kernel(bits, names, *refs):
    R = dict(zip(names, refs, strict=True))
    g = lambda *ns: [R[n] for n in ns]
    tok, mem, cot, lengths, mmask, tags, emb, tab = g("tok", "mem", "cot", "lengths", "mmask", "tags", "emb", "tab")
    vqk, vvq, vso, vckv, vco, vhin, vhout = g("vqk", "vvq", "vso", "vckv", "vco", "vhin", "vhout")
    s0, s1, s2, gst, acc = g("s0", "s1", "s2", "gst", "acc")
    n1, n2, n1T, n2T, n3T, memT = g("n1", "n2", "n1T", "n2T", "n3T", "memT")
    qk1, vx1, q2r, kv2, kvT, mix1, mix2, lse = g("qk1", "vx1", "q2r", "kv2", "kvT", "mix1", "mix2", "lse")
    gvq2, rows, mask2, tagv, btab, sm, smb, gmv = g("gvq2", "rows", "mask2", "tagv", "btab", "sm", "smb", "gmv")
    gsend, grecv, rsend, rrecv, lsem, osem, ssend, srecv, tsend, trecv, credit = g(
        "gsend", "grecv", "rsend", "rrecv", "lsem", "osem", "ssend", "srecv", "tsend", "trecv", "credit")

    dp = lax.axis_index("dp")
    t = lax.axis_index("tensor")
    c = lax.rem(t, 2)
    x = t // 2
    tc = t + 1 - 2 * c
    tx = t + 2 - 4 * x
    td = tc + 2 - 4 * x
    bit = [lax.rem(dp // (1 << b), 2) for b in range(bits)]
    pb = [dp + (1 << b) - (2 << b) * bit[b] for b in range(bits)]
    y, z1, z2 = bit[0], bit[1], bit[2]
    quad, quad_y, quad_z = y + 2 * z1, (1 - y) + 2 * z1, y + 2 * (1 - z1)
    quad_d = 3 - quad

    remote = Remote

    def fwd_shard(s):
        a, b = lax.rem(s, 2), s // 2
        return 2 * (x + b * (1 - 2 * x)) + c + a * (1 - 2 * c)

    def bwd_shard(s):
        a, b = 1 - s // 2, 1 - lax.rem(s, 2)
        return 2 * (x + b * (1 - 2 * x)) + c + a * (1 - 2 * c)

    barrier = pltpu.get_barrier_semaphore()
    partners = [(dp, tc), (dp, tx), (dp, td)] + [(p, t) for p in pb]
    for p in partners:
        pl.semaphore_signal(barrier, inc=1, device_id=p, device_id_type=MESH)
    pl.semaphore_wait(barrier, len(partners))

    weight = {"qk": vqk, "vq": vvq, "so": vso, "ckv": vckv, "co": vco, "hin": vhin, "hout": vhout}
    source = {"so": R["so_in"], "co": R["co_in"], "hin": R["hin_in"], "hout": R["hout_in"]}

    def gather_copies(name):
        i, v = GATHERED.index(name), weight[name]
        height = v.shape[1]
        q = height // 4
        own = source.get(name, v.at[t])

        def copy(j, rws, to, src=None):
            return remote(v.at[tx, rws] if src is None else src, v.at[tx if src is None else t, rws],
                          gsend.at[i, j], grecv.at[i, j], to)

        core = (dp, tc)
        d = {
            "core": remote(own, v.at[t], gsend.at[i, 0], grecv.at[i, 0], core),
            "x": copy(1, rows_of(quad * q, q), (dp, tx), own.at[rows_of(quad * q, q)]),
            "y": copy(2, rows_of(quad * q, q), (pb[0], t)),
            "z": copy(3, rows_of(quad * q, q), (pb[1], t)),
            "cx": copy(4, rows_of(quad * q, q), core),
            "cy": copy(5, rows_of(quad_y * q, q), core),
            "cz": copy(6, rows_of(quad_z * q, q), core),
        }
        if height == 768:
            h = q // 2
            d["yd"] = copy(7, rows_of(quad_z * q, h), (pb[0], t))
            d["zd"] = copy(8, rows_of(quad_y * q + h, h), (pb[1], t))
            d["cyd"] = copy(9, rows_of(quad_d * q, h), core)
            d["czd"] = copy(10, rows_of(quad_d * q + h, h), core)
        elif name == "so":
            d["yd"] = copy(7, rows_of(quad_z * q, q), (pb[0], t))
            d["cyd"] = copy(9, rows_of(quad_d * q, q), core)
        else:
            d["zd"] = copy(8, rows_of(quad_y * q, q), (pb[1], t))
            d["czd"] = copy(10, rows_of(quad_d * q, q), core)
        return d

    def local_copies(name):
        return pltpu.make_async_copy(source[name], weight[name].at[t], lsem.at[GATHERED.index(name)])

    def gather_1(*ns):
        for n in ns:
            d = gather_copies(n)
            d["x"].wait_recv()
            for k in ("y", "z", "cx"):
                d[k].start()

    def gather_2(*ns):
        for n in ns:
            d = gather_copies(n)
            d["y"].wait_recv()
            if "zd" in d:
                d["zd"].start()
            d["cy"].start()
            d["z"].wait_recv()
            if "yd" in d:
                d["yd"].start()
            d["cz"].start()

    def gather_3(*ns):
        for n in ns:
            d = gather_copies(n)
            for a, b in (("yd", "cyd"), ("zd", "czd")):
                if a in d:
                    d[a].wait_recv()
                    d[b].start()

    def gather_4(*ns):
        for n in ns:
            d = gather_copies(n)
            for k in ("cx", "cy", "cz", "cyd", "czd"):
                if k in d:
                    d[k].wait_recv()

    def gather_core(*ns):
        for n in ns:
            gather_copies(n)["core"].wait_recv()
            if n in source:
                local_copies(n).wait()

    def gather_sent(*ns):
        for n in ns:
            for d in gather_copies(n).values():
                d.wait_send()

    for n in source:
        local_copies(n).start()
    for n, a, b in (("qk", "sq", "sk"), ("vq", "sv", "cq")):
        weight[n][t] = jnp.concatenate([R[a][...], R[b][...]], axis=0).T
    for n in ("qk", "vq", "so"):
        d = gather_copies(n)
        d["x"].start()
        d["core"].start()
    btab[t, 0:3, :] = mm(tab[...], bucket_onehot())
    table_copies = [remote(btab.at[t], btab.at[t], tsend.at[j], trecv.at[j], (dp, to)) for j, to in enumerate((tc, tx, td))]
    for d in table_copies:
        d.start()
    vckv[t] = jnp.concatenate([R["ck"][...], R["cv"][...]], axis=0).T
    for n in ("ckv", "co", "hin", "hout"):
        d = gather_copies(n)
        d["x"].start()
        d["core"].start()

    f = CHUNKS.index
    table = {}
    for n in CHUNKS:
        if n.startswith("hin"):
            k = int(n[3:]) * 256
            table[n] = Chunk(vhin, 0, 768, k, 256, R["rb1a"].at[:, :, pl.ds(k, 256)], R["rb2hin"].at[:, pl.ds(k, 256)])
        elif n.startswith("hout"):
            k = int(n[4:]) * 256
            table[n] = Chunk(vhout, k, 256, 0, 768, R["rb1b"].at[:, pl.ds(k, 256), :], R["rb2hout"].at[pl.ds(k, 256), :])
        else:
            rb1 = {"ckv": lambda: R["rb1a"].at[:, :, pl.ds(0, 384)], "qk": lambda: R["rb1a"].at[:, :, pl.ds(384, 384)],
                   "vq": lambda: R["rb1b"].at[:, :, pl.ds(0, 384)], "so": lambda: R["rb1so"], "co": lambda: R["rb1co"]}[n]()
            v = weight[n]
            table[n] = Chunk(v, 0, v.shape[1], 0, v.shape[2], rb1, R["rb2" + n])
    outs = {"hin": R["ohin"], "hout": R["ohout"], "co": R["oco"], "ckv": R["ockv"], "so": R["oso"], "qk": R["oqk"], "vq": R["ovq"]}

    def r_copy(n, j):
        k, i = table[n], f(n)
        sems = (rsend.at[i, j], rrecv.at[i, j])
        if j == 0:
            return remote(k.whole(td), k.first.at[0], *sems, (dp, tc))
        if j == 1:
            return remote(k.whole(tc), k.first.at[1], *sems, (dp, tc))
        if j == 2:
            return remote(k.whole(tx), k.second, *sems, (dp, tx))
        if j == 3:
            return remote(k.piece(t, 1 - y), R["yb_" + n], *sems, (pb[0], t))
        if j == 4:
            return remote(k.piece(t, y, 1 - z1), R["zb_" + n], *sems, (pb[1], t))
        if j == 5:
            return remote(k.piece(t, y, z1, 1 - z2), R["wb_" + n], *sems, (pb[2], t))
        if j == 6:
            e = k.result(y, z1, z2)
            return remote(e, e, *sems, (pb[2], t))
        if j == 7:
            e = k.result(y, z1)
            return remote(e, e, *sems, (pb[1], t))
        if j == 8:
            e = k.result(y)
            return remote(e, e, *sems, (pb[0], t))
        e = k.piece(t, y, z1, z2)
        return remote(e, R["eb_" + n].at[j - 9], *sems, (pb[j - 6], t))

    def out_copy(n):
        k = table[n]
        if n.startswith("hin"):
            dst = outs["hin"].at[:, pl.ds(k.col0, 256)]
        elif n.startswith("hout"):
            dst = outs["hout"].at[pl.ds(k.row0, 256), :]
        else:
            dst = outs[n]
        return pltpu.make_async_copy(k.second, dst, osem.at[f(n)])

    def step(n, j):
        k = table[n]
        if j == 0:
            r_copy(n, 0).start()
            r_copy(n, 1).start()
        elif j == 1:
            r_copy(n, 0).wait_recv()
            add_into(k.whole(tx), [k.first.at[0]])
            r_copy(n, 2).start()
        elif j == 2:
            r_copy(n, 1).wait_recv()
            add_into(k.whole(t), [k.first.at[1]])
        elif j == 3:
            r_copy(n, 2).wait_recv()
            add_into(k.whole(t), [k.second])
            r_copy(n, 3).start()
        elif j == 4:
            r_copy(n, 3).wait_recv()
            add_into(k.piece(t, y), [R["yb_" + n]])
            r_copy(n, 4).start()
        elif j == 5:
            r_copy(n, 4).wait_recv()
            add_into(k.piece(t, y, z1), [R["zb_" + n]])
            r_copy(n, 5).start()
        elif j == 6:
            r_copy(n, 5).wait_recv()
            own = k.piece(t, y, z1, z2)
            add_into(own, [R["wb_" + n]], k.result(y, z1, z2) if bits == 3 else None)
            for b in range(3, bits):
                r_copy(n, 6 + b).start()
                r_copy(n, 6 + b).wait()
                add_into(own, [R["eb_" + n].at[b - 3]], k.result(y, z1, z2) if b == bits - 1 else None)
            r_copy(n, 6).start()
        elif j == 7:
            r_copy(n, 6).wait_recv()
            r_copy(n, 7).start()
        elif j == 8:
            r_copy(n, 7).wait_recv()
            r_copy(n, 8).start()
        elif j == 9:
            r_copy(n, 8).wait_recv()
            out_copy(n).start()

    to = [(dp, tc), (dp, tx)] + [(p, t) for p in pb]

    def small_step(j):
        if j:
            copy = remote(sm, smb.at[j - 1], ssend.at[j - 1], srecv.at[j - 1], to[j - 1])
            copy.wait()
            sm[...] = sm[...] + smb[j - 1]
        if j < len(to):
            remote(sm, smb.at[j], ssend.at[j], srecv.at[j], to[j]).start()

    def run(place):
        for n, j in SCHEDULE[place]:
            if n == "small":
                small_step(j)
                continue
            if (n, j) == FIRST_REUSE:
                pl.semaphore_wait(credit, 1)
            step(n, j)
            if (n, j) == LAST_OF_FEED:
                pl.semaphore_signal(credit, inc=1, device_id=(dp, tc), device_id_type=MESH)

    g_self, g_cross, g_hid = (R[n][...].astype(F32).reshape(1, 768) for n in ("gain1", "gain2", "gain3"))
    lane384 = lax.broadcasted_iota(jnp.int32, (1, 384), 1)
    ji = lax.broadcasted_iota(jnp.int32, (256, 256), 0)
    ii = lax.broadcasted_iota(jnp.int32, (256, 256), 1)
    length = lengths[t]
    allowed = lambda: (ji <= ii) & (ji < length)
    tagv[...] = jnp.broadcast_to((tags[...] == 1).astype(F32), (128, 256)).T
    tagged = lambda: jnp.concatenate([tagv[...]] * 6, axis=1) > 0.5
    x0 = tok[...].astype(F32) + jnp.where(tagged(), emb[1:2, :].astype(F32), emb[0:1, :].astype(F32))
    s0[...] = x0
    nn = (x0 * inverse_of(x0) * g_self).astype(BF)
    n1[...] = nn
    n1T[...] = nn.T
    gather_core("qk", "vq")
    for d in table_copies:
        d.wait_recv()

    def bias_of(shard, i):
        return pltpu.roll(jnp.broadcast_to(btab[shard, i:i + 1, :], (256, 256)), 0, 1, stride=1, stride_axis=0)

    def project_memory(shard):
        def block(r, _):
            at = rows_of(r * 256, 256)
            kv2[shard, at, :] = mm(mem[at, :], vckv[shard]).astype(BF)
            return 0
        lax.fori_loop(0, 4, block, 0)

    def transpose_memory():
        valid = mmask[pl.ds(t, 1), :]
        mask2[...] = jnp.broadcast_to(jnp.where(valid == 1, 0.0, MASKED).astype(F32), (128, 1024)).T
        memT[...] = mem[...].T

    def hooks(s, table_of):
        for k, todo in table_of.items():
            @pl.when(s == k)
            def _():
                todo()

    def before_far_shards():
        gather_1("qk")
        transpose_memory()
        gather_1("vq")
        gather_core("ckv")
        project_memory(t)
        gather_1("so")
        gather_2("qk")
        project_memory(tc)
        gather_2("vq", "so")
        gather_1("ckv", "co")
        gather_3("qk", "vq", "so")
        gather_4("qk", "vq")

    def self_forward(s, _):
        hooks(s, {2: before_far_shards, 3: lambda: (gather_2("ckv", "co"), gather_1("hin"))})
        k = fwd_shard(s)
        a = mm(n1[...], vqk[k])
        qk1[k] = jnp.where(lane384 < 192, a * 0.125, a).astype(BF)
        v = mm(n1[...], vvq[k]).astype(BF)
        vx1[k] = v
        vT = v.T
        for i in range(3):
            q, kk = qk1[k, :, 64 * i:64 * i + 64], qk1[k, :, 192 + 64 * i:256 + 64 * i]
            scores = jnp.where(allowed(), mm(kk, q, NT) + bias_of(k, i), MASKED)
            most = jnp.max(scores, axis=0, keepdims=True)
            p = jnp.exp(scores - most)
            total = jnp.sum(p, axis=0, keepdims=True)
            o = mm(vT[64 * i:64 * i + 64, :], p.astype(BF))
            mix1[k, 64 * i:64 * i + 64, :] = (o / total).astype(BF)
            lse[k, i:i + 1, :] = most + jnp.log(total)
        return 0

    lax.fori_loop(0, 4, self_forward, 0)
    gather_3("ckv", "co")
    gather_core("so")
    gather_4("so")

    def project_out(target, mix, w):
        def block(k, _):
            target[...] += mm(mix[k].T, w[k])
            return 0
        lax.fori_loop(0, 4, block, 0)

    s1[...] = s0[...]
    project_out(s1, mix1, vso)
    x1 = s1[...]
    nn = (x1 * inverse_of(x1) * g_cross).astype(BF)
    n2[...] = nn
    n2T[...] = nn.T

    def cross_scores(shard, i, r, q):
        at = slice(256 * r, 256 * r + 256)
        return mm(kv2[shard, at, 64 * i:64 * i + 64], q, NT) + jnp.concatenate([mask2[at, :]] * 2, axis=1)

    def cross_forward(s, _):
        def far():
            gather_4("ckv")
            gather_2("hin")
            project_memory(tx)

        hooks(s, {1: lambda: gather_1("hout"), 2: far, 3: lambda: (project_memory(td), gather_3("hin"), gather_2("hout"))})
        k = fwd_shard(s)
        q2r[k] = (mm(n2[...], vvq[k]) * 0.125).astype(BF)
        kvT[...] = kv2[k, :, 128:384].T
        for i in range(3):
            q = q2r[k, :, 192 + 64 * i:256 + 64 * i]
            ss = [cross_scores(k, i, r, q) for r in range(4)]
            most = jnp.max(jnp.maximum(jnp.maximum(ss[0], ss[1]), jnp.maximum(ss[2], ss[3])), axis=0, keepdims=True)
            total, o = 0.0, 0.0
            for r in range(4):
                p = jnp.exp(ss[r] - most)
                total = total + jnp.sum(p, axis=0, keepdims=True)
                o = o + mm(kvT[64 + 64 * i:128 + 64 * i, 256 * r:256 * r + 256], p.astype(BF))
            mix2[k, 64 * i:64 * i + 64, :] = (o / total).astype(BF)
            lse[4 + k, i:i + 1, :] = most + jnp.log(total)
        return 0

    lax.fori_loop(0, 4, cross_forward, 0)
    gather_core("co")
    gather_4("co")
    s2[...] = s1[...]
    project_out(s2, mix2, vco)
    x2 = s2[...]
    nn = (x2 * inverse_of(x2) * g_hid).astype(BF)
    n3T[...] = nn.T
    rows[...] = nn
    acc[...] = x2
    gst[...] = jnp.zeros_like(x2)
    gather_core("hin", "hout")

    def feed(j, _):
        def far():
            gather_3("hout")
            gather_4("hin", "hout")
            gather_sent("hin", "hout")

        hooks(j, {6: far, 8: lambda: run("feed8"), 10: lambda: run("feed10")})
        k = fwd_shard(lax.rem(j, 2) + 2 * (j // 6))
        cs = pl.ds(pl.multiple_of((lax.rem(j, 6) // 2) * 256, 256), 256)
        v = mm(rows[...], vhin[k, :, cs])
        phi = 0.5 * (1.0 + lax.erf(v * np.float32(1 / math.sqrt(2))))
        act = (v * phi).astype(BF)
        slope = phi + v * (jnp.exp(-0.5 * v * v) * np.float32(1 / math.sqrt(2 * math.pi)))
        acc[...] += mm(act, vhout[k, cs, :])
        gb = (slope * mm(cot[...], vhout[k, cs, :], NT)).astype(BF)
        gst[...] += mm(gb, vhin[k, :, cs], NT)
        vhin[k, :, cs] = mm(n3T[...], gb).astype(BF)
        vhout[k, cs, :] = mm(act.T, cot[...]).astype(BF)
        return 0

    lax.fori_loop(0, 12, feed, 0)
    run("feed_end")
    gather_sent("qk", "vq", "so", "ckv", "co")
    for d in table_copies:
        d.wait_send()
    lo_v, gt_v = R["lov"], R["gtv"]
    lo_v[...] = acc[...].astype(BF)
    lo_copy = pltpu.make_async_copy(lo_v, R["lo"], lsem.at[7])
    lo_copy.start()
    d, gain = norm_back(x2, inverse_of(x2), g_hid, gst[...])

    def put_small(row, value):
        for i in range(3):
            at = 3 * row + i
            sm[at // 8, at % 8:at % 8 + 1, :] = value[:, 256 * i:256 * i + 256]

    sm[...] = jnp.zeros_like(sm)
    put_small(4, gain)
    gst[...] = cot[...].astype(F32) + d
    run("norm3")
    rows[...] = gst[...].astype(BF)
    acc[...] = jnp.zeros_like(x2)

    def cross_backward(s, _):
        hooks(s, {i: (lambda i=i: run("cross%d" % i)) for i in range(4)})
        k = bwd_shard(s)
        rw = rows[...]
        w = vco[k]
        G = mm(rw, w, NT).astype(BF)
        GT = mm(w, rw, NT).astype(BF)
        vco[k] = mm(mix2[k], rw).astype(BF)
        kvT[...] = kv2[k, :, 0:256].T
        dqs, dks, dvs = [], [], []
        for i in range(3):
            q = q2r[k, :, 192 + 64 * i:256 + 64 * i]
            gi = G[:, 64 * i:64 * i + 64]
            r = jnp.sum(mix2[k, 64 * i:64 * i + 64, :].astype(F32) * GT[64 * i:64 * i + 64, :].astype(F32), axis=0, keepdims=True)
            ls = lse[4 + k, i:i + 1, :]
            dq, dk, dv = 0.0, [], []
            for b in range(4):
                at = slice(256 * b, 256 * b + 256)
                p = jnp.exp(cross_scores(k, i, b, q) - ls)
                dp_ = mm(kv2[k, at, 192 + 64 * i:256 + 64 * i], gi, NT)
                gs = (p * (dp_ - r)).astype(BF)
                dv.append(mm(p.astype(BF), gi).astype(BF))
                dk.append(mm(gs, q).astype(BF))
                dq = dq + mm(kvT[64 * i:64 * i + 64, at], gs)
            dqs.append(dq * 0.125)
            dks.append(dk)
            dvs.append(dv)
        for b in range(4):
            kv2[k, 256 * b:256 * b + 256, :] = jnp.concatenate([v[b] for v in dks + dvs], axis=1)
        gvq2[k, :, 192:384] = jnp.concatenate(dqs, axis=0).astype(BF).T
        acc[...] += mm(jnp.where(lane384 >= 192, gvq2[k], 0).astype(BF), vvq[k], NT)
        return 0

    lax.fori_loop(0, 4, cross_backward, 0)
    run("cross_end")

    def memory_grad(r, _):
        at = rows_of(r * 256, 256)
        total = mm(kv2[0, at, :], vckv[0], NT)
        for k in range(1, 4):
            total = total + mm(kv2[k, at, :], vckv[k], NT)
        gmv[at, :] = total.astype(BF)
        return 0

    lax.fori_loop(0, 4, memory_grad, 0)
    gm_copy = pltpu.make_async_copy(gmv, R["gmem"], lsem.at[8])
    gm_copy.start()
    run("mem_half")

    def memory_weights(s, _):
        k = bwd_shard(s)

        def block(r, _):
            at = rows_of(r * 256, 256)
            vckv[k, at, :] = mm(memT[at, :], kv2[k]).astype(BF)
            return 0
        lax.fori_loop(0, 3, block, 0)
        return 0

    lax.fori_loop(0, 4, memory_weights, 0)
    run("mem_end")
    d, gain = norm_back(s1[...], inverse_of(s1[...]), g_cross, acc[...])
    put_small(3, gain)
    gst[...] += d
    rows[...] = gst[...].astype(BF)
    acc[...] = jnp.zeros_like(x2)

    def self_backward(s, _):
        hooks(s, {i: (lambda i=i: run("self%d" % i)) for i in range(4)})
        k = bwd_shard(s)
        rw = rows[...]
        w = vso[k]
        G = mm(rw, w, NT).astype(BF)
        GT = mm(w, rw, NT).astype(BF)
        vso[k] = mm(mix1[k], rw).astype(BF)
        kT = qk1[k, :, 128:384].T
        flip = (ji + ii == 255).astype(BF)
        dqs, dks, dvs = [], [], []
        for i in range(3):
            q, kk = qk1[k, :, 64 * i:64 * i + 64], qk1[k, :, 192 + 64 * i:256 + 64 * i]
            gi = G[:, 64 * i:64 * i + 64]
            r = jnp.sum(mix1[k, 64 * i:64 * i + 64, :].astype(F32) * GT[64 * i:64 * i + 64, :].astype(F32), axis=0, keepdims=True)
            scores = jnp.where(allowed(), mm(kk, q, NT) + bias_of(k, i), MASKED)
            p = jnp.exp(scores - lse[k, i:i + 1, :])
            dp_ = mm(vx1[k, :, 64 * i:64 * i + 64], gi, NT)
            gs = (p * (dp_ - r)).astype(BF)
            dvs.append(mm(p.astype(BF), gi).astype(BF))
            dks.append(mm(gs, q).astype(BF))
            dqs.append(mm(kT[64 + 64 * i:128 + 64 * i, :], gs) * 0.125)
            shifted = pltpu.roll(mm(flip, gs), 1, 1, stride=1, stride_axis=0)
            sm[2 + k, i:i + 1, :] = jnp.sum(shifted, axis=0, keepdims=True)
        g_qk = jnp.concatenate([jnp.concatenate(dqs, axis=0).astype(BF).T] + dks, axis=1)
        g_vq = jnp.concatenate(dvs + [gvq2[k, :, 192:384]], axis=1)
        acc[...] += mm(g_qk, vqk[k], NT) + mm(jnp.where(lane384 < 192, g_vq, 0).astype(BF), vvq[k], NT)
        vqk[k] = mm(n1T[...], g_qk).astype(BF)
        vvq[k] = jnp.where(lane384 < 192, mm(n1T[...], g_vq), mm(n2T[...], g_vq)).astype(BF)
        return 0

    lax.fori_loop(0, 4, self_backward, 0)
    run("self_end")
    d, gain = norm_back(s0[...], inverse_of(s0[...]), g_self, acc[...])
    put_small(2, gain)
    g0 = gst[...] + d
    gt_v[...] = g0.astype(BF)
    gt_copy = pltpu.make_async_copy(gt_v, R["gtok"], lsem.at[9])
    gt_copy.start()
    put_small(0, jnp.sum(jnp.where(tagged(), 0.0, g0), axis=0, keepdims=True))
    put_small(1, jnp.sum(jnp.where(tagged(), g0, 0.0), axis=0, keepdims=True))

    run("fin")
    run("end")
    for j in range(6, len(to) + 1):
        small_step(j)
    R["smo"][...] = sm[0:2]
    R["dgo"][...] = sm[2 + t]
    for n in CHUNKS:
        for j in range(9 + bits - 3):
            if j < 9:
                r_copy(n, j).wait_send()
        out_copy(n).wait()
    lo_copy.wait()
    gm_copy.wait()
    gt_copy.wait()


SCHEDULE = {
    'feed8': (('hin0', 0), ('hout0', 0),),
    'feed10': (('hin1', 0), ('hout1', 0), ('hin0', 1), ('hin0', 2),),
    'feed_end': (('hout0', 1), ('hin1', 1), ('hout1', 1), ('hin2', 0), ('hout2', 0), ('hout0', 2), ('hin1', 2), ('hout1', 2),),
    'norm3': (('hin2', 1),),
    'cross0': (('hin2', 2), ('hout2', 1),),
    'cross1': (('hin0', 3), ('hout2', 2),),
    'cross2': (('co', 0),),
    'cross3': (('co', 1), ('hin0', 4), ('hout0', 3),),
    'cross_end': (('hin1', 3), ('hin0', 5), ('co', 2),),
    'mem_half': (('hin0', 6), ('hout0', 4),),
    'mem_end': (('ckv', 0), ('hin0', 7), ('hin1', 4), ('hout1', 3), ('hout0', 5),),
    'self0': (),
    'self1': (('ckv', 1), ('hin0', 8), ('hin2', 3), ('ckv', 2), ('hin1', 5),),
    'self2': (('so', 0), ('hout0', 6), ('hout1', 4),),
    'self3': (('so', 1), ('hin0', 9), ('hin1', 6), ('hout2', 3),),
    'self_end': (('qk', 0), ('vq', 0), ('hout0', 7), ('hout1', 5), ('hin2', 4), ('so', 2), ('hin1', 7), ('co', 3),),
    'fin': (('small', 0), ('qk', 1), ('hout0', 8), ('vq', 1), ('hout2', 4), ('qk', 2), ('small', 1), ('hout1', 6), ('co', 4), ('vq', 2),),
    'end': (('hin2', 5), ('hin1', 8), ('hout0', 9), ('hout2', 5), ('ckv', 3), ('hout1', 7), ('co', 5), ('hin1', 9), ('hin2', 6), ('so', 3), ('hout2', 6), ('hout1', 8), ('ckv', 4), ('co', 6), ('so', 4), ('hin2', 7), ('hout2', 7), ('hout1', 9), ('qk', 3), ('ckv', 5), ('co', 7), ('so', 5), ('hin2', 8), ('hout2', 8), ('qk', 4), ('ckv', 6), ('vq', 3), ('hin2', 9), ('co', 8), ('small', 2), ('so', 6), ('hout2', 9), ('qk', 5), ('ckv', 7), ('so', 7), ('vq', 4), ('qk', 6), ('co', 9), ('small', 3), ('ckv', 8), ('so', 8), ('vq', 5), ('qk', 7), ('ckv', 9), ('small', 4), ('so', 9), ('vq', 6), ('qk', 8), ('small', 5), ('vq', 7), ('qk', 9), ('vq', 8), ('vq', 9),),
}


def layer(bits, ins):
    S = jax.ShapeDtypeStruct
    V, A, M = (pl.BlockSpec(memory_space=s) for s in (pltpu.VMEM, pl.ANY, pltpu.SMEM))
    vm = pltpu.VMEM
    in_names = ("tok", "mem", "cot", "lengths", "mmask", "tags", "emb", "gain1", "gain2", "gain3", "tab", "sq", "sk", "sv", "cq", "ck", "cv",
                "so_in", "co_in", "hin_in", "hout_in")
    in_specs = [V, V, V, M] + [V] * 13 + [A] * 4
    out = {
        "lo": S((256, 768), BF), "gtok": S((256, 768), BF), "gmem": S((1024, 768), BF), "smo": S((2, 8, 256), F32), "dgo": S((8, 256), F32),
        "oqk": S((768, 384), BF), "ovq": S((768, 384), BF), "ockv": S((768, 384), BF), "oso": S((192, 768), BF), "oco": S((192, 768), BF),
        "ohin": S((768, 768), BF), "ohout": S((768, 768), BF),
    }
    out_specs = [V if n in ("smo", "dgo") else A for n in out]
    wide, tall = (256, 768), (768, 256)
    scratch = {
        "vqk": vm((4, 768, 384), BF), "vvq": vm((4, 768, 384), BF), "vckv": vm((4, 768, 384), BF),
        "vso": vm((4, 192, 768), BF), "vco": vm((4, 192, 768), BF), "vhin": vm((4, 768, 768), BF), "vhout": vm((4, 768, 768), BF),
        "s0": vm(wide, F32), "s1": vm(wide, F32), "s2": vm(wide, F32), "gst": vm(wide, F32), "acc": vm(wide, F32),
        "n1": vm(wide, BF), "n2": vm(wide, BF), "n1T": vm(tall, BF), "n2T": vm(tall, BF), "n3T": vm(tall, BF), "memT": vm((768, 1024), BF),
        "qk1": vm((4, 256, 384), BF), "vx1": vm((4, 256, 384), BF), "q2r": vm((4, 256, 384), BF), "kv2": vm((4, 1024, 384), BF),
        "kvT": vm((256, 1024), BF), "mix1": vm((4, 192, 256), BF), "mix2": vm((4, 192, 256), BF), "lse": vm((8, 8, 256), F32),
        "gvq2": vm((4, 256, 384), BF), "rows": vm(wide, BF), "mask2": vm((1024, 128), F32), "tagv": vm((256, 128), F32),
        "btab": vm((4, 8, 256), F32), "sm": vm((6, 8, 256), F32), "smb": vm((2 + bits, 6, 8, 256), F32), "gmv": vm((1024, 768), BF),
        "lov": vm(wide, BF), "gtv": vm(wide, BF),
        "rb1a": vm((2, 768, 768), BF), "rb1b": vm((2, 768, 768), BF), "rb1so": vm((2, 192, 768), BF), "rb1co": vm((2, 192, 768), BF),
        "rb2hin": vm((768, 768), BF), "rb2hout": vm((768, 768), BF),
        "rb2co": vm((192, 768), BF), "rb2so": vm((192, 768), BF), "rb2ckv": vm((768, 384), BF), "rb2qk": vm((768, 384), BF), "rb2vq": vm((768, 384), BF),
    }
    shape_of = {"hin": (768, 256), "hou": (256, 768), "co": (192, 768), "so": (192, 768), "ckv": (768, 384), "qk": (768, 384), "vq": (768, 384)}
    for n in CHUNKS:
        r, w = shape_of[n[:3]]
        k = Chunk(None, 0, r, 0, w, None, None)
        scratch["yb_" + n], scratch["zb_" + n], scratch["wb_" + n] = vm(k.half, BF), vm(k.quarter, BF), vm(k.eighth, BF)
        if bits > 3:
            scratch["eb_" + n] = vm((bits - 3,) + k.eighth, BF)
    dma = pltpu.SemaphoreType.DMA
    sems = {
        "gsend": dma((7, 11)), "grecv": dma((7, 11)), "rsend": dma((11, 6 + bits)), "rrecv": dma((11, 6 + bits)), "lsem": dma((10,)),
        "osem": dma((11,)), "ssend": dma((2 + bits,)), "srecv": dma((2 + bits,)), "tsend": dma((3,)), "trecv": dma((3,)),
        "credit": pltpu.SemaphoreType.REGULAR,
    }
    names = in_names + tuple(out) + tuple(scratch) + tuple(sems)

    def kernel(*refs):
        layer_kernel(bits, names, *refs)

    return pl.pallas_call(
        kernel, out_shape=list(out.values()), in_specs=in_specs, out_specs=out_specs,
        scratch_shapes=list(scratch.values()) + list(sems.values()),
        compiler_params=pltpu.CompilerParams(collective_id=0, has_side_effects=True, vmem_limit_bytes=VMEM_LIMIT),
    )(*ins)


VMEM_LIMIT = 64 * 1024 * 1024 - 64 * 1024


def bucket_of(length=256):
    exact = BUCKETS // 2
    n = np.arange(length)
    far = exact + np.floor(np.log(np.maximum(n, 1) / exact) / math.log(MAX_DISTANCE / exact) * (BUCKETS - exact)).astype(np.int32)
    return np.where(n < exact, n, np.minimum(far, BUCKETS - 1)).astype(np.int32)


def finish_kernel(lo, gtok, gmem, smo, dgo, qk, vq, ckv, so, co, hin, hout,
                  o_lo, o_gtok, o_gmem, o_emb, o_g1, o_g2, o_g3, o_sq, o_sk, o_sv, o_so, o_pb, o_cq, o_ck, o_cv, o_co, o_hin, o_hout):
    o_lo[...] = lo[...]
    o_gtok[...] = gtok[...]
    o_gmem[...] = gmem[...]
    for source, first, second in ((qk, o_sq, o_sk), (vq, o_sv, o_cq), (ckv, o_ck, o_cv)):
        turned = source[...].T.astype(F32)
        first[...] = turned[0:192, :]
        second[...] = turned[192:384, :]
    o_so[...] = so[...].astype(F32)
    o_co[...] = co[...].astype(F32)
    o_hin[...] = hin[...].astype(F32)
    o_hout[...] = hout[...].astype(F32)

    @pl.when(pl.program_id(0) == 0)
    def _():
        def small(row):
            return jnp.concatenate([smo[(3 * row + i) // 8, (3 * row + i) % 8:(3 * row + i) % 8 + 1, :] for i in range(3)], axis=1)
        o_emb[0:1, :] = small(0)
        o_emb[1:2, :] = small(1)
        o_g1[...] = small(2).reshape(768)
        o_g2[...] = small(3).reshape(768)
        o_g3[...] = small(4).reshape(768)
        total = lax.dot_general(dgo[...], bucket_onehot().astype(F32), NT, precision=lax.Precision.HIGHEST, preferred_element_type=F32)
        o_pb[...] = total[0:3, :]


def finish(args):
    S = jax.ShapeDtypeStruct
    n = 2
    cut = lambda r, w: pl.BlockSpec((r // n, w), lambda i: (i, 0))
    turned = pl.BlockSpec((192, 768 // n), lambda i: (0, i))
    full = lambda *s: pl.BlockSpec(s, lambda i: (0,) * len(s))
    flat, square = (192, 768), (768, 768)
    ends = [cut(256, 768), cut(256, 768), cut(1024, 768)]
    in_specs = ends + [full(2, 8, 256), full(8, 256)] + [cut(768, 384)] * 3 + [cut(*flat)] * 2 + [cut(*square)] * 2
    shapes = [S((256, 768), BF), S((256, 768), BF), S((1024, 768), BF), S((2, 768), F32)] + [S((768,), F32)] * 3
    shapes += [S(flat, F32)] * 3 + [S(flat, F32), S((3, 32), F32)] + [S(flat, F32)] * 3 + [S(flat, F32), S(square, F32), S(square, F32)]
    out_specs = ends + [full(2, 768)] + [full(768)] * 3
    out_specs += [turned] * 3 + [cut(*flat), full(3, 32)] + [turned] * 3 + [cut(*flat), cut(*square), cut(*square)]
    return pl.pallas_call(finish_kernel, grid=(n,), out_shape=shapes, in_specs=in_specs, out_specs=out_specs,
                          compiler_params=pltpu.CompilerParams(vmem_limit_bytes=VMEM_LIMIT))(*args)


def per_device(bits, tokens, memory, cotangent, lengths, memory_mask, token_tags, embedding, gain_self, gain_cross, gain_hidden,
               self_query, self_key, self_value, self_output, position_bias, cross_query, cross_key, cross_value,
               cross_output, hidden_in, hidden_out):
    lo, gtok, gmem, smo, dgo, qk, vq, ckv, so, co, hin, hout = layer(bits, (
        tokens[0], memory[0], cotangent[0], lengths, memory_mask, token_tags, embedding, gain_self, gain_cross, gain_hidden, position_bias.T,
        self_query.T, self_key.T, self_value.T, cross_query.T, cross_key.T, cross_value.T, self_output, cross_output, hidden_in, hidden_out))
    (lo, gtok, gmem, g_emb, g1, g2, g3, sq, sk, sv, g_so, pb, cq, ck, cv, g_co, hi, ho) = finish(
        (lo, gtok, gmem, smo, dgo, qk, vq, ckv, so, co, hin, hout))
    return (lo[None], gtok[None], gmem[None], g_emb, g1, g2, g3, sq.T, sk.T, sv.T, g_so, pb.T, cq.T, ck.T, cv.T, g_co, hi, ho)


def solution(mesh):
    bits = int(math.log2(mesh.shape["dp"]))
    item = P(("dp", "tensor"), None, None)
    col, row, rep = P(None, "tensor"), P("tensor", None), P()
    in_specs = (item, item, item, P("dp"), P("dp", None), P(("dp", "tensor"), None), rep, rep, rep, rep,
                col, col, col, row, col, col, col, col, row, col, row)
    out_specs = (item, item, item, rep, rep, rep, rep, col, col, col, row, col, col, col, col, row, col, row)
    return jax.shard_map(lambda *a: per_device(bits, *a), mesh=mesh, in_specs=in_specs, out_specs=out_specs, check_vma=False)
```

```python
import math
from types import SimpleNamespace

import jax
import jax.numpy as jnp
import numpy as np
from jax import lax
from jax.experimental import pallas as pl
from jax.experimental.pallas import tpu as pltpu
from jax.sharding import PartitionSpec as P

EPSILON = 1e-6
MASKED = -1e9
BUCKETS = 32
MAX_DISTANCE = 128
VMEM_LIMIT = 64 * 1024 * 1024 - 64 * 1024
F32 = jnp.float32
BF = jnp.bfloat16
NN = (((1,), (0,)), ((), ()))
NT = (((1,), (1,)), ((), ()))
MESH = pl.DeviceIdType.MESH

UNITS = ((0, 0, 384), (0, 384, 384), (1, 0, 384), (1, 384, 384), (2, 0, 512), (2, 512, 512), (2, 1024, 512))
CHUNKS = (
    (2, 0, 256, 'xyq'),
    (2, 256, 256, 'yqx'),
    (2, 512, 256, 'xyq'),
    (2, 768, 256, 'yzxw'),
    (2, 1024, 128, 'xyzw'),
    (2, 1152, 384, 'xyzw'),
    (1, 384, 384, 'xyzw'),
    (1, 0, 384, 'xyzw'),
    (0, 0, 256, 'xyq'),
    (0, 256, 256, 'xyzw'),
    (0, 512, 128, 'xyzw'),
    (0, 640, 128, 'xyzw'),
)
SCHEDULE = (
    (), (11, 2, 3, 21, 12, 13, 4, 31, 22, 23, 14), (), (), (1,), (32, 33, 41, 24), (), (34, 51), (), (), (42, 43), (52, 53, 61),
    (44, 54), (), (62, 63), (1000, 1010), (64, 1001), (1002, 1011, 1012, 1020, 1030), (), (1021, 1022, 1031, 1032, 1040, 1050),
    (), (), (1041, 1042, 1051, 1052, 1003, 1013), (1060, 1023), (1061, 1033, 1043), (1062, 1004), (1014, 1024, 1034), (), (),
    (1070, 1044), (), (), (1005, 1053, 1071), (1072, 1045), (1080, 1090, 1100, 1110, 1025), (1081,),
    (1082, 1091, 1092, 1101, 1102, 1111, 1006, 1046, 1112, 1054), (200, 1015, 1063),
    (1026, 1047, 201, 1035, 1055, 1007, 1048, 1016, 1064, 1036, 1056, 1027, 1073, 1065, 1049, 1037, 1017, 1057, 1083, 1038, 1066, 1074, 1058, 1084, 1093, 1067, 1075, 1039, 1103, 1085, 1068, 1113, 202, 1059, 1076, 1094, 1104, 1086, 1095, 1077, 1105, 1069, 1096, 1114, 1078, 203, 1106, 1115, 1097, 204, 1087, 1107, 1116, 1098, 1108, 1079, 205, 1117, 1099, 1118, 1109, 1119),
)


class Remote:
    def __init__(self, *args):
        self.args = args

    def made(self):
        src, dst, send, recv, to = self.args
        return pltpu.make_async_remote_copy(
            src_ref=src, dst_ref=dst, send_sem=send, recv_sem=recv, device_id=to, device_id_type=MESH)

    def start(self):
        self.made().start()

    def wait(self):
        self.made().wait()

    def wait_send(self):
        self.made().wait_send()

    def wait_recv(self):
        self.made().wait_recv()


def mm(a, b, d=NN):
    return lax.dot_general(a, b, d, preferred_element_type=F32)


def inverse_of(h):
    return lax.rsqrt(jnp.mean(h * h, axis=-1, keepdims=True) + EPSILON)


def norm_back(h, inv, g, r):
    s = r * g
    gain = jnp.sum(r * h * inv, axis=0, keepdims=True)
    return inv * s - h * (inv * inv * inv) * jnp.mean(s * h, axis=-1, keepdims=True), gain


def rows_of(start, size):
    return pl.ds(pl.multiple_of(start, 16), size)


def add_into(dst, parts, into=None):
    rows = dst.shape[0]
    into = dst if into is None else into
    step = next(n for n in (64, 48, 32, 16) if rows % n == 0)

    def block(i, _):
        at = rows_of(i * step, step)
        total = dst[at, :].astype(F32)
        for part in parts:
            total = total + part[at, :].astype(F32)
        into[at, :] = total.astype(BF)
        return 0

    lax.fori_loop(0, rows // step, block, 0)


def bucket_of(length=256):
    exact = BUCKETS // 2
    n = np.arange(length)
    far = exact + np.floor(np.log(np.maximum(n, 1) / exact) / math.log(MAX_DISTANCE / exact) * (BUCKETS - exact)).astype(np.int32)
    return np.where(n < exact, n, np.minimum(far, BUCKETS - 1)).astype(np.int32)


def bucket_onehot():
    bucket = bucket_of()
    n = lax.broadcasted_iota(jnp.int32, (BUCKETS, 256), 1)
    chosen = jnp.zeros((BUCKETS, 256), jnp.int32)
    for b in range(1, BUCKETS):
        chosen = chosen + jnp.where(n >= int(np.argmax(bucket >= b)), 1, 0)
    return (chosen == lax.broadcasted_iota(jnp.int32, (BUCKETS, 256), 0)).astype(BF)


def third(size, i):
    cut = {96: (32, 32, 32), 128: (32, 48, 48)}[size]
    return sum(cut[:i]), cut[i]


def layer_kernel(bits, r):
    dp = lax.axis_index("dp")
    t = lax.axis_index("tensor")
    c = lax.rem(t, 2)
    x = t // 2
    tc = t + 1 - 2 * c
    tx = t + 2 - 4 * x
    td = tc + 2 - 4 * x
    bit = [lax.rem(dp // (1 << b), 2) for b in range(bits)]
    pb = [dp + (1 << b) - (2 << b) * bit[b] for b in range(bits)]
    y, z1, z2 = bit[0], bit[1], bit[2]
    quad, quad_y, quad_z = y + 2 * z1, (1 - y) + 2 * z1, y + 2 * (1 - z1)
    quad_d = 3 - quad
    weights = (r.own, r.cross, r.feed)

    def fwd_shard(s):
        a, b = lax.rem(s, 2), s // 2
        return 2 * (x + b * (1 - 2 * x)) + c + a * (1 - 2 * c)

    def bwd_shard(s):
        a, b = 1 - s // 2, 1 - lax.rem(s, 2)
        return 2 * (x + b * (1 - 2 * x)) + c + a * (1 - 2 * c)

    loads = []

    def load(src, dst):
        loads.append(pltpu.make_async_copy(src, dst, r.lsem.at[len(loads)]))
        loads[-1].start()
        return loads[-1]

    slot = lambda v, i: v.at[t, pl.ds(192 * i, 192), :]
    token_load = load(r.tok_in, r.tok)
    self_loads = [load(src, slot(r.own, i)) for i, src in enumerate((r.sq, r.sk, r.sv, r.so))]
    cross_loads = [load(src, slot(r.cross, i)) for i, src in enumerate((r.ck, r.cv, r.cq, r.co))]
    hin_load = load(r.hin, r.raw)
    hout_loads = [load(r.hout.at[pl.ds(256 * i, 256), :], r.feed.at[t, pl.ds(512 * i + 256, 256), :]) for i in range(3)]
    memory_load = load(r.mem_in, r.mem)
    cotangent_load = load(r.cot_in, r.cot)

    barrier = pltpu.get_barrier_semaphore()
    partners = [(dp, tc), (dp, tx), (dp, td)] + [(p, t) for p in pb]
    for p in partners:
        pl.semaphore_signal(barrier, inc=1, device_id=p, device_id_type=MESH)

    g_self, g_cross, g_hid = (g[...].astype(F32).reshape(1, 768) for g in (r.gain1, r.gain2, r.gain3))
    ji = lax.broadcasted_iota(jnp.int32, (256, 256), 0)
    ii = lax.broadcasted_iota(jnp.int32, (256, 256), 1)
    length = r.lengths[t]
    allowed = lambda: (ji <= ii) & (ji < length)
    r.btab[t, 0:3, :] = mm(r.tab[...], bucket_onehot())
    r.tagv[...] = jnp.broadcast_to((r.tags[...] == 1).astype(F32), (128, 256)).T
    tagged = lambda: jnp.concatenate([r.tagv[...]] * 6, axis=1) > 0.5
    token_load.wait()
    x0 = r.tok[...].astype(F32) + jnp.where(tagged(), r.emb[1:2, :].astype(F32), r.emb[0:1, :].astype(F32))
    r.s0[...] = x0
    r.n1[...] = (x0 * inverse_of(x0) * g_self).astype(BF)
    for d in self_loads:
        d.wait()
    pl.semaphore_wait(barrier, len(partners))

    def gather_copy(u, j):
        a, row, size = UNITS[u]
        v, q = weights[a], size // 4
        sems = (r.gsend.at[u, j], r.grecv.at[u, j])
        at = lambda shard, quarter, first=0, n=q: v.at[shard, rows_of(row + quarter * q + first, n), :]
        core, over_x, over_y, over_z = (dp, tc), (dp, tx), (pb[0], t), (pb[1], t)
        if j == 0:
            ref, to = v.at[t, pl.ds(row, size), :], core
        elif j == 1:
            ref, to = at(t, quad), over_x
        elif j == 2:
            ref, to = at(t, quad_d, *third(q, 0)), over_x
        elif j == 3:
            ref, to = at(tx, quad), over_y
        elif j == 4:
            ref, to = at(tx, quad), over_z
        elif j == 5:
            ref, to = at(tx, quad), core
        elif j == 6:
            ref, to = at(tx, quad_y, *third(q, 2)), over_z
        elif j == 7:
            ref, to = at(tx, quad_y), core
        elif j == 8:
            ref, to = at(tx, quad_z, *third(q, 1)), over_y
        elif j == 9:
            ref, to = at(tx, quad_z), core
        else:
            ref, to = at(tx, quad_d), core
        return Remote(ref, ref, *sems, to)

    GATHER = {0: ((), (1, 2, 0)), 1: ((1,), (3, 4, 5)), 2: ((3,), (6, 7)), 3: ((4,), (8, 9)), 4: ((2, 8, 6), (10,)),
              5: ((0,), ()), 6: ((5, 7, 9, 10), ())}

    def gather_step(u, step):
        arrived, onward = GATHER[step]
        for j in arrived:
            gather_copy(u, j).wait_recv()
        for j in onward:
            gather_copy(u, j).start()

    def gather_sent(us, js):
        for u in us:
            for j in js:
                gather_copy(u, j).wait_send()

    last_of_feed = max(n for n, k in enumerate(CHUNKS) if k[0] == 2)

    def view(n, shard, first=0, size=None):
        a, row, rows, _ = CHUNKS[n]
        return weights[a].at[shard, rows_of(row + first, rows if size is None else size), :]

    def place(n, halves):
        first, size = 0, CHUNKS[n][2]
        for b in halves:
            size = size // 2
            first = first + b * size
        return first, size

    def result(n, halves):
        first, size = place(n, halves)
        return r.result[n].at[rows_of(first, size), :]

    flips = ((0, 1), (1, 0), (1, 1))
    turn = lambda b, f: b + f * (1 - 2 * b)
    along_z = [dp + f1 * (2 - 4 * z1) + f2 * (4 - 8 * z2) for f1, f2 in flips]

    def plan_of(n):
        order, buffers = CHUNKS[n][3], iter(r.parts[n])
        halves, shards, stages, gathers, count = [], [tx, t], [], [], iter(range(99))

        def copy(src, dst, to):
            j = next(count)
            return Remote(src, dst, r.rsend.at[n, j], r.rrecv.at[n, j], to)

        def piece(shard, at):
            return view(n, shard, *place(n, at))

        for d in order:
            buf = next(buffers)
            if d == "x":
                stages.append(([copy(piece(tx, halves), buf.at[0], (dp, tx))], [(piece(t, halves), [buf.at[0]])]))
                shards = [t]
                continue
            if d == "q":
                mine, others = [z1, z2], [([turn(z1, f1), turn(z2, f2)], p) for (f1, f2), p in zip(flips, along_z)]
            else:
                b = "yzw".index(d)
                mine, others = [bit[b]], [([1 - bit[b]], pb[b])]
            m = len(others)
            stages.append((
                [copy(piece(k, halves + o), buf.at[m * i + j], (p, t)) for i, k in enumerate(shards) for j, (o, p) in enumerate(others)],
                [(piece(k, halves + mine), [buf.at[m * i + j] for j in range(m)]) for i, k in enumerate(shards)]))
            halves = halves + mine
            gathers.append((list(halves), [p for _, p in others]))
        back = [[copy(result(n, at), result(n, at), (p, t)) for p in ps] for at, ps in reversed(gathers)]
        more = [(copy(piece(t, halves), r.more[n].at[b - 3], (pb[b], t)), r.more[n].at[b - 3]) for b in range(3, bits)]
        core = [copy(view(n, td), r.first[n].at[0], (dp, tc)), copy(view(n, tc), r.first[n].at[1], (dp, tc))]
        return SimpleNamespace(core=core, stages=stages, back=back, more=more, mine=piece(t, halves), result=result(n, halves))

    plans = [plan_of(n) for n in range(len(CHUNKS))]

    def out_copy(n):
        a, row, rows, _ = CHUNKS[n]
        return pltpu.make_async_copy(r.result[n], (r.own_out, r.cross_out, r.feed_out)[a].at[pl.ds(row, rows), :], r.osem.at[n])

    def start(copies):
        for d in copies:
            d.start()

    def reduce_step(n, j):
        p = plans[n]
        x_first = CHUNKS[n][3][0] == "x"
        if j == 0:
            if n == last_of_feed + 1:
                pl.semaphore_wait(r.credit, 1)
            start(p.core)
        elif j == 1:
            p.core[0].wait_recv()
            add_into(view(n, tx), [r.first[n].at[0]])
            if x_first:
                start(p.stages[0][0])
        elif j == 2:
            p.core[1].wait_recv()
            add_into(view(n, t), [r.first[n].at[1]])
            if n == last_of_feed:
                pl.semaphore_signal(r.credit, inc=1, device_id=(dp, tc), device_id_type=MESH)
            if not x_first:
                start(p.stages[0][0])
        elif j - 3 < len(p.stages):
            copies, sums = p.stages[j - 3]
            for d in copies:
                d.wait_recv()
            last = j - 2 == len(p.stages)
            for target, parts in sums:
                add_into(target, parts, p.result if last and not p.more else None)
            if not last:
                start(p.stages[j - 2][0])
                return
            for i, (copy, part) in enumerate(p.more):
                copy.start()
                copy.wait()
                add_into(p.mine, [part], p.result if i + 1 == len(p.more) else None)
            start(p.back[0])
        else:
            i = j - 3 - len(p.stages)
            for d in p.back[i]:
                d.wait_recv()
            if i + 1 < len(p.back):
                start(p.back[i + 1])
            else:
                out_copy(n).start()

    to = [(dp, tc), (dp, tx)] + [(p, t) for p in pb]

    def small_step(j):
        if j:
            Remote(r.sm, r.smb.at[j - 1], r.ssend.at[j - 1], r.srecv.at[j - 1], to[j - 1]).wait()
            r.sm[...] = r.sm[...] + r.smb[j - 1]
        if j < len(to):
            Remote(r.sm, r.smb.at[j], r.ssend.at[j], r.srecv.at[j], to[j]).start()

    places = iter(SCHEDULE)

    def run(todo):
        for e in todo:
            if e >= 1000:
                reduce_step((e - 1000) // 10, e % 10)
            elif e >= 200:
                small_step(e - 200)
            else:
                gather_step(e // 10, e % 10)

    def here():
        run(next(places))

    def take(count):
        return [next(places) for _ in range(count)]

    def hooks(s, todos, extra=None):
        for k, todo in enumerate(todos):
            more = (extra or {}).get(k)
            if todo or more:
                @pl.when(s == k)
                def _():
                    run(todo)
                    if more:
                        more()

    gather_step(0, 0)
    gather_step(1, 0)
    tables = [Remote(r.btab.at[t], r.btab.at[t], r.tsend.at[j], r.trecv.at[j], (dp, k)) for j, k in enumerate((tc, tx, td))]
    for d in tables:
        d.start()
    for d in cross_loads:
        d.wait()
    gather_step(2, 0)
    gather_step(3, 0)
    hin_load.wait()
    for d in hout_loads:
        d.wait()
    for i in range(3):
        r.feed[t, 512 * i:512 * i + 256, :] = r.raw[:, 256 * i:256 * i + 256].T
        gather_step(4 + i, 0)
    def bias_of(shard, i):
        return pltpu.roll(jnp.broadcast_to(r.btab[shard, i:i + 1, :], (256, 256)), 0, 1, stride=1, stride_axis=0)

    lane576 = lax.broadcasted_iota(jnp.int32, (1, 576), 1)

    def project_memory(shard):
        w = r.cross.at[shard, pl.ds(0, 384), :]

        def block(i, _):
            at = rows_of(i * 256, 256)
            r.kv[shard, at, :] = mm(r.mem[at, :], w[...], NT).astype(BF)
            return 0
        lax.fori_loop(0, 4, block, 0)
        for i in range(4):
            r.kvT[shard, :, 256 * i:256 * i + 256] = mm(w[...], r.mem[256 * i:256 * i + 256, :], NT).astype(BF)

    def near_memory():
        memory_load.wait()
        valid = r.mmask[pl.ds(t, 1), :]
        r.mask2[...] = jnp.broadcast_to(jnp.where(valid == 1, 0.0, MASKED).astype(F32), (128, 1024)).T
        project_memory(t)
        run(inside[0])
        gather_step(2, 5)
        project_memory(tc)
        run(inside[1])
        gather_step(0, 6)
        gather_step(1, 6)

    def self_near():
        gather_step(0, 5)
        gather_step(1, 5)
        for d in tables:
            d.wait_recv()

    def self_forward(s, _):
        hooks(s, turns, {1: self_near, 2: near_memory})
        k = fwd_shard(s)
        w = r.own.at[k, pl.ds(0, 576), :]
        a = mm(r.n1[...], w[...], NT)
        r.qkv[k] = jnp.where(lane576 < 192, a * 0.125, a).astype(BF)
        r.kvT1[k] = mm(r.own[k, 192:576, :], r.n1[...], NT).astype(BF)
        for i in range(3):
            q, kk = r.qkv[k, :, 64 * i:64 * i + 64], r.qkv[k, :, 192 + 64 * i:256 + 64 * i]
            scores = jnp.where(allowed(), mm(kk, q, NT) + bias_of(k, i), MASKED)
            most = jnp.max(scores, axis=0, keepdims=True)
            p = jnp.exp(scores - most)
            total = jnp.sum(p, axis=0, keepdims=True)
            o = mm(r.kvT1[k, 192 + 64 * i:256 + 64 * i, :], p.astype(BF))
            r.mix1[k, 64 * i:64 * i + 64, :] = (o / total).astype(BF)
            r.lse[k, i:i + 1, :] = most + jnp.log(total)
        return 0

    def project_out(target, mix, w):
        def block(k, _):
            target[...] += mm(mix[k].T, w[k, 576:768, :])
            return 0
        lax.fori_loop(0, 4, block, 0)

    inside, turns = take(2), take(4)
    lax.fori_loop(0, 4, self_forward, 0)
    here()
    r.s1[...] = r.s0[...]
    project_out(r.s1, r.mix1, r.own)
    x1 = r.s1[...]
    r.n2[...] = (x1 * inverse_of(x1) * g_cross).astype(BF)
    here()
    gather_step(3, 5)

    def cross_scores(shard, i, b, q):
        at = slice(256 * b, 256 * b + 256)
        return mm(r.kv[shard, at, 64 * i:64 * i + 64], q, NT) + jnp.concatenate([r.mask2[at, :]] * 2, axis=1)

    def far_memory_1():
        project_memory(tx)

    def far_memory_2():
        gather_step(2, 6)
        gather_step(3, 6)
        project_memory(td)

    def cross_forward(s, _):
        hooks(s, turns_1, {2: far_memory_1, 3: far_memory_2})
        k = fwd_shard(s)
        w = r.cross.at[k, pl.ds(384, 192), :]
        r.q2[k] = (mm(r.n2[...], w[...], NT) * 0.125).astype(BF)
        for i in range(3):
            q = r.q2[k, :, 64 * i:64 * i + 64]
            ss = [cross_scores(k, i, b, q) for b in range(4)]
            most = jnp.max(jnp.maximum(jnp.maximum(ss[0], ss[1]), jnp.maximum(ss[2], ss[3])), axis=0, keepdims=True)
            total, o = 0.0, 0.0
            for b in range(4):
                p = jnp.exp(ss[b] - most)
                total = total + jnp.sum(p, axis=0, keepdims=True)
                o = o + mm(r.kvT[k, 192 + 64 * i:256 + 64 * i, 256 * b:256 * b + 256], p.astype(BF))
            r.mix2[k, 64 * i:64 * i + 64, :] = (o / total).astype(BF)
            r.lse[4 + k, i:i + 1, :] = most + jnp.log(total)
        return 0

    turns_1 = take(4)
    lax.fori_loop(0, 4, cross_forward, 0)
    here()
    r.s2[...] = r.s1[...]
    project_out(r.s2, r.mix2, r.cross)
    x2 = r.s2[...]
    r.rows[...] = (x2 * inverse_of(x2) * g_hid).astype(BF)
    r.acc[...] = x2
    r.gst[...] = jnp.zeros_like(x2)
    cotangent_load.wait()
    for u in (4, 5, 6):
        gather_step(u, 5)

    def feed_waits(u):
        def far():
            gather_step(u, 6)
            gather_sent((u,), range(3, 11))
        return {0: lambda: gather_sent((u,), (0, 1, 2)), 1: far}

    def feed(j, _):
        hooks(j, turns_2, {2 * i + k: f for i in range(3) for k, f in feed_waits(4 + i).items()})
        pair = lax.rem(j, 2)
        first = (j // 2) * 512
        refs, acts, gbs = [], [], []
        for i in range(2):
            k = fwd_shard(2 * pair + i)
            w_in, w_out = (r.feed.at[k, rows_of(first + 256 * m, 256), :] for m in range(2))
            v = mm(r.rows[...], w_in[...], NT)
            ga = mm(r.cot[...], w_out[...], NT)
            phi = 0.5 * (1.0 + lax.erf(v * np.float32(1 / math.sqrt(2))))
            acts.append((v * phi).astype(BF))
            slope = phi + v * (jnp.exp(-0.5 * v * v) * np.float32(1 / math.sqrt(2 * math.pi)))
            gbs.append((slope * ga).astype(BF))
            refs.append((w_in, w_out))
        r.acc[...] += mm(acts[0], refs[0][1][...]) + mm(acts[1], refs[1][1][...])
        r.gst[...] += mm(gbs[0], refs[0][0][...]) + mm(gbs[1], refs[1][0][...])
        for (w_in, w_out), act, gb in zip(refs, acts, gbs):
            w_in[...] = mm(gb.T, r.rows[...]).astype(BF)
            w_out[...] = mm(act.T, r.cot[...]).astype(BF)
        return 0

    turns_2 = take(6)
    lax.fori_loop(0, 6, feed, 0)
    here()
    gather_sent(range(4), range(11))
    for d in tables:
        d.wait_send()
    r.lov[...] = r.acc[...].astype(BF)
    stores = [pltpu.make_async_copy(a, b, r.esem.at[i]) for i, (a, b) in enumerate(((r.lov, r.lo), (r.gmv, r.gmem), (r.gtv, r.gtok)))]
    stores[0].start()
    d, gain = norm_back(x2, inverse_of(x2), g_hid, r.gst[...])

    def put_small(row, value):
        for i in range(3):
            at = 3 * row + i
            r.sm[at // 8, at % 8:at % 8 + 1, :] = value[:, 256 * i:256 * i + 256]

    r.sm[...] = jnp.zeros_like(r.sm)
    put_small(4, gain)
    r.gst[...] = r.cot[...].astype(F32) + d
    here()
    r.rows[...] = r.gst[...].astype(BF)
    r.acc[...] = jnp.zeros_like(x2)

    def cross_backward(s, _):
        hooks(s, turns_3)
        k = bwd_shard(s)
        rw = r.rows[...]
        w = r.cross[k, 576:768, :]
        G = mm(rw, w, NT).astype(BF)
        GT = mm(w, rw, NT).astype(BF)
        r.cross[k, 576:768, :] = mm(r.mix2[k], rw).astype(BF)
        dqs, dks, dvs = [], [], []
        for i in range(3):
            q = r.q2[k, :, 64 * i:64 * i + 64]
            gi, gT = G[:, 64 * i:64 * i + 64], GT[64 * i:64 * i + 64, :]
            inner = jnp.sum(r.mix2[k, 64 * i:64 * i + 64, :].astype(F32) * gT.astype(F32), axis=0, keepdims=True)
            ls = r.lse[4 + k, i:i + 1, :]
            dq, dk, dv = 0.0, [], []
            for b in range(4):
                at = slice(256 * b, 256 * b + 256)
                p = jnp.exp(cross_scores(k, i, b, q) - ls)
                dp_ = mm(r.kv[k, at, 192 + 64 * i:256 + 64 * i], gi, NT)
                gs = (p * (dp_ - inner)).astype(BF)
                dq = dq + mm(r.kvT[k, 64 * i:64 * i + 64, at], gs)
                dk.append(mm(gs, q).astype(BF))
                dv.append(mm(p.astype(BF), gi).astype(BF))
            dqs.append((dq * 0.125).astype(BF))
            dks.append(dk)
            dvs.append(dv)
        for b in range(4):
            r.kv[k, 256 * b:256 * b + 256, :] = jnp.concatenate([v[b] for v in dks + dvs], axis=1)
        r.kvT[k] = r.kv[k].T
        dqT = jnp.concatenate(dqs, axis=0)
        r.acc[...] += mm(dqT.T, r.cross[k, 384:576, :])
        r.cross[k, 384:576, :] = mm(dqT, r.n2[...]).astype(BF)
        return 0

    turns_3 = take(4)
    lax.fori_loop(0, 4, cross_backward, 0)
    here()

    def memory_grad(i, _):
        at = rows_of(i * 256, 256)
        total = 0.0
        for k in range(4):
            total = total + mm(r.kv[k, at, :], r.cross[k, 0:384, :])
        r.gmv[at, :] = total.astype(BF)
        return 0

    lax.fori_loop(0, 4, memory_grad, 0)
    stores[1].start()
    here()

    def memory_weights(s, _):
        hooks(s, turns_4)
        k = bwd_shard(s)

        def block(i, _):
            at = rows_of(i * 192, 192)
            r.cross[k, at, :] = mm(r.kvT[k, at, :], r.mem[...]).astype(BF)
            return 0
        lax.fori_loop(0, 2, block, 0)
        return 0

    turns_4 = take(4)
    lax.fori_loop(0, 4, memory_weights, 0)
    here()
    d, gain = norm_back(r.s1[...], inverse_of(r.s1[...]), g_cross, r.acc[...])
    put_small(3, gain)
    r.gst[...] += d
    r.rows[...] = r.gst[...].astype(BF)
    r.acc[...] = jnp.zeros_like(x2)

    def self_backward(s, _):
        hooks(s, turns_5)
        k = bwd_shard(s)
        rw = r.rows[...]
        w = r.own[k, 576:768, :]
        G = mm(rw, w, NT).astype(BF)
        GT = mm(w, rw, NT).astype(BF)
        r.own[k, 576:768, :] = mm(r.mix1[k], rw).astype(BF)
        flip = (ji + ii == 255).astype(BF)
        dqs, dks, dvs = [], [], []
        for i in range(3):
            q, kk = r.qkv[k, :, 64 * i:64 * i + 64], r.qkv[k, :, 192 + 64 * i:256 + 64 * i]
            gi, gT = G[:, 64 * i:64 * i + 64], GT[64 * i:64 * i + 64, :]
            inner = jnp.sum(r.mix1[k, 64 * i:64 * i + 64, :].astype(F32) * gT.astype(F32), axis=0, keepdims=True)
            scores = jnp.where(allowed(), mm(kk, q, NT) + bias_of(k, i), MASKED)
            p = jnp.exp(scores - r.lse[k, i:i + 1, :])
            dp_ = mm(r.qkv[k, :, 384 + 64 * i:448 + 64 * i], gi, NT)
            gs = (p * (dp_ - inner)).astype(BF)
            dvs.append(mm(p.astype(BF), gi).astype(BF))
            dks.append(mm(gs, q).astype(BF))
            dqs.append((mm(r.kvT1[k, 64 * i:64 * i + 64, :], gs) * 0.125).astype(BF))
            shifted = pltpu.roll(mm(flip, gs), 1, 1, stride=1, stride_axis=0)
            r.sm[2 + k, i:i + 1, :] = jnp.sum(shifted, axis=0, keepdims=True)
        dqT = jnp.concatenate(dqs, axis=0)
        dkv = jnp.concatenate(dks + dvs, axis=1)
        r.acc[...] += mm(dqT.T, r.own[k, 0:192, :]) + mm(dkv, r.own[k, 192:576, :])
        r.own[k, 0:192, :] = mm(dqT, r.n1[...]).astype(BF)
        r.own[k, 192:576, :] = mm(dkv.T, r.n1[...]).astype(BF)
        return 0

    turns_5 = take(4)
    lax.fori_loop(0, 4, self_backward, 0)
    here()
    d, gain = norm_back(r.s0[...], inverse_of(r.s0[...]), g_self, r.acc[...])
    put_small(2, gain)
    g0 = r.gst[...] + d
    r.gtv[...] = g0.astype(BF)
    stores[2].start()
    put_small(0, jnp.sum(jnp.where(tagged(), 0.0, g0), axis=0, keepdims=True))
    put_small(1, jnp.sum(jnp.where(tagged(), g0, 0.0), axis=0, keepdims=True))
    here()
    here()
    for j in range(6, len(to) + 1):
        small_step(j)
    r.smo[...] = r.sm[0:2]
    r.dgo[...] = r.sm[2 + t]
    for n, p in enumerate(plans):
        for d in p.core + sum([copies for copies, _ in p.stages], []) + sum(p.back, []):
            d.wait_send()
        out_copy(n).wait()
    for d in stores:
        d.wait()


def layer(bits, ins):
    S = jax.ShapeDtypeStruct
    V, A, M = (pl.BlockSpec(memory_space=s) for s in (pltpu.VMEM, pl.ANY, pltpu.SMEM))
    vm = pltpu.VMEM
    inputs = dict(tok_in=A, mem_in=A, cot_in=A, lengths=M, mmask=V, tags=V, emb=V, gain1=V, gain2=V, gain3=V, tab=V,
                  sq=A, sk=A, sv=A, so=A, cq=A, ck=A, cv=A, co=A, hin=A, hout=A)
    wide, square = (256, 768), (768, 768)
    out = dict(lo=S(wide, BF), gtok=S(wide, BF), gmem=S((1024, 768), BF), smo=S((2, 8, 256), F32), dgo=S((8, 256), F32),
               own_out=S(square, BF), cross_out=S(square, BF), feed_out=S((1536, 768), BF))
    out_specs = [A, A, A, V, V, A, A, A]
    sizes = [n for _, _, n, _ in CHUNKS]

    def parts_of(n, order):
        shards, buffers = 2, []
        for d in order:
            if d == "x":
                shards = 1
                buffers.append(vm((1, n, 768), BF))
            else:
                n = n // 4 if d == "q" else n // 2
                buffers.append(vm((shards * (3 if d == "q" else 1), n, 768), BF))
        return buffers

    scratch = dict(
        own=vm((4, 768, 768), BF), cross=vm((4, 768, 768), BF), feed=vm((4, 1536, 768), BF), raw=vm(square, BF),
        tok=vm(wide, BF), cot=vm(wide, BF), mem=vm((1024, 768), BF),
        s0=vm(wide, F32), s1=vm(wide, F32), s2=vm(wide, F32), gst=vm(wide, F32), acc=vm(wide, F32),
        n1=vm(wide, BF), n2=vm(wide, BF), rows=vm(wide, BF),
        qkv=vm((4, 256, 576), BF), kvT1=vm((4, 384, 256), BF), q2=vm((4, 256, 192), BF),
        kv=vm((4, 1024, 384), BF), kvT=vm((4, 384, 1024), BF), mix1=vm((4, 192, 256), BF), mix2=vm((4, 192, 256), BF),
        lse=vm((8, 8, 256), F32), mask2=vm((1024, 128), F32), tagv=vm((256, 128), F32), btab=vm((4, 8, 256), F32),
        sm=vm((6, 8, 256), F32), smb=vm((2 + bits, 6, 8, 256), F32), gmv=vm((1024, 768), BF), lov=vm(wide, BF), gtv=vm(wide, BF),
        receive=vm((2, 1536, 768), BF),
    )
    parts = [parts_of(n, order) for _, _, n, order in CHUNKS]
    results = [vm((n, 768), BF) for n in sizes]
    more = [vm((bits - 3, n // 8, 768), BF) for n in sizes] if bits > 3 else []
    dma = pltpu.SemaphoreType.DMA
    sems = dict(gsend=dma((7, 11)), grecv=dma((7, 11)), rsend=dma((len(CHUNKS), 16 + bits)), rrecv=dma((len(CHUNKS), 16 + bits)), lsem=dma((15,)), osem=dma((len(CHUNKS),)),
                esem=dma((3,)), ssend=dma((2 + bits,)), srecv=dma((2 + bits,)), tsend=dma((3,)), trecv=dma((3,)),
                credit=pltpu.SemaphoreType.REGULAR)
    names = list(inputs) + list(out) + list(scratch) + list(sems)

    def kernel(*refs):
        r = SimpleNamespace(**dict(zip(names, refs)))
        rest = iter(refs[len(names):])
        r.parts = [[next(rest) for _ in p] for p in parts]
        r.result = [next(rest) for _ in results]
        r.more = [next(rest) for _ in more]
        r.first, at = [], [0, 0]
        for a, _, n, _ in CHUNKS:
            shared = int(a != 2)
            r.first.append(r.receive.at[:, pl.ds(at[shared], n), :])
            at[shared] += n
        layer_kernel(bits, r)

    return pl.pallas_call(
        kernel, out_shape=list(out.values()), in_specs=list(inputs.values()), out_specs=out_specs,
        scratch_shapes=list(scratch.values()) + list(sems.values()) + sum(parts, []) + results + more,
        compiler_params=pltpu.CompilerParams(collective_id=0, has_side_effects=True, vmem_limit_bytes=VMEM_LIMIT),
    )(*ins)


def finish_kernel(lo, gtok, gmem, smo, dgo, own, cross, feed,
                  o_lo, o_gtok, o_gmem, o_emb, o_g1, o_g2, o_g3, o_sq, o_sk, o_sv, o_so, o_pb, o_cq, o_ck, o_cv, o_co, o_hin, o_hout):
    o_lo[...] = lo[...]
    o_gtok[...] = gtok[...]
    o_gmem[...] = gmem[...]
    for i, o in enumerate((o_sq, o_sk, o_sv, o_so)):
        o[...] = own[192 * i:192 * i + 192, :].astype(F32)
    for i, o in enumerate((o_ck, o_cv, o_cq, o_co)):
        o[...] = cross[192 * i:192 * i + 192, :].astype(F32)
    for i in range(3):
        o_hin[:, 256 * i:256 * i + 256] = feed[512 * i:512 * i + 256, :].T.astype(F32)
        o_hout[256 * i:256 * i + 256, :] = feed[512 * i + 256:512 * i + 512, :].astype(F32)

    @pl.when(pl.program_id(0) == 0)
    def _():
        def small(row):
            return jnp.concatenate([smo[(3 * row + i) // 8, (3 * row + i) % 8:(3 * row + i) % 8 + 1, :] for i in range(3)], axis=1)
        o_emb[0:1, :] = small(0)
        o_emb[1:2, :] = small(1)
        o_g1[...] = small(2).reshape(768)
        o_g2[...] = small(3).reshape(768)
        o_g3[...] = small(4).reshape(768)
        total = lax.dot_general(dgo[...], bucket_onehot().astype(F32), NT, precision=lax.Precision.HIGHEST, preferred_element_type=F32)
        o_pb[...] = total[0:3, :]


def finish(args):
    S = jax.ShapeDtypeStruct
    n = 3
    cut = lambda rows: pl.BlockSpec((rows, 768 // n), lambda i: (0, i))
    full = lambda *s: pl.BlockSpec(s, lambda i: (0,) * len(s))
    flat, square = S((192, 768), F32), S((768, 768), F32)
    shapes = [S((256, 768), BF), S((256, 768), BF), S((1024, 768), BF), S((2, 768), F32)] + [S((768,), F32)] * 3
    shapes += [flat] * 4 + [S((3, 32), F32)] + [flat] * 4 + [square, square]
    ends = [cut(256), cut(256), cut(1024)]
    in_specs = ends + [full(2, 8, 256), full(8, 256), cut(768), cut(768), cut(1536)]
    out_specs = ends + [full(2, 768)] + [full(768)] * 3 + [cut(192)] * 4 + [full(3, 32)] + [cut(192)] * 4
    out_specs += [pl.BlockSpec((768 // n, 768), lambda i: (i, 0)), cut(768)]
    return pl.pallas_call(finish_kernel, grid=(n,), out_shape=shapes, in_specs=in_specs, out_specs=out_specs,
                          compiler_params=pltpu.CompilerParams(vmem_limit_bytes=VMEM_LIMIT))(*args)


def per_device(bits, tokens, memory, cotangent, lengths, memory_mask, token_tags, embedding, gain_self, gain_cross, gain_hidden,
               self_query, self_key, self_value, self_output, position_bias, cross_query, cross_key, cross_value,
               cross_output, hidden_in, hidden_out):
    parts = layer(bits, (
        tokens[0], memory[0], cotangent[0], lengths, memory_mask, token_tags, embedding, gain_self, gain_cross, gain_hidden, position_bias.T,
        self_query.T, self_key.T, self_value.T, self_output, cross_query.T, cross_key.T, cross_value.T, cross_output, hidden_in, hidden_out))
    lo, gtok, gmem, g_emb, g1, g2, g3, sq, sk, sv, so, pb, cq, ck, cv, co, hin, hout = finish(parts)
    return (lo[None], gtok[None], gmem[None], g_emb, g1, g2, g3, sq.T, sk.T, sv.T, so, pb.T, cq.T, ck.T, cv.T, co, hin, hout)


def solution(mesh):
    bits = int(math.log2(mesh.shape["dp"]))
    item = P(("dp", "tensor"), None, None)
    col, row, rep = P(None, "tensor"), P("tensor", None), P()
    in_specs = (item, item, item, P("dp"), P("dp", None), P(("dp", "tensor"), None), rep, rep, rep, rep,
                col, col, col, row, col, col, col, col, row, col, row)
    out_specs = (item, item, item, rep, rep, rep, rep, col, col, col, row, col, col, col, col, row, col, row)
    return jax.shard_map(lambda *a: per_device(bits, *a), mesh=mesh, in_specs=in_specs, out_specs=out_specs, check_vma=False)
```

```python
import math
from types import SimpleNamespace

import jax
import jax.numpy as jnp
import numpy as np
from jax import lax
from jax.experimental import pallas as pl
from jax.experimental.pallas import tpu as pltpu
from jax.sharding import PartitionSpec as P

EPSILON = 1e-6
MASKED = -1e9
BUCKETS = 32
MAX_DISTANCE = 128
VMEM_LIMIT = 64 * 1024 * 1024 - 64 * 1024
F32 = jnp.float32
BF = jnp.bfloat16
NN = (((1,), (0,)), ((), ()))
NT = (((1,), (1,)), ((), ()))
MESH = pl.DeviceIdType.MESH

UNITS = ((0, 384), (384, 384))
CHUNKS = (
    (2, 0, 256, 'yq'),
    (2, 256, 256, 'yq'),
    (2, 512, 256, 'yzw'),
    (2, 768, 256, 'yzw'),
    (2, 1024, 512, 'yzw'),
    (1, 384, 128, 'yxzw'),
    (1, 512, 256, 'xyzw'),
    (1, 0, 256, 'xyzw'),
    (1, 256, 128, 'xzwy'),
    (0, 0, 384, 'yq'),
    (0, 384, 384, 'yzw'),
)
SCHEDULE = (
    (), (), (), (), (), (), (1, 11, 2, 3, 12, 13, 4), (), (14,), (), (), (), (), (), (), (), (), (1000, 1010, 1020),
    (1030, 1040, 1001, 1011, 1021, 1031, 1041), (1002,), (), (1012,), (1050, 1060, 1022, 1003), (1013, 1032, 1023), (),
    (1051, 1052, 1061, 1062, 1004), (1042,), (), (), (1070, 1080, 1014), (), (1033,), (), (1024, 1053), (1043,), (1005, 1034),
    (1071, 1072, 1081, 1082, 1015, 1025), (1090,), (1100, 1063, 1044, 1091, 1054, 1101, 1035, 1026, 1064, 1055, 1045, 1036),
    (200, 1065),
    (1092, 1056, 201, 1046, 1102, 1073, 1066, 1027, 1083, 202, 1093, 1037, 1057, 1103, 1067, 1084, 1047, 1058, 1074, 1094, 203, 1068, 1059, 1104, 1085, 1075, 204, 1095, 1105, 1069, 1076, 1086, 205, 1087, 1106, 1077, 1088, 1078, 1107, 1089, 1079),
)


class Remote:
    def __init__(self, *args):
        self.args = args

    def made(self):
        src, dst, send, recv, to = self.args
        return pltpu.make_async_remote_copy(
            src_ref=src, dst_ref=dst, send_sem=send, recv_sem=recv, device_id=to, device_id_type=MESH)

    def start(self):
        self.made().start()

    def wait(self):
        self.made().wait()

    def wait_send(self):
        self.made().wait_send()

    def wait_recv(self):
        self.made().wait_recv()


def mm(a, b, d=NN):
    return lax.dot_general(a, b, d, preferred_element_type=F32)


def inverse_of(h):
    return lax.rsqrt(jnp.mean(h * h, axis=-1, keepdims=True) + EPSILON)


def norm_back(h, inv, g, r):
    s = r * g
    gain = jnp.sum(r * h * inv, axis=0, keepdims=True)
    return inv * s - h * (inv * inv * inv) * jnp.mean(s * h, axis=-1, keepdims=True), gain


def rows_of(start, size):
    return pl.ds(pl.multiple_of(start, 16), size)


def add_into(dst, parts, into=None):
    rows = dst.shape[0]
    into = dst if into is None else into
    step = next(n for n in (64, 48, 32, 16) if rows % n == 0)

    def block(i, _):
        at = rows_of(i * step, step)
        total = dst[at, :].astype(F32)
        for part in parts:
            total = total + part[at, :].astype(F32)
        into[at, :] = total.astype(BF)
        return 0

    lax.fori_loop(0, rows // step, block, 0)


def bucket_of(length=256):
    exact = BUCKETS // 2
    n = np.arange(length)
    far = exact + np.floor(np.log(np.maximum(n, 1) / exact) / math.log(MAX_DISTANCE / exact) * (BUCKETS - exact)).astype(np.int32)
    return np.where(n < exact, n, np.minimum(far, BUCKETS - 1)).astype(np.int32)


def bucket_onehot():
    bucket = bucket_of()
    n = lax.broadcasted_iota(jnp.int32, (BUCKETS, 256), 1)
    chosen = jnp.zeros((BUCKETS, 256), jnp.int32)
    for b in range(1, BUCKETS):
        chosen = chosen + jnp.where(n >= int(np.argmax(bucket >= b)), 1, 0)
    return (chosen == lax.broadcasted_iota(jnp.int32, (BUCKETS, 256), 0)).astype(BF)


def third(size, i):
    cut = {96: (32, 32, 32), 128: (32, 48, 48)}[size]
    return sum(cut[:i]), cut[i]


def layer_kernel(bits, r):
    dp = lax.axis_index("dp")
    t = lax.axis_index("tensor")
    c = lax.rem(t, 2)
    x = t // 2
    tc = t + 1 - 2 * c
    tx = t + 2 - 4 * x
    td = tc + 2 - 4 * x
    bit = [lax.rem(dp // (1 << b), 2) for b in range(bits)]
    pb = [dp + (1 << b) - (2 << b) * bit[b] for b in range(bits)]
    y, z1, z2 = bit[0], bit[1], bit[2]
    quad, quad_y, quad_z = y + 2 * z1, (1 - y) + 2 * z1, y + 2 * (1 - z1)
    quad_d = 3 - quad
    weights = (r.own, r.cross, r.feed)
    slot_of = lambda a, shard: shard if a == 1 else lax.rem(shard, 2)
    mine, other = rows_of(256 * x, 256), rows_of(256 - 256 * x, 256)

    def fwd_shard(s):
        a, b = lax.rem(s, 2), s // 2
        return 2 * (x + b * (1 - 2 * x)) + c + a * (1 - 2 * c)

    def bwd_shard(s):
        a, b = 1 - s // 2, 1 - lax.rem(s, 2)
        return 2 * (x + b * (1 - 2 * x)) + c + a * (1 - 2 * c)

    def item_shard(s):
        a, b = lax.rem(s, 2), s // 2
        return x + b * (1 - 2 * x), c + a * (1 - 2 * c)

    loads = []

    def load(src, dst):
        loads.append(pltpu.make_async_copy(src, dst, r.lsem.at[len(loads)]))
        loads[-1].start()
        return loads[-1]

    slot = lambda v, k, i: v.at[k, pl.ds(192 * i, 192), :]
    token_load = load(r.tok_in, r.tok)
    self_loads = [load(src, slot(r.own, c, i)) for i, src in enumerate((r.sq, r.sk, r.sv, r.so))]
    cross_loads = [load(src, slot(r.cross, t, i)) for i, src in enumerate((r.ck, r.cv, r.cq, r.co))]
    memory_load = load(r.mem_in, r.mem)
    feed_loads = [load(src, r.feed.at[c, pl.ds(768 * i, 768), :]) for i, src in enumerate((r.hin, r.hout))]
    cotangent_load = load(r.cot_in, r.cot.at[mine, :])

    barrier = pltpu.get_barrier_semaphore()
    partners = [(dp, tc), (dp, tx)] + [(p, t) for p in pb]
    for p in partners:
        pl.semaphore_signal(barrier, inc=1, device_id=p, device_id_type=MESH)

    g_self, g_cross, g_hid = (g[...].astype(F32).reshape(1, 768) for g in (r.gain1, r.gain2, r.gain3))
    ji = lax.broadcasted_iota(jnp.int32, (256, 256), 0)
    ii = lax.broadcasted_iota(jnp.int32, (256, 256), 1)
    r.btab[c, 0:3, :] = mm(r.tab[...], bucket_onehot())
    r.tagv[...] = jnp.broadcast_to((r.tags[...] == 1).astype(F32), (128, 256)).T
    tagged = lambda: jnp.concatenate([r.tagv[...]] * 6, axis=1) > 0.5
    token_load.wait()
    x0 = r.tok[...].astype(F32) + jnp.where(tagged(), r.emb[1:2, :].astype(F32), r.emb[0:1, :].astype(F32))
    r.s0[...] = x0
    r.n1[mine, :] = (x0 * inverse_of(x0) * g_self).astype(BF)
    pl.semaphore_wait(barrier, len(partners))

    def gather_copy(u, j):
        row, size = UNITS[u]
        v, q = r.cross, size // 4
        sems = (r.gsend.at[u, j], r.grecv.at[u, j])
        at = lambda shard, quarter, first=0, n=q: v.at[shard, rows_of(row + quarter * q + first, n), :]
        core, over_x, over_y, over_z = (dp, tc), (dp, tx), (pb[0], t), (pb[1], t)
        if j == 0:
            ref, to = v.at[t, pl.ds(row, size), :], core
        elif j == 1:
            ref, to = at(t, quad), over_x
        elif j == 2:
            ref, to = at(t, quad_d, *third(q, 0)), over_x
        elif j == 3:
            ref, to = at(tx, quad), over_y
        elif j == 4:
            ref, to = at(tx, quad), over_z
        elif j == 5:
            ref, to = at(tx, quad), core
        elif j == 6:
            ref, to = at(tx, quad_y, *third(q, 2)), over_z
        elif j == 7:
            ref, to = at(tx, quad_y), core
        elif j == 8:
            ref, to = at(tx, quad_z, *third(q, 1)), over_y
        elif j == 9:
            ref, to = at(tx, quad_z), core
        else:
            ref, to = at(tx, quad_d), core
        return Remote(ref, ref, *sems, to)

    GATHER = {0: ((), (1, 2, 0)), 1: ((1,), (3, 4, 5)), 2: ((3,), (6, 7)), 3: ((4,), (8, 9)), 4: ((2, 8, 6), (10,)),
              5: ((0,), ()), 6: ((5, 7, 9, 10), ())}

    def gather_step(u, step):
        arrived, onward = GATHER[step]
        for j in arrived:
            gather_copy(u, j).wait_recv()
        for j in onward:
            gather_copy(u, j).start()

    def gather_sent(us, js):
        for u in us:
            for j in js:
                gather_copy(u, j).wait_send()

    def view(n, shard, first=0, size=None):
        a, row, rows, _ = CHUNKS[n]
        return weights[a].at[slot_of(a, shard), rows_of(row + first, rows if size is None else size), :]

    def place(n, halves):
        first, size = 0, CHUNKS[n][2]
        for b in halves:
            size = size // 2
            first = first + b * size
        return first, size

    def result(n, halves):
        first, size = place(n, halves)
        return r.result[n].at[rows_of(first, size), :]

    flips = ((0, 1), (1, 0), (1, 1))
    turn = lambda b, f: b + f * (1 - 2 * b)
    along_z = [dp + f1 * (2 - 4 * z1) + f2 * (4 - 8 * z2) for f1, f2 in flips]

    def plan_of(n):
        order, buffers = CHUNKS[n][3], iter(r.parts[n])
        halves, shards, stages, gathers, count = [], [tx, t] if "x" in order else [t], [], [], iter(range(99))

        def copy(src, dst, to):
            j = next(count)
            return Remote(src, dst, r.rsend.at[n, j], r.rrecv.at[n, j], to)

        def piece(shard, at):
            return view(n, shard, *place(n, at))

        for d in order:
            buf = next(buffers)
            if d == "x":
                stages.append(([copy(piece(tx, halves), buf.at[0], (dp, tx))], [(piece(t, halves), [buf.at[0]])]))
                shards = [t]
                continue
            if d == "q":
                mine, others = [z1, z2], [([turn(z1, f1), turn(z2, f2)], p) for (f1, f2), p in zip(flips, along_z)]
            else:
                b = "yzw".index(d)
                mine, others = [bit[b]], [([1 - bit[b]], pb[b])]
            m = len(others)
            stages.append((
                [copy(piece(k, halves + o), buf.at[m * i + j], (p, t)) for i, k in enumerate(shards) for j, (o, p) in enumerate(others)],
                [(piece(k, halves + mine), [buf.at[m * i + j] for j in range(m)]) for i, k in enumerate(shards)]))
            halves = halves + mine
            gathers.append((list(halves), [p for _, p in others]))
        back = [[copy(result(n, at), result(n, at), (p, t)) for p in ps] for at, ps in reversed(gathers)]
        more = [(copy(piece(t, halves), r.more[n].at[b - 3], (pb[b], t)), r.more[n].at[b - 3]) for b in range(3, bits)]
        far = [(td, tx)] if "x" in order else []
        core = [(copy(view(n, a), r.first[n].at[i], (dp, tc)), view(n, b), r.first[n].at[i]) for i, (a, b) in enumerate(far + [(tc, t)])]
        return SimpleNamespace(core=core, stages=stages, back=back, more=more, mine=piece(t, halves), result=result(n, halves))

    plans = [plan_of(n) for n in range(len(CHUNKS))]

    def out_copy(n):
        a, row, rows, _ = CHUNKS[n]
        return pltpu.make_async_copy(r.result[n], (r.own_out, r.cross_out, r.feed_out)[a].at[pl.ds(row, rows), :], r.osem.at[n])

    def start(copies):
        for d in copies:
            d.start()

    def reduce_step(n, j):
        p = plans[n]
        m = len(p.core)
        if j == 0:
            start([d for d, _, _ in p.core])
        elif j <= m:
            copy, target, part = p.core[j - 1]
            copy.wait_recv()
            add_into(target, [part])
            if j == (1 if CHUNKS[n][3][0] == "x" else m):
                start(p.stages[0][0])
        elif j - m <= len(p.stages):
            copies, sums = p.stages[j - m - 1]
            for d in copies:
                d.wait_recv()
            last = j - m == len(p.stages)
            for target, parts in sums:
                add_into(target, parts, p.result if last and not p.more else None)
            if not last:
                start(p.stages[j - m][0])
                return
            for i, (copy, part) in enumerate(p.more):
                copy.start()
                copy.wait()
                add_into(p.mine, [part], p.result if i + 1 == len(p.more) else None)
            start(p.back[0])
        else:
            i = j - m - 1 - len(p.stages)
            for d in p.back[i]:
                d.wait_recv()
            if i + 1 < len(p.back):
                start(p.back[i + 1])
            else:
                out_copy(n).start()

    to = [(dp, tc), (dp, tx)] + [(p, t) for p in pb]

    def small_step(j):
        if j:
            Remote(r.sm, r.smb.at[j - 1], r.ssend.at[j - 1], r.srecv.at[j - 1], to[j - 1]).wait()
            r.sm[...] = r.sm[...] + r.smb[j - 1]
        if j < len(to):
            Remote(r.sm, r.smb.at[j], r.ssend.at[j], r.srecv.at[j], to[j]).start()

    places = iter(SCHEDULE)

    def run(todo):
        for e in todo:
            if e >= 1000:
                reduce_step((e - 1000) // 10, e % 10)
            elif e >= 200:
                small_step(e - 200)
            else:
                gather_step(e // 10, e % 10)

    def here():
        run(next(places))

    def take(count):
        return [next(places) for _ in range(count)]

    def hooks(s, todos, extra=None):
        for k, todo in enumerate(todos):
            more = (extra or {}).get(k)
            if todo or more:
                @pl.when(s == k)
                def _():
                    run(todo)
                    if more:
                        more()

    def over_x(j, src, dst):
        return Remote(src, dst, r.xsend.at[j], r.xrecv.at[j], (dp, tx))

    def to_core(j, src, dst):
        return Remote(src, dst, r.csend.at[j], r.crecv.at[j], (dp, tc))

    trade = [over_x(j, v.at[mine, :], v.at[mine, :]) for j, v in enumerate((r.n1, r.cot, r.n3, r.rows1))]
    trade_n1, trade_cot, trade_n3, trade_rows = trade
    give = [over_x(4 + j, r.out.at[j], r.arrived.at[j]) for j in range(4)]
    give_s1, give_lo, give_gn, give_gn1 = give
    core_own, core_feed, core_tab = (to_core(j, v.at[c], v.at[c]) for j, v in enumerate((r.own, r.feed, r.btab)))
    trade_n1.start()
    for d in self_loads:
        d.wait()
    core_own.start()
    core_tab.start()
    for d in cross_loads:
        d.wait()
    gather_step(0, 0)
    gather_step(1, 0)
    for d in feed_loads:
        d.wait()
    core_feed.start()

    lane576 = lax.broadcasted_iota(jnp.int32, (1, 576), 1)

    def bias_of(f, i):
        return pltpu.roll(jnp.broadcast_to(r.btab[f, i:i + 1, :], (256, 256)), 0, 1, stride=1, stride_axis=0)

    def allowed(e):
        return (ji <= ii) & (ji < r.lengths[2 * e + c])

    def columns(e):
        return pl.ds(pl.multiple_of(256 * e, 256), 256)

    def project_memory(shard):
        w = r.cross.at[shard, pl.ds(0, 384), :]

        def block(i, _):
            at = rows_of(i * 256, 256)
            r.kv[shard, at, :] = mm(r.mem[at, :], w[...], NT).astype(BF)
            return 0
        lax.fori_loop(0, 4, block, 0)
        for i in range(4):
            r.kvT[shard, :, 256 * i:256 * i + 256] = mm(w[...], r.mem[256 * i:256 * i + 256, :], NT).astype(BF)

    def near_self():
        core_own.wait_recv()
        core_tab.wait_recv()

    def near_memory():
        memory_load.wait()
        valid = r.mmask[pl.ds(t, 1), :]
        r.mask2[...] = jnp.broadcast_to(jnp.where(valid == 1, 0.0, MASKED).astype(F32), (128, 1024)).T
        project_memory(t)
        run(turns[3])
        gather_step(0, 5)
        project_memory(tc)
        run(turns[4])
        trade_n1.wait_recv()

    def self_forward(s, _):
        hooks(s, [turns[0], turns[1], turns[2], turns[5]], {1: near_self, 2: near_memory})
        e, f = item_shard(s)
        k = 2 * e + f
        rows = r.n1.at[rows_of(256 * e, 256), :]
        a = mm(rows[...], r.own[f, 0:576, :], NT)
        r.qkv[k] = jnp.where(lane576 < 192, a * 0.125, a).astype(BF)
        r.kvT1[k] = mm(r.own[f, 192:576, :], rows[...], NT).astype(BF)
        for i in range(3):
            q, kk = r.qkv[k, :, 64 * i:64 * i + 64], r.qkv[k, :, 192 + 64 * i:256 + 64 * i]
            scores = jnp.where(allowed(e), mm(kk, q, NT) + bias_of(f, i), MASKED)
            most = jnp.max(scores, axis=0, keepdims=True)
            p = jnp.exp(scores - most)
            total = jnp.sum(p, axis=0, keepdims=True)
            o = mm(r.kvT1[k, 192 + 64 * i:256 + 64 * i, :], p.astype(BF))
            r.mix1[f, 64 * i:64 * i + 64, columns(e)] = (o / total).astype(BF)
            r.lse[k, i:i + 1, :] = most + jnp.log(total)
        return 0

    def self_out(e):
        return mm(r.mix1[0, :, columns(e)].T, r.own[0, 576:768, :]) + mm(r.mix1[1, :, columns(e)].T, r.own[1, 576:768, :])

    turns = take(6)
    lax.fori_loop(0, 4, self_forward, 0)
    r.out[0] = self_out(1 - x).astype(BF)
    give_s1.start()
    cotangent_load.wait()
    trade_cot.start()
    r.s1[...] = r.s0[...] + self_out(x)
    here()
    project_memory(tx)
    here()
    gather_step(0, 6)
    project_memory(td)
    here()
    give_s1.wait_recv()
    x1 = r.s1[...] + r.arrived[0].astype(F32)
    r.s1[...] = x1
    r.n2[...] = (x1 * inverse_of(x1) * g_cross).astype(BF)
    gather_step(1, 5)

    def cross_scores(shard, i, b, q):
        at = slice(256 * b, 256 * b + 256)
        return mm(r.kv[shard, at, 64 * i:64 * i + 64], q, NT) + jnp.concatenate([r.mask2[at, :]] * 2, axis=1)

    def cross_forward(s, _):
        hooks(s, turns_1, {3: lambda: gather_step(1, 6)})
        k = fwd_shard(s)
        r.q2[k] = (mm(r.n2[...], r.cross[k, 384:576, :], NT) * 0.125).astype(BF)
        for i in range(3):
            q = r.q2[k, :, 64 * i:64 * i + 64]
            ss = [cross_scores(k, i, b, q) for b in range(4)]
            most = jnp.max(jnp.maximum(jnp.maximum(ss[0], ss[1]), jnp.maximum(ss[2], ss[3])), axis=0, keepdims=True)
            total, o = 0.0, 0.0
            for b in range(4):
                p = jnp.exp(ss[b] - most)
                total = total + jnp.sum(p, axis=0, keepdims=True)
                o = o + mm(r.kvT[k, 192 + 64 * i:256 + 64 * i, 256 * b:256 * b + 256], p.astype(BF))
            r.mix2[k, 64 * i:64 * i + 64, :] = (o / total).astype(BF)
            r.lse[4 + k, i:i + 1, :] = most + jnp.log(total)
        return 0

    turns_1 = take(4)
    lax.fori_loop(0, 4, cross_forward, 0)
    here()
    x2 = r.s1[...]
    for k in range(4):
        x2 = x2 + mm(r.mix2[k].T, r.cross[k, 576:768, :])
    r.s2[...] = x2
    r.n3[mine, :] = (x2 * inverse_of(x2) * g_hid).astype(BF)
    trade_n3.start()
    r.sums[mine, :] = x2
    r.sums[other, :] = jnp.zeros_like(x2)
    r.grads[...] = jnp.zeros_like(r.grads)
    core_feed.wait_recv()

    def far_rows():
        trade_cot.wait_recv()
        trade_n3.wait_recv()

    def feed(s, _):
        hooks(s, [turns_2[0], (), turns_2[1]], {2: far_rows})
        e, f = item_shard(s)
        at = rows_of(256 * e, 256)
        rows, cot = r.n3.at[at, :], r.cot.at[at, :]
        for i in range(3):
            cs = slice(256 * i, 256 * i + 256)
            v = mm(rows[...], r.feed[f, 0:768, cs])
            ga = mm(cot[...], r.feed[f, 768 + 256 * i:1024 + 256 * i, :], NT)
            phi = 0.5 * (1.0 + lax.erf(v * np.float32(1 / math.sqrt(2))))
            act = (v * phi).astype(BF)
            slope = phi + v * (jnp.exp(-0.5 * v * v) * np.float32(1 / math.sqrt(2 * math.pi)))
            r.act[:, cs] = act
            r.actT[f, cs, columns(e)] = act.T
            r.gb[f, at, cs] = (slope * ga).astype(BF)
        r.sums[at, :] += mm(r.act[...], r.feed[f, 768:1536, :])
        r.grads[at, :] += mm(r.gb[f, at, :], r.feed[f, 0:768, :], NT)
        return 0

    turns_2 = take(2)
    lax.fori_loop(0, 4, feed, 0)
    r.out[2] = r.grads[other, :].astype(BF)
    give_gn.start()
    r.out[1] = r.sums[other, :].astype(BF)
    give_lo.start()
    here()
    core_feed.wait_send()

    def feed_weights(f, _):
        def block(i, _):
            at = rows_of(256 * i, 256)
            r.feed[f, at, :] = mm(r.n3[:, pl.ds(pl.multiple_of(256 * i, 256), 256)].T, r.gb[f]).astype(BF)
            return 0
        lax.fori_loop(0, 3, block, 0)
        return 0

    lax.fori_loop(0, 2, feed_weights, 0)
    here()

    def feed_out_weights(f, _):
        def block(i, _):
            at = rows_of(256 * i, 256)
            r.feed[f, rows_of(768 + 256 * i, 256), :] = mm(r.actT[f, at, :], r.cot[...]).astype(BF)
            return 0
        lax.fori_loop(0, 3, block, 0)
        return 0

    lax.fori_loop(0, 2, feed_out_weights, 0)
    here()
    give_gn.wait_recv()
    d, gain = norm_back(x2, inverse_of(x2), g_hid, r.grads[mine, :] + r.arrived[2].astype(F32))

    def put_small(row, value):
        for i in range(3):
            at = 3 * row + i
            r.sm[at // 8, at % 8:at % 8 + 1, :] = value[:, 256 * i:256 * i + 256]

    r.sm[...] = jnp.zeros_like(r.sm)
    put_small(4, gain)
    r.gst[...] = r.cot[mine, :].astype(F32) + d
    gather_sent(range(2), range(11))
    here()
    r.rows2[...] = r.gst[...].astype(BF)
    r.acc[...] = jnp.zeros_like(x2)

    def cross_backward(s, _):
        hooks(s, turns_3)
        k = bwd_shard(s)
        rw = r.rows2[...]
        w = r.cross[k, 576:768, :]
        G = mm(rw, w, NT).astype(BF)
        GT = mm(w, rw, NT).astype(BF)
        r.cross[k, 576:768, :] = mm(r.mix2[k], rw).astype(BF)
        dqs, dks, dvs = [], [], []
        for i in range(3):
            q = r.q2[k, :, 64 * i:64 * i + 64]
            gi, gT = G[:, 64 * i:64 * i + 64], GT[64 * i:64 * i + 64, :]
            inner = jnp.sum(r.mix2[k, 64 * i:64 * i + 64, :].astype(F32) * gT.astype(F32), axis=0, keepdims=True)
            ls = r.lse[4 + k, i:i + 1, :]
            dq, dk, dv = 0.0, [], []
            for b in range(4):
                at = slice(256 * b, 256 * b + 256)
                p = jnp.exp(cross_scores(k, i, b, q) - ls)
                dp_ = mm(r.kv[k, at, 192 + 64 * i:256 + 64 * i], gi, NT)
                gs = (p * (dp_ - inner)).astype(BF)
                dq = dq + mm(r.kvT[k, 64 * i:64 * i + 64, at], gs)
                dk.append(mm(gs, q).astype(BF))
                dv.append(mm(p.astype(BF), gi).astype(BF))
            dqs.append((dq * 0.125).astype(BF))
            dks.append(dk)
            dvs.append(dv)
        for b in range(4):
            r.kv[k, 256 * b:256 * b + 256, :] = jnp.concatenate([v[b] for v in dks + dvs], axis=1)
        r.kvT[k] = r.kv[k].T
        dqT = jnp.concatenate(dqs, axis=0)
        r.acc[...] += mm(dqT.T, r.cross[k, 384:576, :])
        r.cross[k, 384:576, :] = mm(dqT, r.n2[...]).astype(BF)
        return 0

    turns_3 = take(4)
    lax.fori_loop(0, 4, cross_backward, 0)
    here()
    x1 = r.s1[...]
    d, gain = norm_back(x1, inverse_of(x1), g_cross, r.acc[...])
    put_small(3, gain)
    x1 = r.gst[...] + d
    r.gst[...] = x1
    r.rows1[mine, :] = x1.astype(BF)
    trade_rows.start()
    here()
    give_lo.wait_recv()
    r.lov[...] = (r.sums[mine, :] + r.arrived[1].astype(F32)).astype(BF)
    stores = [pltpu.make_async_copy(a, b, r.esem.at[i]) for i, (a, b) in enumerate(((r.lov, r.lo), (r.gmv, r.gmem), (r.gtv, r.gtok)))]
    stores[0].start()

    def memory_grad(i, _):
        at = rows_of(i * 256, 256)
        total = 0.0
        for k in range(4):
            total = total + mm(r.kv[k, at, :], r.cross[k, 0:384, :])
        r.gmv[at, :] = total.astype(BF)
        return 0

    lax.fori_loop(0, 4, memory_grad, 0)
    stores[1].start()
    here()

    def memory_weights(s, _):
        hooks(s, turns_4)
        k = bwd_shard(s)

        def block(i, _):
            at = rows_of(i * 192, 192)
            r.cross[k, at, :] = mm(r.kvT[k, at, :], r.mem[...]).astype(BF)
            return 0
        lax.fori_loop(0, 2, block, 0)
        return 0

    turns_4 = take(4)
    lax.fori_loop(0, 4, memory_weights, 0)
    here()
    r.grads[...] = jnp.zeros_like(r.grads)

    def self_backward(s, _):
        hooks(s, turns_5, {2: trade_rows.wait_recv})
        e, f = item_shard(s)
        k = 2 * e + f
        here_rows = rows_of(256 * e, 256)
        rw = r.rows1[here_rows, :]
        w = r.own[f, 576:768, :]
        G = mm(rw, w, NT).astype(BF)
        GT = mm(w, rw, NT).astype(BF)
        flip = (ji + ii == 255).astype(BF)
        dqs, dks, dvs = [], [], []
        for i in range(3):
            q, kk = r.qkv[k, :, 64 * i:64 * i + 64], r.qkv[k, :, 192 + 64 * i:256 + 64 * i]
            gi, gT = G[:, 64 * i:64 * i + 64], GT[64 * i:64 * i + 64, :]
            inner = jnp.sum(r.mix1[f, 64 * i:64 * i + 64, columns(e)].astype(F32) * gT.astype(F32), axis=0, keepdims=True)
            scores = jnp.where(allowed(e), mm(kk, q, NT) + bias_of(f, i), MASKED)
            p = jnp.exp(scores - r.lse[k, i:i + 1, :])
            dp_ = mm(r.qkv[k, :, 384 + 64 * i:448 + 64 * i], gi, NT)
            gs = (p * (dp_ - inner)).astype(BF)
            dvs.append(mm(p.astype(BF), gi).astype(BF))
            dks.append(mm(gs, q).astype(BF))
            dqs.append((mm(r.kvT1[k, 64 * i:64 * i + 64, :], gs) * 0.125).astype(BF))
            shifted = pltpu.roll(mm(flip, gs), 1, 1, stride=1, stride_axis=0)
            r.sm[2 + 2 * x + f, i:i + 1, :] += jnp.sum(shifted, axis=0, keepdims=True)
        dqT = jnp.concatenate(dqs, axis=0)
        dkv = jnp.concatenate(dks + dvs, axis=1)
        r.gT[f, 0:192, columns(e)] = dqT
        r.gT[f, 192:576, columns(e)] = dkv.T
        r.grads[here_rows, :] += mm(dqT.T, r.own[f, 0:192, :]) + mm(dkv, r.own[f, 192:576, :])
        return 0

    turns_5 = take(4)
    lax.fori_loop(0, 4, self_backward, 0)
    r.out[3] = r.grads[other, :].astype(BF)
    give_gn1.start()
    core_own.wait_send()
    here()
    for f in range(2):
        r.own[f, 0:384, :] = mm(r.gT[f, 0:384, :], r.n1[...]).astype(BF)
    here()
    for f in range(2):
        r.own[f, 384:576, :] = mm(r.gT[f, 384:576, :], r.n1[...]).astype(BF)
        r.own[f, 576:768, :] = mm(r.mix1[f], r.rows1[...]).astype(BF)
    here()
    give_gn1.wait_recv()
    x0 = r.s0[...]
    d, gain = norm_back(x0, inverse_of(x0), g_self, r.grads[mine, :] + r.arrived[3].astype(F32))
    put_small(2, gain)
    g0 = r.gst[...] + d
    r.gtv[...] = g0.astype(BF)
    stores[2].start()
    put_small(0, jnp.sum(jnp.where(tagged(), 0.0, g0), axis=0, keepdims=True))
    put_small(1, jnp.sum(jnp.where(tagged(), g0, 0.0), axis=0, keepdims=True))
    here()
    here()
    for j in range(6, len(to) + 1):
        small_step(j)
    r.smo[...] = r.sm[0:2]
    r.dgo[...] = r.sm[2 + t]
    for n, p in enumerate(plans):
        for d in [d for d, _, _ in p.core] + sum([copies for copies, _ in p.stages], []) + sum(p.back, []):
            d.wait_send()
        out_copy(n).wait()
    for d in stores:
        d.wait()
    for d in trade + give + [core_tab]:
        d.wait_send()


def layer(bits, ins):
    S = jax.ShapeDtypeStruct
    V, A, M = (pl.BlockSpec(memory_space=s) for s in (pltpu.VMEM, pl.ANY, pltpu.SMEM))
    vm = pltpu.VMEM
    inputs = dict(tok_in=A, mem_in=A, cot_in=A, lengths=M, mmask=V, tags=V, emb=V, gain1=V, gain2=V, gain3=V, tab=V,
                  sq=A, sk=A, sv=A, so=A, cq=A, ck=A, cv=A, co=A, hin=A, hout=A)
    wide, square = (256, 768), (768, 768)
    out = dict(lo=S(wide, BF), gtok=S(wide, BF), gmem=S((1024, 768), BF), smo=S((2, 8, 256), F32), dgo=S((8, 256), F32),
               own_out=S(square, BF), cross_out=S(square, BF), feed_out=S((1536, 768), BF))
    out_specs = [A, A, A, V, V, A, A, A]
    sizes = [n for _, _, n, _ in CHUNKS]

    def parts_of(n, order):
        shards, buffers = 2 if "x" in order else 1, []
        for d in order:
            if d == "x":
                shards = 1
                buffers.append(vm((1, n, 768), BF))
            else:
                n = n // 4 if d == "q" else n // 2
                buffers.append(vm((shards * (3 if d == "q" else 1), n, 768), BF))
        return buffers

    both = (512, 768)
    scratch = dict(
        own=vm((2, 768, 768), BF), cross=vm((4, 768, 768), BF), feed=vm((2, 1536, 768), BF),
        tok=vm(wide, BF), cot=vm(both, BF), mem=vm((1024, 768), BF), n1=vm(both, BF), n3=vm(both, BF), rows1=vm(both, BF),
        out=vm((4, 256, 768), BF), arrived=vm((4, 256, 768), BF),
        s0=vm(wide, F32), s1=vm(wide, F32), s2=vm(wide, F32), gst=vm(wide, F32), acc=vm(wide, F32), sums=vm(both, F32), grads=vm(both, F32),
        n2=vm(wide, BF), rows2=vm(wide, BF), act=vm(wide, BF), actT=vm((2, 768, 512), BF), gb=vm((2, 512, 768), BF),
        qkv=vm((4, 256, 576), BF), kvT1=vm((4, 384, 256), BF), q2=vm((4, 256, 192), BF), gT=vm((2, 576, 512), BF),
        kv=vm((4, 1024, 384), BF), kvT=vm((4, 384, 1024), BF), mix1=vm((2, 192, 512), BF), mix2=vm((4, 192, 256), BF),
        lse=vm((8, 8, 256), F32), mask2=vm((1024, 128), F32), tagv=vm((256, 128), F32), btab=vm((2, 8, 256), F32),
        sm=vm((6, 8, 256), F32), smb=vm((2 + bits, 6, 8, 256), F32), gmv=vm((1024, 768), BF), lov=vm(wide, BF), gtv=vm(wide, BF),
    )
    first = [vm((2 if "x" in order else 1, n, 768), BF) for _, _, n, order in CHUNKS]
    parts = [parts_of(n, order) for _, _, n, order in CHUNKS]
    results = [vm((n, 768), BF) for n in sizes]
    more = [vm((bits - 3, n // 8, 768), BF) for n in sizes] if bits > 3 else []
    dma = pltpu.SemaphoreType.DMA
    sems = dict(gsend=dma((2, 11)), grecv=dma((2, 11)), xsend=dma((8,)), xrecv=dma((8,)), csend=dma((3,)), crecv=dma((3,)), rsend=dma((len(CHUNKS), 16 + bits)), rrecv=dma((len(CHUNKS), 16 + bits)), lsem=dma((13,)), osem=dma((len(CHUNKS),)),
                esem=dma((3,)), ssend=dma((2 + bits,)), srecv=dma((2 + bits,)))
    names = list(inputs) + list(out) + list(scratch) + list(sems)

    def kernel(*refs):
        r = SimpleNamespace(**dict(zip(names, refs)))
        rest = iter(refs[len(names):])
        r.parts = [[next(rest) for _ in p] for p in parts]
        r.result = [next(rest) for _ in results]
        r.more = [next(rest) for _ in more]
        r.first = [next(rest) for _ in first]
        layer_kernel(bits, r)

    return pl.pallas_call(
        kernel, out_shape=list(out.values()), in_specs=list(inputs.values()), out_specs=out_specs,
        scratch_shapes=list(scratch.values()) + list(sems.values()) + sum(parts, []) + results + more + first,
        compiler_params=pltpu.CompilerParams(collective_id=0, has_side_effects=True, vmem_limit_bytes=VMEM_LIMIT),
    )(*ins)


def finish_kernel(lo, gtok, gmem, smo, dgo, own, cross, feed,
                  o_lo, o_gtok, o_gmem, o_emb, o_g1, o_g2, o_g3, o_sq, o_sk, o_sv, o_so, o_pb, o_cq, o_ck, o_cv, o_co, o_hin, o_hout):
    o_lo[...] = lo[...]
    o_gtok[...] = gtok[...]
    o_gmem[...] = gmem[...]
    for i, o in enumerate((o_sq, o_sk, o_sv, o_so)):
        o[...] = own[192 * i:192 * i + 192, :].astype(F32)
    for i, o in enumerate((o_ck, o_cv, o_cq, o_co)):
        o[...] = cross[192 * i:192 * i + 192, :].astype(F32)
    o_hin[...] = feed[0:768, :].astype(F32)
    o_hout[...] = feed[768:1536, :].astype(F32)

    @pl.when(pl.program_id(0) == 0)
    def _():
        def small(row):
            return jnp.concatenate([smo[(3 * row + i) // 8, (3 * row + i) % 8:(3 * row + i) % 8 + 1, :] for i in range(3)], axis=1)
        o_emb[0:1, :] = small(0)
        o_emb[1:2, :] = small(1)
        o_g1[...] = small(2).reshape(768)
        o_g2[...] = small(3).reshape(768)
        o_g3[...] = small(4).reshape(768)
        total = lax.dot_general(dgo[...], bucket_onehot().astype(F32), NT, precision=lax.Precision.HIGHEST, preferred_element_type=F32)
        o_pb[...] = total[0:3, :]


def finish(args):
    S = jax.ShapeDtypeStruct
    n = 3
    cut = lambda rows: pl.BlockSpec((rows, 768 // n), lambda i: (0, i))
    full = lambda *s: pl.BlockSpec(s, lambda i: (0,) * len(s))
    flat, square = S((192, 768), F32), S((768, 768), F32)
    shapes = [S((256, 768), BF), S((256, 768), BF), S((1024, 768), BF), S((2, 768), F32)] + [S((768,), F32)] * 3
    shapes += [flat] * 4 + [S((3, 32), F32)] + [flat] * 4 + [square, square]
    ends = [cut(256), cut(256), cut(1024)]
    in_specs = ends + [full(2, 8, 256), full(8, 256), cut(768), cut(768), cut(1536)]
    out_specs = ends + [full(2, 768)] + [full(768)] * 3 + [cut(192)] * 4 + [full(3, 32)] + [cut(192)] * 4
    out_specs += [cut(768), cut(768)]
    return pl.pallas_call(finish_kernel, grid=(n,), out_shape=shapes, in_specs=in_specs, out_specs=out_specs,
                          compiler_params=pltpu.CompilerParams(vmem_limit_bytes=VMEM_LIMIT))(*args)


def per_device(bits, tokens, memory, cotangent, lengths, memory_mask, token_tags, embedding, gain_self, gain_cross, gain_hidden,
               self_query, self_key, self_value, self_output, position_bias, cross_query, cross_key, cross_value,
               cross_output, hidden_in, hidden_out):
    parts = layer(bits, (
        tokens[0], memory[0], cotangent[0], lengths, memory_mask, token_tags, embedding, gain_self, gain_cross, gain_hidden, position_bias.T,
        self_query.T, self_key.T, self_value.T, self_output, cross_query.T, cross_key.T, cross_value.T, cross_output, hidden_in, hidden_out))
    lo, gtok, gmem, g_emb, g1, g2, g3, sq, sk, sv, so, pb, cq, ck, cv, co, hin, hout = finish(parts)
    return (lo[None], gtok[None], gmem[None], g_emb, g1, g2, g3, sq.T, sk.T, sv.T, so, pb.T, cq.T, ck.T, cv.T, co, hin, hout)


def solution(mesh):
    bits = int(math.log2(mesh.shape["dp"]))
    item = P(("dp", "tensor"), None, None)
    col, row, rep = P(None, "tensor"), P("tensor", None), P()
    in_specs = (item, item, item, P("dp"), P("dp", None), P(("dp", "tensor"), None), rep, rep, rep, rep,
                col, col, col, row, col, col, col, col, row, col, row)
    out_specs = (item, item, item, rep, rep, rep, rep, col, col, col, row, col, col, col, col, row, col, row)
    return jax.shard_map(lambda *a: per_device(bits, *a), mesh=mesh, in_specs=in_specs, out_specs=out_specs, check_vma=False)
```

```python
import math
from types import SimpleNamespace

import jax
import jax.numpy as jnp
import numpy as np
from jax import lax
from jax.experimental import pallas as pl
from jax.experimental.pallas import tpu as pltpu
from jax.sharding import PartitionSpec as P

EPSILON = 1e-6
MASKED = -1e9
BUCKETS = 32
MAX_DISTANCE = 128
VMEM_LIMIT = 64 * 1024 * 1024 - 64 * 1024
F32 = jnp.float32
BF = jnp.bfloat16
NN = (((1,), (0,)), ((), ()))
NT = (((1,), (1,)), ((), ()))
MESH = pl.DeviceIdType.MESH

UNITS = ((0, 384), (384, 192), (576, 192))
CHUNKS = (
    (2, 0, 256, 'yzw'),
    (2, 256, 256, 'yzw'),
    (2, 512, 256, 'yq'),
    (2, 768, 256, 'zyw'),
    (2, 1024, 512, 'yzw'),
    (1, 384, 128, 'yxzw'),
    (1, 512, 256, 'yxzw'),
    (1, 0, 128, 'yxzw'),
    (1, 128, 256, 'yxzw'),
    (0, 0, 384, 'yzw'),
    (0, 384, 128, 'yq'),
    (0, 512, 256, 'zwy'),
)
SCHEDULE = (
    (), (), (), (1,), (), (2, 3), (4, 11), (), (12, 13), (14,), (21,), (), (22, 23), (24,), (), (), (), (), (1000,), (1010,),
    (1020,), (1030,), (), (1040, 1001, 1011, 1021, 1031), (1041,), (), (), (1050, 1060), (1004,), (1002,), (1012, 1032, 1003),
    (1022, 1013), (), (), (1051, 1052, 1042, 1061, 1062, 1023), (1033, 1014, 1005), (), (), (1070, 1080, 1053, 1043), (), (), (),
    (), (1054, 1024), (1063, 1034), (1071, 1072, 1081, 1082, 1015), (1090,),
    (1100, 1110, 1025, 1055, 1006, 1064, 1044, 1091, 1101, 1111, 1035, 1073, 1016, 1056, 1065), (200,),
    (1074, 1083, 201, 1112, 1045, 1007, 1075, 1084, 202, 1113, 1066, 1092, 1102, 1085, 1093, 1046, 1017, 203, 1076, 1057, 1086, 1067, 204, 1114, 1058, 1094, 1047, 1068, 1077, 1087, 1059, 205, 1103, 1078, 1115, 1069, 1088, 1095, 1079, 1104, 1036, 1089, 1096, 1105, 1116, 1037, 1097, 1117),
)


class Remote:
    def __init__(self, *args):
        self.args = args

    def made(self):
        src, dst, send, recv, to = self.args
        return pltpu.make_async_remote_copy(
            src_ref=src, dst_ref=dst, send_sem=send, recv_sem=recv, device_id=to, device_id_type=MESH)

    def start(self):
        self.made().start()

    def wait(self):
        self.made().wait()

    def wait_send(self):
        self.made().wait_send()

    def wait_recv(self):
        self.made().wait_recv()


def mm(a, b, d=NN):
    return lax.dot_general(a, b, d, preferred_element_type=F32)


def inverse_of(h):
    return lax.rsqrt(jnp.mean(h * h, axis=-1, keepdims=True) + EPSILON)


def norm_back(h, inv, g, r):
    s = r * g
    gain = jnp.sum(r * h * inv, axis=0, keepdims=True)
    return inv * s - h * (inv * inv * inv) * jnp.mean(s * h, axis=-1, keepdims=True), gain


def rows_of(start, size):
    return pl.ds(pl.multiple_of(start, 16), size)


def add_into(dst, parts, into=None):
    rows = dst.shape[0]
    into = dst if into is None else into
    step = next(n for n in (64, 48, 32, 16) if rows % n == 0)

    def block(i, _):
        at = rows_of(i * step, step)
        total = dst[at, :].astype(F32)
        for part in parts:
            total = total + part[at, :].astype(F32)
        into[at, :] = total.astype(BF)
        return 0

    lax.fori_loop(0, rows // step, block, 0)


def bucket_of(length=256):
    exact = BUCKETS // 2
    n = np.arange(length)
    far = exact + np.floor(np.log(np.maximum(n, 1) / exact) / math.log(MAX_DISTANCE / exact) * (BUCKETS - exact)).astype(np.int32)
    return np.where(n < exact, n, np.minimum(far, BUCKETS - 1)).astype(np.int32)


def bucket_onehot():
    bucket = bucket_of()
    n = lax.broadcasted_iota(jnp.int32, (BUCKETS, 256), 1)
    chosen = jnp.zeros((BUCKETS, 256), jnp.int32)
    for b in range(1, BUCKETS):
        chosen = chosen + jnp.where(n >= int(np.argmax(bucket >= b)), 1, 0)
    return (chosen == lax.broadcasted_iota(jnp.int32, (BUCKETS, 256), 0)).astype(BF)


def layer_kernel(bits, r):
    dp = lax.axis_index("dp")
    t = lax.axis_index("tensor")
    c = lax.rem(t, 2)
    x = t // 2
    tc = t + 1 - 2 * c
    tx = t + 2 - 4 * x
    td = tc + 2 - 4 * x
    bit = [lax.rem(dp // (1 << b), 2) for b in range(bits)]
    pb = [dp + (1 << b) - (2 << b) * bit[b] for b in range(bits)]
    y, z1, z2 = bit[0], bit[1], bit[2]
    quad, quad_y, quad_z = y + 2 * z1, (1 - y) + 2 * z1, y + 2 * (1 - z1)
    quad_d = 3 - quad
    weights = (r.own, r.cross, r.feed)
    slot_of = lambda a, shard: shard if a == 1 else lax.rem(shard, 2)
    mine, other = rows_of(256 * x, 256), rows_of(256 - 256 * x, 256)

    def fwd_shard(s):
        a, b = lax.rem(s, 2), s // 2
        return 2 * (x + b * (1 - 2 * x)) + c + a * (1 - 2 * c)

    def bwd_shard(s):
        a, b = 1 - s // 2, 1 - lax.rem(s, 2)
        return 2 * (x + b * (1 - 2 * x)) + c + a * (1 - 2 * c)

    def item_shard(s):
        a, b = lax.rem(s, 2), s // 2
        return x + b * (1 - 2 * x), c + a * (1 - 2 * c)

    loads = []

    def load(src, dst):
        loads.append(pltpu.make_async_copy(src, dst, r.lsem.at[len(loads)]))
        loads[-1].start()
        return loads[-1]

    slot = lambda v, k, i: v.at[k, pl.ds(192 * i, 192), :]
    token_load = load(r.tok_in, r.tok)
    small_loads = [load(a, b) for a, b in ((r.emb_in, r.emb), (r.tags_in, r.tags), (r.gain1_in, r.gain1), (r.tab_in, r.tab),
                                           (r.gain2_in, r.gain2), (r.gain3_in, r.gain3), (r.mmask_in, r.mmask))]
    key_loads = [load(src, slot(r.cross, t, i)) for i, src in enumerate((r.ck, r.cv))]
    self_loads = [load(src, slot(r.own, c, i)) for i, src in enumerate((r.sq, r.sk, r.sv, r.so))]
    query_loads = [load(src, slot(r.cross, t, 2 + i)) for i, src in enumerate((r.cq, r.co))]
    memory_load = load(r.mem_in, r.mem)
    feed_loads = [load(src, r.feed.at[c, pl.ds(768 * i, 768), :]) for i, src in enumerate((r.hin, r.hout))]
    cotangent_load = load(r.cot_in, r.cot.at[mine, :])

    barrier = pltpu.get_barrier_semaphore()
    partners = [(dp, tc), (dp, tx)] + [(p, t) for p in pb]
    for p in partners:
        pl.semaphore_signal(barrier, inc=1, device_id=p, device_id_type=MESH)

    for d in small_loads:
        d.wait()
    g_self, g_cross, g_hid = (g[...].astype(F32).reshape(1, 768) for g in (r.gain1, r.gain2, r.gain3))
    ji = lax.broadcasted_iota(jnp.int32, (256, 256), 0)
    ii = lax.broadcasted_iota(jnp.int32, (256, 256), 1)
    r.btab[c, 0:3, :] = mm(r.tab[...], bucket_onehot())
    r.tagv[...] = jnp.broadcast_to((r.tags[...] == 1).astype(F32), (128, 256)).T
    tagged = lambda: jnp.concatenate([r.tagv[...]] * 6, axis=1) > 0.5
    token_load.wait()
    x0 = r.tok[...].astype(F32) + jnp.where(tagged(), r.emb[1:2, :].astype(F32), r.emb[0:1, :].astype(F32))
    r.s0[...] = x0
    r.n1[mine, :] = (x0 * inverse_of(x0) * g_self).astype(BF)
    pl.semaphore_wait(barrier, len(partners))

    def gather_copy(u, j):
        row, size = UNITS[u]
        v, q = r.cross, size // 4
        part = 32 if q == 48 else q // 2
        sems = (r.gsend.at[u, j], r.grecv.at[u, j])
        at = lambda shard, quarter, first=0, n=q: v.at[shard, rows_of(row + quarter * q + first, n), :]
        core, over_x, over_y, over_z = (dp, tc), (dp, tx), (pb[0], t), (pb[1], t)
        if j == 0:
            ref, to = v.at[t, pl.ds(row, size), :], core
        elif j == 1:
            ref, to = at(t, quad), over_x
        elif j == 3:
            ref, to = at(tx, quad), over_y
        elif j == 4:
            ref, to = at(tx, quad), over_z
        elif j == 5:
            ref, to = at(tx, quad), core
        elif j == 6:
            ref, to = at(tx, quad_y, part, q - part), over_z
        elif j == 7:
            ref, to = at(tx, quad_y), core
        elif j == 8:
            ref, to = at(tx, quad_z, 0, part), over_y
        elif j == 9:
            ref, to = at(tx, quad_z), core
        else:
            ref, to = at(tx, quad_d), core
        return Remote(ref, ref, *sems, to)

    GATHER = {0: ((), (1, 0)), 1: ((1,), (3, 4, 5)), 2: ((3,), (6, 7)), 3: ((4,), (8, 9)), 4: ((8, 6), (10,)),
              5: ((0,), ()), 6: ((5, 7, 9, 10), ())}

    def gather_step(u, step):
        arrived, onward = GATHER[step]
        for j in arrived:
            gather_copy(u, j).wait_recv()
        for j in onward:
            gather_copy(u, j).start()

    def gather_sent(us, js):
        for u in us:
            for j in js:
                gather_copy(u, j).wait_send()

    def view(n, shard, first=0, size=None):
        a, row, rows, _ = CHUNKS[n]
        return weights[a].at[slot_of(a, shard), rows_of(row + first, rows if size is None else size), :]

    def place(n, halves):
        first, size = 0, CHUNKS[n][2]
        for b in halves:
            size = size // 2
            first = first + b * size
        return first, size

    def result(n, halves):
        first, size = place(n, halves)
        return r.result[n].at[rows_of(first, size), :]

    flips = ((0, 1), (1, 0), (1, 1))
    turn = lambda b, f: b + f * (1 - 2 * b)
    along_z = [dp + f1 * (2 - 4 * z1) + f2 * (4 - 8 * z2) for f1, f2 in flips]

    def plan_of(n):
        order, buffers = CHUNKS[n][3], iter(r.parts[n])
        halves, shards, stages, gathers, count = [], [tx, t] if "x" in order else [t], [], [], iter(range(99))

        def copy(src, dst, to):
            j = next(count)
            return Remote(src, dst, r.rsend.at[n, j], r.rrecv.at[n, j], to)

        def piece(shard, at):
            return view(n, shard, *place(n, at))

        for d in order:
            buf = next(buffers)
            if d == "x":
                stages.append(([copy(piece(tx, halves), buf.at[0], (dp, tx))], [(piece(t, halves), [buf.at[0]])]))
                shards = [t]
                continue
            if d == "q":
                mine, others = [z1, z2], [([turn(z1, f1), turn(z2, f2)], p) for (f1, f2), p in zip(flips, along_z)]
            else:
                b = "yzw".index(d)
                mine, others = [bit[b]], [([1 - bit[b]], pb[b])]
            m = len(others)
            stages.append((
                [copy(piece(k, halves + o), buf.at[m * i + j], (p, t)) for i, k in enumerate(shards) for j, (o, p) in enumerate(others)],
                [(piece(k, halves + mine), [buf.at[m * i + j] for j in range(m)]) for i, k in enumerate(shards)]))
            halves = halves + mine
            gathers.append((list(halves), [p for _, p in others]))
        back = [[copy(result(n, at), result(n, at), (p, t)) for p in ps] for at, ps in reversed(gathers)]
        more = [(copy(piece(t, halves), r.more[n].at[b - 3], (pb[b], t)), r.more[n].at[b - 3]) for b in range(3, bits)]
        far = [(td, tx)] if "x" in order else []
        core = [(copy(view(n, a), r.first[n].at[i], (dp, tc)), view(n, b), r.first[n].at[i]) for i, (a, b) in enumerate(far + [(tc, t)])]
        return SimpleNamespace(core=core, stages=stages, back=back, more=more, mine=piece(t, halves), result=result(n, halves))

    plans = [plan_of(n) for n in range(len(CHUNKS))]

    def out_copy(n):
        a, row, rows, _ = CHUNKS[n]
        return pltpu.make_async_copy(r.result[n], (r.own_out, r.cross_out, r.feed_out)[a].at[pl.ds(row, rows), :], r.osem.at[n])

    def start(copies):
        for d in copies:
            d.start()

    def reduce_step(n, j):
        p = plans[n]
        m = len(p.core)
        if j == 0:
            start([d for d, _, _ in p.core])
        elif j <= m:
            copy, target, part = p.core[j - 1]
            copy.wait_recv()
            add_into(target, [part])
            if j == (1 if CHUNKS[n][3][0] == "x" else m):
                start(p.stages[0][0])
        elif j - m <= len(p.stages):
            copies, sums = p.stages[j - m - 1]
            for d in copies:
                d.wait_recv()
            last = j - m == len(p.stages)
            for target, parts in sums:
                add_into(target, parts, p.result if last and not p.more else None)
            if not last:
                start(p.stages[j - m][0])
                return
            for i, (copy, part) in enumerate(p.more):
                copy.start()
                copy.wait()
                add_into(p.mine, [part], p.result if i + 1 == len(p.more) else None)
            start(p.back[0])
        else:
            i = j - m - 1 - len(p.stages)
            for d in p.back[i]:
                d.wait_recv()
            if i + 1 < len(p.back):
                start(p.back[i + 1])
            else:
                out_copy(n).start()

    to = [(dp, tc), (dp, tx)] + [(p, t) for p in pb]

    def small_step(j):
        if j:
            Remote(r.sm, r.smb.at[j - 1], r.ssend.at[j - 1], r.srecv.at[j - 1], to[j - 1]).wait()
            r.sm[...] = r.sm[...] + r.smb[j - 1]
        if j < len(to):
            Remote(r.sm, r.smb.at[j], r.ssend.at[j], r.srecv.at[j], to[j]).start()

    places = iter(SCHEDULE)

    def run(todo):
        for e in todo:
            if e >= 1000:
                reduce_step((e - 1000) // 10, e % 10)
            elif e >= 200:
                small_step(e - 200)
            else:
                gather_step(e // 10, e % 10)

    def here():
        run(next(places))

    def take(count):
        return [next(places) for _ in range(count)]

    def hooks(s, todos, extra=None):
        for k, todo in enumerate(todos):
            more = (extra or {}).get(k)
            if todo or more:
                @pl.when(s == k)
                def _():
                    run(todo)
                    if more:
                        more()

    def over_x(j, src, dst):
        return Remote(src, dst, r.xsend.at[j], r.xrecv.at[j], (dp, tx))

    def to_core(j, src, dst):
        return Remote(src, dst, r.csend.at[j], r.crecv.at[j], (dp, tc))

    def half(start, h):
        return rows_of(start + 128 * h, 128)

    trade_cot, trade_rows = trade = [over_x(j, v.at[mine, :], v.at[mine, :]) for j, v in enumerate((r.cot, r.rows1))]
    trade_n1, trade_n3 = ([over_x(2 + 2 * j + h, v.at[half(256 * x, h), :], v.at[half(256 * x, h), :]) for h in range(2)]
                          for j, v in enumerate((r.n1, r.n3)))
    give_lo, give_gn1 = give = [over_x(6 + j, r.out.at[i], r.arrived.at[i]) for j, i in enumerate((1, 3))]
    give_s1, give_gn = ([over_x(8 + 2 * j + h, r.out.at[i, half(0, h), :], r.arrived.at[i, half(0, h), :]) for h in range(2)]
                        for j, i in enumerate((0, 2)))
    core_own, core_feed, core_tab = (to_core(j, v.at[c], v.at[c]) for j, v in enumerate((r.own, r.feed, r.btab)))
    for d in key_loads:
        d.wait()
    gather_step(0, 0)
    start(trade_n1)
    for d in self_loads:
        d.wait()
    core_own.start()
    core_tab.start()
    for d in query_loads:
        d.wait()
    gather_step(1, 0)
    for d in feed_loads:
        d.wait()
    core_feed.start()

    def bias_of(f, i):
        return pltpu.roll(jnp.broadcast_to(r.btab[f, i:i + 1, :], (256, 256)), 0, 1, stride=1, stride_axis=0)

    def allowed(e):
        return (ji <= ii) & (ji < r.lengths[2 * e + c])

    lane = lax.broadcasted_iota(jnp.int32, (1, 128), 1)
    low, high = lane < 64, lane >= 64

    def of_keys(a):
        wide = jnp.concatenate([a, jnp.zeros((a.shape[0], 64), a.dtype)], axis=1)
        return [jnp.where(low, wide[:, 0:128], 0), jnp.where(high, wide[:, 0:128], 0), jnp.where(low, wide[:, 128:256], 0)]

    def of_values(a):
        wide = jnp.concatenate([jnp.zeros((a.shape[0], 64), a.dtype), a], axis=1)
        return [jnp.where(high, wide[:, 0:128], 0), jnp.where(low, wide[:, 128:256], 0), jnp.where(high, wide[:, 128:256], 0)]

    key_lanes = (slice(0, 128), slice(0, 128), slice(128, 256))
    value_lanes = (slice(128, 256), slice(256, 384), slice(256, 384))

    def columns(e):
        return pl.ds(pl.multiple_of(256 * e, 256), 256)

    def project_memory(shard):
        w = r.cross.at[shard, pl.ds(0, 384), :]

        def block(i, _):
            at = rows_of(i * 256, 256)
            r.kv[shard, at, :] = mm(r.mem[at, :], w[...], NT).astype(BF)
            return 0
        lax.fori_loop(0, 4, block, 0)
        for i in range(4):
            r.kvT[shard, :, 256 * i:256 * i + 256] = mm(w[...], r.mem[256 * i:256 * i + 256, :], NT).astype(BF)

    def near_self():
        core_own.wait_recv()
        core_tab.wait_recv()

    def near_memory():
        memory_load.wait()
        valid = r.mmask[pl.ds(t, 1), :]
        r.mask2[...] = jnp.broadcast_to(jnp.where(valid == 1, 0.0, MASKED).astype(F32), (128, 1024)).T
        project_memory(t)
        here()
        gather_step(0, 5)
        project_memory(tc)

    def self_forward(s, _):
        hooks(s, turns, {1: near_self})
        e, f = x, c + s * (1 - 2 * c)
        k = 2 * e + f
        rows = r.n1.at[rows_of(256 * e, 256), :]
        r.q1[k] = (mm(rows[...], r.own[f, 0:192, :], NT) * 0.125).astype(BF)
        r.kv1[k] = mm(rows[...], r.own[f, 192:576, :], NT).astype(BF)
        q = of_keys(r.q1[k])
        r.kvT1[k] = mm(r.own[f, 192:576, :], rows[...], NT).astype(BF)
        for i in range(3):
            scores = jnp.where(allowed(e), mm(r.kv1[k, :, key_lanes[i]], q[i], NT) + bias_of(f, i), MASKED)
            most = jnp.max(scores, axis=0, keepdims=True)
            p = jnp.exp(scores - most)
            total = jnp.sum(p, axis=0, keepdims=True)
            o = mm(r.kvT1[k, 192 + 64 * i:256 + 64 * i, :], p.astype(BF))
            r.mix1[f, 64 * i:64 * i + 64, columns(e)] = (o / total).astype(BF)
            r.lse[k, i:i + 1, :] = most + jnp.log(total)
        return 0

    def self_far(h):
        n, e, cols = 128 * (h + 1), 1 - x, slice(128 * h, 128 * h + 128)

        def turn(i, _):
            f = c + i * (1 - 2 * c)
            k = 2 * e + f
            rows = r.n1.at[half(256 * e, h), :]
            r.q1[k, cols, :] = (mm(rows[...], r.own[f, 0:192, :], NT) * 0.125).astype(BF)
            r.kv1[k, cols, :] = mm(rows[...], r.own[f, 192:576, :], NT).astype(BF)
            r.kvT1[k, :, cols] = mm(r.own[f, 192:576, :], rows[...], NT).astype(BF)
            q = of_keys(r.q1[k, cols, :])
            for j in range(3):
                scores = mm(r.kv1[k, 0:n, key_lanes[j]], q[j], NT) + bias_of(f, j)[0:n, cols]
                scores = jnp.where(allowed(e)[0:n, cols], scores, MASKED)
                most = jnp.max(scores, axis=0, keepdims=True)
                p = jnp.exp(scores - most)
                total = jnp.sum(p, axis=0, keepdims=True)
                o = mm(r.kvT1[k, 192 + 64 * j:256 + 64 * j, 0:n], p.astype(BF))
                r.mix1[f, 64 * j:64 * j + 64, pl.ds(pl.multiple_of(256 * e + 128 * h, 128), 128)] = (o / total).astype(BF)
                r.lse[k, j:j + 1, cols] = most + jnp.log(total)
            return 0

        lax.fori_loop(0, 2, turn, 0)
        r.out[0, cols, :] = self_out(pl.ds(pl.multiple_of(256 * e + 128 * h, 128), 128)).astype(BF)
        give_s1[h].start()

    def self_out(at):
        return mm(r.mix1[0, :, at].T, r.own[0, 576:768, :]) + mm(r.mix1[1, :, at].T, r.own[1, 576:768, :])

    turns = take(2)
    lax.fori_loop(0, 2, self_forward, 0)
    here()
    near_memory()
    for h in range(2):
        here()
        trade_n1[h].wait_recv()
        self_far(h)
    gather_step(2, 0)
    cotangent_load.wait()
    trade_cot.start()
    r.s1[...] = r.s0[...] + self_out(columns(x))
    here()
    project_memory(tx)
    here()
    gather_step(0, 6)
    project_memory(td)
    here()
    for d in give_s1:
        d.wait_recv()
    x1 = r.s1[...] + r.arrived[0].astype(F32)
    r.s1[...] = x1
    r.n2[...] = (x1 * inverse_of(x1) * g_cross).astype(BF)
    gather_step(1, 5)

    def cross_scores(shard, i, b, q):
        at = slice(256 * b, 256 * b + 256)
        return mm(r.kv[shard, at, key_lanes[i]], q, NT) + jnp.concatenate([r.mask2[at, :]] * 2, axis=1)

    def cross_forward(s, _):
        hooks(s, turns_1, {3: lambda: gather_step(1, 6)})
        k = fwd_shard(s)
        r.q2[k] = (mm(r.n2[...], r.cross[k, 384:576, :], NT) * 0.125).astype(BF)
        q = of_keys(r.q2[k])
        for i in range(3):
            ss = [cross_scores(k, i, b, q[i]) for b in range(4)]
            most = jnp.max(jnp.maximum(jnp.maximum(ss[0], ss[1]), jnp.maximum(ss[2], ss[3])), axis=0, keepdims=True)
            total, o = 0.0, 0.0
            for b in range(4):
                p = jnp.exp(ss[b] - most)
                total = total + jnp.sum(p, axis=0, keepdims=True)
                o = o + mm(r.kvT[k, 192 + 64 * i:256 + 64 * i, 256 * b:256 * b + 256], p.astype(BF))
            r.mix2[k, 64 * i:64 * i + 64, :] = (o / total).astype(BF)
            r.lse[4 + k, i:i + 1, :] = most + jnp.log(total)
        return 0

    turns_1 = take(4)
    lax.fori_loop(0, 4, cross_forward, 0)
    here()
    gather_step(2, 5)
    gather_step(2, 6)
    x2 = r.s1[...]
    for k in range(4):
        x2 = x2 + mm(r.mix2[k].T, r.cross[k, 576:768, :])
    r.s2[...] = x2
    r.n3[mine, :] = (x2 * inverse_of(x2) * g_hid).astype(BF)
    start(trade_n3)
    r.sums[mine, :] = x2
    r.sums[other, :] = jnp.zeros_like(x2)
    r.grads[...] = jnp.zeros_like(r.grads)
    core_feed.wait_recv()

    def feed(f, first, n):
        at = rows_of(first, n)
        lanes = pl.ds(pl.multiple_of(first, 128), n)
        rows, cot = r.n3.at[at, :], r.cot.at[at, :]
        for i in range(3):
            cs = slice(256 * i, 256 * i + 256)
            v = mm(rows[...], r.feed[f, 0:768, cs])
            ga = mm(cot[...], r.feed[f, 768 + 256 * i:1024 + 256 * i, :], NT)
            phi = 0.5 * (1.0 + lax.erf(v * np.float32(1 / math.sqrt(2))))
            act = (v * phi).astype(BF)
            slope = phi + v * (jnp.exp(-0.5 * v * v) * np.float32(1 / math.sqrt(2 * math.pi)))
            r.act[0:n, cs] = act
            r.actT[f, cs, lanes] = act.T
            r.gb[f, at, cs] = (slope * ga).astype(BF)
        r.sums[at, :] += mm(r.act[0:n, :], r.feed[f, 768:1536, :])
        r.grads[at, :] += mm(r.gb[f, at, :], r.feed[f, 0:768, :], NT)

    def feed_both(first, n):
        def turn(i, _):
            feed(c + i * (1 - 2 * c), first, n)
            return 0
        lax.fori_loop(0, 2, turn, 0)

    here()
    feed_both(256 * x, 256)
    here()
    trade_cot.wait_recv()
    for h in range(2):
        if h:
            here()
        trade_n3[h].wait_recv()
        feed_both(256 - 256 * x + 128 * h, 128)
        r.out[2, 128 * h:128 * h + 128, :] = r.grads[half(256 - 256 * x, h), :].astype(BF)
        give_gn[h].start()
    r.out[1] = r.sums[other, :].astype(BF)
    give_lo.start()
    here()
    core_feed.wait_send()

    for i in range(3):
        n3T = r.n3[:, 256 * i:256 * i + 256].T
        for f in range(2):
            r.feed[f, 256 * i:256 * i + 256, :] = mm(n3T, r.gb[f]).astype(BF)
        here()
    for i in range(3):
        for f in range(2):
            r.feed[f, 768 + 256 * i:1024 + 256 * i, :] = mm(r.actT[f, 256 * i:256 * i + 256, :], r.cot[...]).astype(BF)
        here()
    for d in give_gn:
        d.wait_recv()
    d, gain = norm_back(x2, inverse_of(x2), g_hid, r.grads[mine, :] + r.arrived[2].astype(F32))

    def put_small(row, value):
        for i in range(3):
            at = 3 * row + i
            r.sm[at // 8, at % 8:at % 8 + 1, :] = value[:, 256 * i:256 * i + 256]

    r.sm[...] = jnp.zeros_like(r.sm)
    put_small(4, gain)
    r.gst[...] = r.cot[mine, :].astype(F32) + d
    gather_sent(range(3), (0, 1, 3, 4, 5, 6, 7, 8, 9, 10))
    here()
    r.rows2[...] = r.gst[...].astype(BF)
    r.acc[...] = jnp.zeros_like(x2)

    def cross_backward(s, _):
        hooks(s, turns_3)
        k = bwd_shard(s)
        rw = r.rows2[...]
        w = r.cross[k, 576:768, :]
        G = mm(rw, w, NT).astype(BF)
        GT = mm(w, rw, NT).astype(BF)
        r.cross[k, 576:768, :] = mm(r.mix2[k], rw).astype(BF)
        q, g = of_keys(r.q2[k]), of_values(G)
        inner = [jnp.sum(r.mix2[k, 64 * i:64 * i + 64, :].astype(F32) * GT[64 * i:64 * i + 64, :].astype(F32), axis=0, keepdims=True)
                 for i in range(3)]
        dqs = [0.0, 0.0, 0.0]
        for b in range(4):
            if b == 2:
                hooks(s, turns_m)
            at = slice(256 * b, 256 * b + 256)
            dks, dvs = [], []
            for i in range(3):
                p = jnp.exp(cross_scores(k, i, b, q[i]) - r.lse[4 + k, i:i + 1, :])
                gs = (p * (mm(r.kv[k, at, value_lanes[i]], g[i], NT) - inner[i])).astype(BF)
                dqs[i] = dqs[i] + mm(r.kvT[k, 64 * i:64 * i + 64, at], gs)
                dks.append(mm(gs, q[i]))
                dvs.append(mm(p.astype(BF), g[i]))
            r.kv[k, at, 0:128] = (dks[0] + dks[1]).astype(BF)
            r.kv[k, at, 128:256] = (dks[2] + dvs[0]).astype(BF)
            r.kv[k, at, 256:384] = (dvs[1] + dvs[2]).astype(BF)
        dqs = [(d * 0.125).astype(BF) for d in dqs]
        r.kvT[k] = r.kv[k].T
        dqT = jnp.concatenate(dqs, axis=0)
        r.acc[...] += mm(dqT.T, r.cross[k, 384:576, :])
        r.cross[k, 384:576, :] = mm(dqT, r.n2[...]).astype(BF)
        return 0

    turns_3, turns_m = take(4), take(4)
    lax.fori_loop(0, 4, cross_backward, 0)
    here()
    x1 = r.s1[...]
    d, gain = norm_back(x1, inverse_of(x1), g_cross, r.acc[...])
    put_small(3, gain)
    x1 = r.gst[...] + d
    r.gst[...] = x1
    r.rows1[mine, :] = x1.astype(BF)
    trade_rows.start()
    here()
    give_lo.wait_recv()
    r.lov[...] = (r.sums[mine, :] + r.arrived[1].astype(F32)).astype(BF)
    stores = [pltpu.make_async_copy(a, b, r.esem.at[i]) for i, (a, b) in enumerate(((r.lov, r.lo), (r.gmv, r.gmem), (r.gtv, r.gtok)))]
    stores[0].start()

    def memory_grad(i, _):
        at = rows_of(i * 256, 256)
        total = 0.0
        for k in range(4):
            total = total + mm(r.kv[k, at, :], r.cross[k, 0:384, :])
        r.gmv[at, :] = total.astype(BF)
        return 0

    lax.fori_loop(0, 4, memory_grad, 0)
    stores[1].start()
    here()

    def memory_weights(s, _):
        hooks(s, turns_4)
        k = bwd_shard(s)

        def block(i, _):
            at = rows_of(i * 192, 192)
            r.cross[k, at, :] = mm(r.kvT[k, at, :], r.mem[...]).astype(BF)
            return 0
        lax.fori_loop(0, 2, block, 0)
        return 0

    turns_4 = take(4)
    lax.fori_loop(0, 4, memory_weights, 0)
    here()
    r.grads[...] = jnp.zeros_like(r.grads)

    def self_backward(s, _):
        hooks(s, turns_5, {2: trade_rows.wait_recv})
        e, f = item_shard(s)
        k = 2 * e + f
        here_rows = rows_of(256 * e, 256)
        rw = r.rows1[here_rows, :]
        w = r.own[f, 576:768, :]
        G = mm(rw, w, NT).astype(BF)
        GT = mm(w, rw, NT).astype(BF)
        flip = (ji + ii == 255).astype(BF)
        q, g = of_keys(r.q1[k]), of_values(G)
        dqs, dks, dvs = [], [], []
        for i in range(3):
            gT = GT[64 * i:64 * i + 64, :]
            inner = jnp.sum(r.mix1[f, 64 * i:64 * i + 64, columns(e)].astype(F32) * gT.astype(F32), axis=0, keepdims=True)
            scores = jnp.where(allowed(e), mm(r.kv1[k, :, key_lanes[i]], q[i], NT) + bias_of(f, i), MASKED)
            p = jnp.exp(scores - r.lse[k, i:i + 1, :])
            gs = (p * (mm(r.kv1[k, :, value_lanes[i]], g[i], NT) - inner)).astype(BF)
            dvs.append(mm(p.astype(BF), g[i]))
            dks.append(mm(gs, q[i]))
            dqs.append((mm(r.kvT1[k, 64 * i:64 * i + 64, :], gs) * 0.125).astype(BF))
            shifted = pltpu.roll(mm(flip, gs), 1, 1, stride=1, stride_axis=0)
            r.sm[2 + 2 * x + f, i:i + 1, :] += jnp.sum(shifted, axis=0, keepdims=True)
        dqT = jnp.concatenate(dqs, axis=0)
        dkv = jnp.concatenate([dks[0] + dks[1], dks[2] + dvs[0], dvs[1] + dvs[2]], axis=1).astype(BF)
        r.gT[f, 0:192, columns(e)] = dqT
        r.gT[f, 192:576, columns(e)] = dkv.T
        r.grads[here_rows, :] += mm(dqT.T, r.own[f, 0:192, :]) + mm(dkv, r.own[f, 192:576, :])
        return 0

    turns_5 = take(4)
    lax.fori_loop(0, 4, self_backward, 0)
    r.out[3] = r.grads[other, :].astype(BF)
    give_gn1.start()
    core_own.wait_send()
    here()
    for f in range(2):
        r.own[f, 0:384, :] = mm(r.gT[f, 0:384, :], r.n1[...]).astype(BF)
    here()
    for f in range(2):
        r.own[f, 384:576, :] = mm(r.gT[f, 384:576, :], r.n1[...]).astype(BF)
        r.own[f, 576:768, :] = mm(r.mix1[f], r.rows1[...]).astype(BF)
    here()
    give_gn1.wait_recv()
    x0 = r.s0[...]
    d, gain = norm_back(x0, inverse_of(x0), g_self, r.grads[mine, :] + r.arrived[3].astype(F32))
    put_small(2, gain)
    g0 = r.gst[...] + d
    r.gtv[...] = g0.astype(BF)
    stores[2].start()
    put_small(0, jnp.sum(jnp.where(tagged(), 0.0, g0), axis=0, keepdims=True))
    put_small(1, jnp.sum(jnp.where(tagged(), g0, 0.0), axis=0, keepdims=True))
    here()
    here()
    for j in range(6, len(to) + 1):
        small_step(j)
    r.smo[...] = r.sm[0:2]
    r.dgo[...] = r.sm[2 + t]
    for n, p in enumerate(plans):
        for d in [d for d, _, _ in p.core] + sum([copies for copies, _ in p.stages], []) + sum(p.back, []):
            d.wait_send()
        out_copy(n).wait()
    for d in stores:
        d.wait()
    for d in trade + trade_n1 + trade_n3 + give + give_s1 + give_gn + [core_tab]:
        d.wait_send()


def layer(bits, ins):
    S = jax.ShapeDtypeStruct
    V, A, M = (pl.BlockSpec(memory_space=s) for s in (pltpu.VMEM, pl.ANY, pltpu.SMEM))
    vm = pltpu.VMEM
    inputs = dict(tok_in=A, mem_in=A, cot_in=A, lengths=M, mmask_in=A, tags_in=A, emb_in=A, gain1_in=A, gain2_in=A, gain3_in=A, tab_in=A,
                  sq=A, sk=A, sv=A, so=A, cq=A, ck=A, cv=A, co=A, hin=A, hout=A)
    wide, square = (256, 768), (768, 768)
    out = dict(lo=S(wide, BF), gtok=S(wide, BF), gmem=S((1024, 768), BF), smo=S((2, 8, 256), F32), dgo=S((8, 256), F32),
               own_out=S(square, BF), cross_out=S(square, BF), feed_out=S((1536, 768), BF))
    out_specs = [A, A, A, V, V, A, A, A]
    sizes = [n for _, _, n, _ in CHUNKS]

    def parts_of(n, order):
        shards, buffers = 2 if "x" in order else 1, []
        for d in order:
            if d == "x":
                shards = 1
                buffers.append(vm((1, n, 768), BF))
            else:
                n = n // 4 if d == "q" else n // 2
                buffers.append(vm((shards * (3 if d == "q" else 1), n, 768), BF))
        return buffers

    both = (512, 768)
    scratch = dict(
        own=vm((2, 768, 768), BF), cross=vm((4, 768, 768), BF), feed=vm((2, 1536, 768), BF),
        tok=vm(wide, BF), cot=vm(both, BF), mem=vm((1024, 768), BF), n1=vm(both, BF), n3=vm(both, BF), rows1=vm(both, BF),
        out=vm((4, 256, 768), BF), arrived=vm((4, 256, 768), BF),
        s0=vm(wide, F32), s1=vm(wide, F32), s2=vm(wide, F32), gst=vm(wide, F32), acc=vm(wide, F32), sums=vm(both, F32), grads=vm(both, F32),
        n2=vm(wide, BF), rows2=vm(wide, BF), act=vm(wide, BF), actT=vm((2, 768, 512), BF), gb=vm((2, 512, 768), BF),
        q1=vm((4, 256, 192), BF), kv1=vm((4, 256, 384), BF), kvT1=vm((4, 384, 256), BF), q2=vm((4, 256, 192), BF), gT=vm((2, 576, 512), BF),
        kv=vm((4, 1024, 384), BF), kvT=vm((4, 384, 1024), BF), mix1=vm((2, 192, 512), BF), mix2=vm((4, 192, 256), BF),
        lse=vm((8, 8, 256), F32), mask2=vm((1024, 128), F32), tagv=vm((256, 128), F32), btab=vm((2, 8, 256), F32),
        mmask=vm((4, 1024), jnp.int32), tags=vm((1, 256), jnp.int32), emb=vm((2, 768), BF), gain1=vm((768,), BF), gain2=vm((768,), BF),
        gain3=vm((768,), BF), tab=vm((3, 32), BF),
        sm=vm((6, 8, 256), F32), smb=vm((2 + bits, 6, 8, 256), F32), gmv=vm((1024, 768), BF), lov=vm(wide, BF), gtv=vm(wide, BF),
    )
    first = [vm((2 if "x" in order else 1, n, 768), BF) for _, _, n, order in CHUNKS]
    parts = [parts_of(n, order) for _, _, n, order in CHUNKS]
    results = [vm((n, 768), BF) for n in sizes]
    more = [vm((bits - 3, n // 8, 768), BF) for n in sizes] if bits > 3 else []
    dma = pltpu.SemaphoreType.DMA
    sems = dict(gsend=dma((3, 11)), grecv=dma((3, 11)), xsend=dma((12,)), xrecv=dma((12,)), csend=dma((3,)), crecv=dma((3,)), rsend=dma((len(CHUNKS), 16 + bits)), rrecv=dma((len(CHUNKS), 16 + bits)), lsem=dma((20,)), osem=dma((len(CHUNKS),)),
                esem=dma((3,)), ssend=dma((2 + bits,)), srecv=dma((2 + bits,)))
    names = list(inputs) + list(out) + list(scratch) + list(sems)

    def kernel(*refs):
        r = SimpleNamespace(**dict(zip(names, refs)))
        rest = iter(refs[len(names):])
        r.parts = [[next(rest) for _ in p] for p in parts]
        r.result = [next(rest) for _ in results]
        r.more = [next(rest) for _ in more]
        r.first = [next(rest) for _ in first]
        layer_kernel(bits, r)

    return pl.pallas_call(
        kernel, out_shape=list(out.values()), in_specs=list(inputs.values()), out_specs=out_specs,
        scratch_shapes=list(scratch.values()) + list(sems.values()) + sum(parts, []) + results + more + first,
        compiler_params=pltpu.CompilerParams(collective_id=0, has_side_effects=True, vmem_limit_bytes=VMEM_LIMIT),
    )(*ins)


def finish_kernel(lo, gtok, gmem, smo, dgo, own, cross, feed,
                  o_lo, o_gtok, o_gmem, o_emb, o_g1, o_g2, o_g3, o_sq, o_sk, o_sv, o_so, o_pb, o_cq, o_ck, o_cv, o_co, o_hin, o_hout):
    o_lo[...] = lo[...]
    o_gtok[...] = gtok[...]
    o_gmem[...] = gmem[...]
    for i, o in enumerate((o_sq, o_sk, o_sv, o_so)):
        o[...] = own[192 * i:192 * i + 192, :].astype(F32)
    for i, o in enumerate((o_ck, o_cv, o_cq, o_co)):
        o[...] = cross[192 * i:192 * i + 192, :].astype(F32)
    o_hin[...] = feed[0:768, :].astype(F32)
    o_hout[...] = feed[768:1536, :].astype(F32)

    @pl.when(pl.program_id(0) == 0)
    def _():
        def small(row):
            return jnp.concatenate([smo[(3 * row + i) // 8, (3 * row + i) % 8:(3 * row + i) % 8 + 1, :] for i in range(3)], axis=1)
        o_emb[0:1, :] = small(0)
        o_emb[1:2, :] = small(1)
        o_g1[...] = small(2).reshape(768)
        o_g2[...] = small(3).reshape(768)
        o_g3[...] = small(4).reshape(768)
        total = lax.dot_general(dgo[...], bucket_onehot().astype(F32), NT, precision=lax.Precision.HIGHEST, preferred_element_type=F32)
        o_pb[...] = total[0:3, :]


def finish(args):
    S = jax.ShapeDtypeStruct
    n = 2
    cut = lambda rows: pl.BlockSpec((rows, 768 // n), lambda i: (0, i))
    full = lambda *s: pl.BlockSpec(s, lambda i: (0,) * len(s))
    flat, square = S((192, 768), F32), S((768, 768), F32)
    shapes = [S((256, 768), BF), S((256, 768), BF), S((1024, 768), BF), S((2, 768), F32)] + [S((768,), F32)] * 3
    shapes += [flat] * 4 + [S((3, 32), F32)] + [flat] * 4 + [square, square]
    ends = [cut(256), cut(256), cut(1024)]
    in_specs = ends + [full(2, 8, 256), full(8, 256), cut(768), cut(768), cut(1536)]
    out_specs = ends + [full(2, 768)] + [full(768)] * 3 + [cut(192)] * 4 + [full(3, 32)] + [cut(192)] * 4
    out_specs += [cut(768), cut(768)]
    return pl.pallas_call(finish_kernel, grid=(n,), out_shape=shapes, in_specs=in_specs, out_specs=out_specs,
                          compiler_params=pltpu.CompilerParams(vmem_limit_bytes=VMEM_LIMIT))(*args)


def per_device(bits, tokens, memory, cotangent, lengths, memory_mask, token_tags, embedding, gain_self, gain_cross, gain_hidden,
               self_query, self_key, self_value, self_output, position_bias, cross_query, cross_key, cross_value,
               cross_output, hidden_in, hidden_out):
    parts = layer(bits, (
        tokens[0], memory[0], cotangent[0], lengths, memory_mask, token_tags, embedding, gain_self, gain_cross, gain_hidden, position_bias.T,
        self_query.T, self_key.T, self_value.T, self_output, cross_query.T, cross_key.T, cross_value.T, cross_output, hidden_in, hidden_out))
    lo, gtok, gmem, g_emb, g1, g2, g3, sq, sk, sv, so, pb, cq, ck, cv, co, hin, hout = finish(parts)
    return (lo[None], gtok[None], gmem[None], g_emb, g1, g2, g3, sq.T, sk.T, sv.T, so, pb.T, cq.T, ck.T, cv.T, co, hin, hout)


def solution(mesh):
    bits = int(math.log2(mesh.shape["dp"]))
    item = P(("dp", "tensor"), None, None)
    col, row, rep = P(None, "tensor"), P("tensor", None), P()
    in_specs = (item, item, item, P("dp"), P("dp", None), P(("dp", "tensor"), None), rep, rep, rep, rep,
                col, col, col, row, col, col, col, col, row, col, row)
    out_specs = (item, item, item, rep, rep, rep, rep, col, col, col, row, col, col, col, col, row, col, row)
    return jax.shard_map(lambda *a: per_device(bits, *a), mesh=mesh, in_specs=in_specs, out_specs=out_specs, check_vma=False)
```

```python
import math
from types import SimpleNamespace

import jax
import jax.numpy as jnp
import numpy as np
from jax import lax
from jax.experimental import pallas as pl
from jax.experimental.pallas import tpu as pltpu
from jax.sharding import PartitionSpec as P

EPSILON = 1e-6
MASKED = -1e9
BUCKETS = 32
MAX_DISTANCE = 128
VMEM_LIMIT = 64 * 1024 * 1024 - 64 * 1024
F32 = jnp.float32
BF = jnp.bfloat16
NN = (((1,), (0,)), ((), ()))
NT = (((1,), (1,)), ((), ()))
MESH = pl.DeviceIdType.MESH

UNITS = ((0, 384), (384, 192), (576, 192))
CHUNKS = (
    (2, 0, 256, 'zyw'),
    (2, 256, 256, 'zwy'),
    (2, 512, 256, 'yzw'),
    (2, 768, 256, 'yzw'),
    (2, 1024, 512, 'yzw'),
    (1, 384, 128, 'xyzw'),
    (1, 512, 256, 'xyzw'),
    (1, 0, 128, 'xyzw'),
    (1, 128, 128, 'xyzw'),
    (1, 256, 128, 'xzyw'),
    (0, 0, 256, 'yzw'),
    (0, 256, 256, 'yzw'),
    (0, 512, 256, 'yzw'),
)
SCHEDULE = (
    (), (), (), (1,), (), (2, 3), (4, 11), (), (12, 13), (14,), (21,), (), (22, 23), (24,), (), (), (), (), (1000,), (1010,),
    (1020,), (1030,), (), (1040, 1001, 1011, 1021, 1031), (1041,), (), (1022,), (1032, 1050, 1060, 1023), (1002, 1033, 1013), (),
    (1012,), (), (1024, 1042), (), (1051, 1052, 1061, 1062, 1003, 1014, 1034), (1015, 1025), (), (), (1070, 1080, 1090), (1004,),
    (), (), (1035,), (1043, 1026), (1016, 1053), (1071, 1072, 1081, 1082, 1091, 1092, 1005, 1036), (1100, 1027),
    (1110, 1120, 1054, 1044, 1101, 1111, 1017, 1063, 1121, 1006, 1055, 1037, 1045, 1007), (200, 1102, 1056),
    (201, 1046, 1112, 1103, 1057, 1113, 1064, 1058, 1104, 1093, 1122, 202, 1114, 1065, 1105, 1073, 1123, 1047, 1083, 1115, 1059, 1094, 203, 1066, 1106, 1074, 1124, 1116, 1084, 204, 1095, 1067, 1107, 1075, 1125, 205, 1085, 1096, 1117, 1068, 1076, 1126, 1086, 1069, 1097, 1077, 1087, 1078, 1127, 1088, 1098, 1079, 1099, 1089),
)


class Remote:
    def __init__(self, *args):
        self.args = args

    def made(self):
        src, dst, send, recv, to = self.args
        return pltpu.make_async_remote_copy(
            src_ref=src, dst_ref=dst, send_sem=send, recv_sem=recv, device_id=to, device_id_type=MESH)

    def start(self):
        self.made().start()

    def wait(self):
        self.made().wait()

    def wait_send(self):
        self.made().wait_send()

    def wait_recv(self):
        self.made().wait_recv()


def mm(a, b, d=NN):
    return lax.dot_general(a, b, d, preferred_element_type=F32)


def inverse_of(h):
    return lax.rsqrt(jnp.mean(h * h, axis=-1, keepdims=True) + EPSILON)


def norm_back(h, inv, g, r):
    s = r * g
    gain = jnp.sum(r * h * inv, axis=0, keepdims=True)
    return inv * s - h * (inv * inv * inv) * jnp.mean(s * h, axis=-1, keepdims=True), gain


def rows_of(start, size):
    return pl.ds(pl.multiple_of(start, 16), size)


def add_into(dst, parts, into=None):
    rows = dst.shape[0]
    into = dst if into is None else into
    step = next(n for n in (64, 48, 32, 16) if rows % n == 0)

    def block(i, _):
        at = rows_of(i * step, step)
        total = dst[at, :].astype(F32)
        for part in parts:
            total = total + part[at, :].astype(F32)
        into[at, :] = total.astype(BF)
        return 0

    lax.fori_loop(0, rows // step, block, 0)


def bucket_of(length=256):
    exact = BUCKETS // 2
    n = np.arange(length)
    far = exact + np.floor(np.log(np.maximum(n, 1) / exact) / math.log(MAX_DISTANCE / exact) * (BUCKETS - exact)).astype(np.int32)
    return np.where(n < exact, n, np.minimum(far, BUCKETS - 1)).astype(np.int32)


def bucket_onehot():
    bucket = bucket_of()
    n = lax.broadcasted_iota(jnp.int32, (BUCKETS, 256), 1)
    chosen = jnp.zeros((BUCKETS, 256), jnp.int32)
    for b in range(1, BUCKETS):
        chosen = chosen + jnp.where(n >= int(np.argmax(bucket >= b)), 1, 0)
    return (chosen == lax.broadcasted_iota(jnp.int32, (BUCKETS, 256), 0)).astype(BF)


def layer_kernel(bits, r):
    dp = lax.axis_index("dp")
    t = lax.axis_index("tensor")
    c = lax.rem(t, 2)
    x = t // 2
    tc = t + 1 - 2 * c
    tx = t + 2 - 4 * x
    td = tc + 2 - 4 * x
    bit = [lax.rem(dp // (1 << b), 2) for b in range(bits)]
    pb = [dp + (1 << b) - (2 << b) * bit[b] for b in range(bits)]
    y, z1, z2 = bit[0], bit[1], bit[2]
    quad, quad_y, quad_z = y + 2 * z1, (1 - y) + 2 * z1, y + 2 * (1 - z1)
    quad_d = 3 - quad
    weights = (r.own, r.cross, r.feed)
    slot_of = lambda a, shard: shard if a == 1 else lax.rem(shard, 2)
    mine, other = rows_of(256 * x, 256), rows_of(256 - 256 * x, 256)

    def fwd_shard(s):
        a, b = lax.rem(s, 2), s // 2
        return 2 * (x + b * (1 - 2 * x)) + c + a * (1 - 2 * c)

    def bwd_shard(s):
        a, b = 1 - s // 2, 1 - lax.rem(s, 2)
        return 2 * (x + b * (1 - 2 * x)) + c + a * (1 - 2 * c)

    def item_shard(s):
        a, b = lax.rem(s, 2), s // 2
        return x + b * (1 - 2 * x), c + a * (1 - 2 * c)

    loads = []

    def load(src, dst):
        loads.append(pltpu.make_async_copy(src, dst, r.lsem.at[len(loads)]))
        loads[-1].start()
        return loads[-1]

    slot = lambda v, k, i: v.at[k, pl.ds(192 * i, 192), :]
    token_load = load(r.tok_in, r.tok)
    small_loads = [load(a, b) for a, b in ((r.emb_in, r.emb), (r.tags_in, r.tags), (r.gain1_in, r.gain1), (r.tab_in, r.tab),
                                           (r.gain2_in, r.gain2), (r.gain3_in, r.gain3), (r.mmask_in, r.mmask))]
    key_loads = [load(src, slot(r.cross, t, i)) for i, src in enumerate((r.ck, r.cv))]
    self_loads = [load(src, slot(r.own, c, i)) for i, src in enumerate((r.sq, r.sk, r.sv, r.so))]
    query_loads = [load(src, slot(r.cross, t, 2 + i)) for i, src in enumerate((r.cq, r.co))]
    memory_load = load(r.mem_in, r.mem)
    feed_loads = [load(src, r.feed.at[c, pl.ds(768 * i, 768), :]) for i, src in enumerate((r.hin, r.hout))]
    cotangent_load = load(r.cot_in, r.cot.at[mine, :])

    barrier = pltpu.get_barrier_semaphore()
    partners = [(dp, tc), (dp, tx)] + [(p, t) for p in pb]
    for p in partners:
        pl.semaphore_signal(barrier, inc=1, device_id=p, device_id_type=MESH)

    for d in small_loads:
        d.wait()
    g_self, g_cross, g_hid = (g[...].astype(F32).reshape(1, 768) for g in (r.gain1, r.gain2, r.gain3))
    ji = lax.broadcasted_iota(jnp.int32, (256, 256), 0)
    ii = lax.broadcasted_iota(jnp.int32, (256, 256), 1)
    r.btab[c, 0:3, :] = mm(r.tab[...], bucket_onehot())
    r.tagv[...] = jnp.broadcast_to((r.tags[...] == 1).astype(F32), (128, 256)).T
    tagged = lambda: jnp.concatenate([r.tagv[...]] * 6, axis=1) > 0.5
    token_load.wait()
    x0 = r.tok[...].astype(F32) + jnp.where(tagged(), r.emb[1:2, :].astype(F32), r.emb[0:1, :].astype(F32))
    r.s0[...] = x0
    r.n1[mine, :] = (x0 * inverse_of(x0) * g_self).astype(BF)
    pl.semaphore_wait(barrier, len(partners))

    def gather_copy(u, j):
        row, size = UNITS[u]
        v, q = r.cross, size // 4
        part = 32 if q == 48 else q // 2
        sems = (r.gsend.at[u, j], r.grecv.at[u, j])
        at = lambda shard, quarter, first=0, n=q: v.at[shard, rows_of(row + quarter * q + first, n), :]
        core, over_x, over_y, over_z = (dp, tc), (dp, tx), (pb[0], t), (pb[1], t)
        if j == 0:
            ref, to = v.at[t, pl.ds(row, size), :], core
        elif j == 1:
            ref, to = at(t, quad), over_x
        elif j == 3:
            ref, to = at(tx, quad), over_y
        elif j == 4:
            ref, to = at(tx, quad), over_z
        elif j == 5:
            ref, to = at(tx, quad), core
        elif j == 6:
            ref, to = at(tx, quad_y, part, q - part), over_z
        elif j == 7:
            ref, to = at(tx, quad_y), core
        elif j == 8:
            ref, to = at(tx, quad_z, 0, part), over_y
        elif j == 9:
            ref, to = at(tx, quad_z), core
        else:
            ref, to = at(tx, quad_d), core
        return Remote(ref, ref, *sems, to)

    GATHER = {0: ((), (1, 0)), 1: ((1,), (3, 4, 5)), 2: ((3,), (6, 7)), 3: ((4,), (8, 9)), 4: ((8, 6), (10,)),
              5: ((0,), ()), 6: ((5, 7, 9, 10), ())}

    def gather_step(u, step):
        arrived, onward = GATHER[step]
        for j in arrived:
            gather_copy(u, j).wait_recv()
        for j in onward:
            gather_copy(u, j).start()

    def gather_sent(us, js):
        for u in us:
            for j in js:
                gather_copy(u, j).wait_send()

    def view(n, shard, first=0, size=None):
        a, row, rows, _ = CHUNKS[n]
        return weights[a].at[slot_of(a, shard), rows_of(row + first, rows if size is None else size), :]

    def place(n, halves):
        first, size = 0, CHUNKS[n][2]
        for b in halves:
            size = size // 2
            first = first + b * size
        return first, size

    def result(n, halves):
        first, size = place(n, halves)
        return r.result[n].at[rows_of(first, size), :]

    flips = ((0, 1), (1, 0), (1, 1))
    turn = lambda b, f: b + f * (1 - 2 * b)
    along_z = [dp + f1 * (2 - 4 * z1) + f2 * (4 - 8 * z2) for f1, f2 in flips]

    count = iter(range(999))

    def plan_of(n):
        order, buffers = CHUNKS[n][3], iter(r.parts[n])
        halves, shards, stages, gathers = [], [tx, t] if "x" in order else [t], [], []

        def copy(src, dst, to):
            j = next(count)
            return Remote(src, dst, r.rsend.at[j], r.rrecv.at[j], to)

        def piece(shard, at):
            return view(n, shard, *place(n, at))

        for d in order:
            buf = next(buffers)
            if d == "x":
                stages.append(([copy(piece(tx, halves), buf.at[0], (dp, tx))], [(piece(t, halves), [buf.at[0]])]))
                shards = [t]
                continue
            if d == "q":
                mine, others = [z1, z2], [([turn(z1, f1), turn(z2, f2)], p) for (f1, f2), p in zip(flips, along_z)]
            else:
                b = "yzw".index(d)
                mine, others = [bit[b]], [([1 - bit[b]], pb[b])]
            m = len(others)
            stages.append((
                [copy(piece(k, halves + o), buf.at[m * i + j], (p, t)) for i, k in enumerate(shards) for j, (o, p) in enumerate(others)],
                [(piece(k, halves + mine), [buf.at[m * i + j] for j in range(m)]) for i, k in enumerate(shards)]))
            halves = halves + mine
            gathers.append((list(halves), [p for _, p in others]))
        back = [[copy(result(n, at), result(n, at), (p, t)) for p in ps] for at, ps in reversed(gathers)]
        more = [(copy(piece(t, halves), r.more[n].at[b - 3], (pb[b], t)), r.more[n].at[b - 3]) for b in range(3, bits)]
        far = [(td, tx)] if "x" in order else []
        core = [(copy(view(n, a), r.first[n].at[i], (dp, tc)), view(n, b), r.first[n].at[i]) for i, (a, b) in enumerate(far + [(tc, t)])]
        return SimpleNamespace(core=core, stages=stages, back=back, more=more, mine=piece(t, halves), result=result(n, halves))

    plans = [plan_of(n) for n in range(len(CHUNKS))]

    def out_copy(n):
        a, row, rows, _ = CHUNKS[n]
        return pltpu.make_async_copy(r.result[n], (r.own_out, r.cross_out, r.feed_out)[a].at[pl.ds(row, rows), :], r.osem.at[n])

    def start(copies):
        for d in copies:
            d.start()

    def sent_of(p):
        return [d for d, _, _ in p.core] + sum([copies for copies, _ in p.stages], []) + sum(p.back, [])

    def reduce_step(n, j):
        p = plans[n]
        m = len(p.core)
        if j == 0:
            start([d for d, _, _ in p.core])
        elif j <= m:
            copy, target, part = p.core[j - 1]
            copy.wait_recv()
            add_into(target, [part])
            if j == (1 if CHUNKS[n][3][0] == "x" else m):
                start(p.stages[0][0])
        elif j - m <= len(p.stages):
            copies, sums = p.stages[j - m - 1]
            for d in copies:
                d.wait_recv()
            last = j - m == len(p.stages)
            for target, parts in sums:
                add_into(target, parts, p.result if last and not p.more else None)
            if not last:
                start(p.stages[j - m][0])
                return
            for i, (copy, part) in enumerate(p.more):
                copy.start()
                copy.wait()
                add_into(p.mine, [part], p.result if i + 1 == len(p.more) else None)
            start(p.back[0])
        else:
            i = j - m - 1 - len(p.stages)
            for d in p.back[i]:
                d.wait_recv()
            if i + 1 < len(p.back):
                start(p.back[i + 1])
            else:
                out_copy(n).start()
                for d in sent_of(p)[:-len(p.back[-1])]:
                    d.wait_send()

    to = [(dp, tc), (dp, tx)] + [(p, t) for p in pb]

    small_stores = [pltpu.make_async_copy(r.sm.at[pl.ds(0, 2)], r.smo, r.esem.at[3]),
                    pltpu.make_async_copy(r.sm.at[2 + t], r.dgo, r.esem.at[4])]

    def small_step(j):
        if j:
            Remote(r.sm, r.smb.at[j - 1], r.ssend.at[j - 1], r.srecv.at[j - 1], to[j - 1]).wait()
            r.sm[...] = r.sm[...] + r.smb[j - 1]
        if j == len(to):
            for d in small_stores:
                d.start()
        if j < len(to):
            Remote(r.sm, r.smb.at[j], r.ssend.at[j], r.srecv.at[j], to[j]).start()

    places = iter(SCHEDULE)

    def run(todo):
        for e in todo:
            if e >= 1000:
                reduce_step((e - 1000) // 10, e % 10)
            elif e >= 200:
                small_step(e - 200)
            else:
                gather_step(e // 10, e % 10)

    def here():
        run(next(places))

    def take(count):
        return [next(places) for _ in range(count)]

    def hooks(s, todos, extra=None):
        for k, todo in enumerate(todos):
            more = (extra or {}).get(k)
            if todo or more:
                @pl.when(s == k)
                def _():
                    run(todo)
                    if more:
                        more()

    def over_x(j, src, dst):
        return Remote(src, dst, r.xsend.at[j], r.xrecv.at[j], (dp, tx))

    def to_core(j, src, dst):
        return Remote(src, dst, r.csend.at[j], r.crecv.at[j], (dp, tc))

    def half(start, h):
        return rows_of(start + 128 * h, 128)

    trade_cot, trade_rows = trade = [over_x(j, v.at[mine, :], v.at[mine, :]) for j, v in enumerate((r.cot, r.rows1))]
    trade_n1, trade_n3 = ([over_x(2 + 2 * j + h, v.at[half(256 * x, h), :], v.at[half(256 * x, h), :]) for h in range(2)]
                          for j, v in enumerate((r.n1, r.n3)))
    give_lo, give_gn1 = give = [over_x(6 + j, r.out.at[i], r.arrived.at[i]) for j, i in enumerate((1, 3))]
    give_s1, give_gn = ([over_x(8 + 2 * j + h, r.out.at[i, half(0, h), :], r.arrived.at[i, half(0, h), :]) for h in range(2)]
                        for j, i in enumerate((0, 2)))
    core_own, core_feed, core_tab = (to_core(j, v.at[c], v.at[c]) for j, v in enumerate((r.own, r.feed, r.btab)))
    for d in key_loads:
        d.wait()
    gather_step(0, 0)
    start(trade_n1)
    for d in self_loads:
        d.wait()
    core_own.start()
    core_tab.start()
    for d in query_loads:
        d.wait()
    gather_step(1, 0)
    for d in feed_loads:
        d.wait()
    core_feed.start()

    def bias_of(f, i):
        return pltpu.roll(jnp.broadcast_to(r.btab[f, i:i + 1, :], (256, 256)), 0, 1, stride=1, stride_axis=0)

    def allowed(e):
        return (ji <= ii) & (ji < r.lengths[2 * e + c])

    lane = lax.broadcasted_iota(jnp.int32, (1, 128), 1)
    low, high = lane < 64, lane >= 64

    def of_keys(a):
        wide = jnp.concatenate([a, jnp.zeros((a.shape[0], 64), a.dtype)], axis=1)
        return [jnp.where(low, wide[:, 0:128], 0), jnp.where(high, wide[:, 0:128], 0), jnp.where(low, wide[:, 128:256], 0)]

    def of_values(a):
        wide = jnp.concatenate([jnp.zeros((a.shape[0], 64), a.dtype), a], axis=1)
        return [jnp.where(high, wide[:, 0:128], 0), jnp.where(low, wide[:, 128:256], 0), jnp.where(high, wide[:, 128:256], 0)]

    key_lanes = (slice(0, 128), slice(0, 128), slice(128, 256))
    value_lanes = (slice(128, 256), slice(256, 384), slice(256, 384))

    def columns(e):
        return pl.ds(pl.multiple_of(256 * e, 256), 256)

    def project_memory(shard):
        w = r.cross.at[shard, pl.ds(0, 384), :]

        def block(i, _):
            at = rows_of(i * 256, 256)
            r.kv[shard, at, :] = mm(r.mem[at, :], w[...], NT).astype(BF)
            return 0
        lax.fori_loop(0, 4, block, 0)
        for i in range(4):
            r.kvT[shard, :, 256 * i:256 * i + 256] = mm(w[...], r.mem[256 * i:256 * i + 256, :], NT).astype(BF)

    def near_self():
        core_own.wait_recv()
        core_tab.wait_recv()

    def near_memory():
        memory_load.wait()
        valid = r.mmask[pl.ds(t, 1), :]
        r.mask2[...] = jnp.broadcast_to(jnp.where(valid == 1, 0.0, MASKED).astype(F32), (128, 1024)).T
        project_memory(t)
        here()
        gather_step(0, 5)
        project_memory(tc)

    def self_forward(s, _):
        hooks(s, turns, {1: near_self})
        e, f = x, c + s * (1 - 2 * c)
        k = 2 * e + f
        rows = r.n1.at[rows_of(256 * e, 256), :]
        r.q1[k] = (mm(rows[...], r.own[f, 0:192, :], NT) * 0.125).astype(BF)
        r.kv1[k] = mm(rows[...], r.own[f, 192:576, :], NT).astype(BF)
        q = of_keys(r.q1[k])
        r.kvT1[k] = mm(r.own[f, 192:576, :], rows[...], NT).astype(BF)
        for i in range(3):
            scores = jnp.where(allowed(e), mm(r.kv1[k, :, key_lanes[i]], q[i], NT) + bias_of(f, i), MASKED)
            most = jnp.max(scores, axis=0, keepdims=True)
            p = jnp.exp(scores - most)
            total = jnp.sum(p, axis=0, keepdims=True)
            o = mm(r.kvT1[k, 192 + 64 * i:256 + 64 * i, :], p.astype(BF))
            r.mix1[f, 64 * i:64 * i + 64, columns(e)] = (o / total).astype(BF)
            r.lse[k, i:i + 1, :] = most + jnp.log(total)
        return 0

    def self_far(h):
        n, e, cols = 128 * (h + 1), 1 - x, slice(128 * h, 128 * h + 128)

        def turn(i, _):
            f = c + i * (1 - 2 * c)
            k = 2 * e + f
            rows = r.n1.at[half(256 * e, h), :]
            r.q1[k, cols, :] = (mm(rows[...], r.own[f, 0:192, :], NT) * 0.125).astype(BF)
            r.kv1[k, cols, :] = mm(rows[...], r.own[f, 192:576, :], NT).astype(BF)
            r.kvT1[k, :, cols] = mm(r.own[f, 192:576, :], rows[...], NT).astype(BF)
            q = of_keys(r.q1[k, cols, :])
            for j in range(3):
                scores = mm(r.kv1[k, 0:n, key_lanes[j]], q[j], NT) + bias_of(f, j)[0:n, cols]
                scores = jnp.where(allowed(e)[0:n, cols], scores, MASKED)
                most = jnp.max(scores, axis=0, keepdims=True)
                p = jnp.exp(scores - most)
                total = jnp.sum(p, axis=0, keepdims=True)
                o = mm(r.kvT1[k, 192 + 64 * j:256 + 64 * j, 0:n], p.astype(BF))
                r.mix1[f, 64 * j:64 * j + 64, pl.ds(pl.multiple_of(256 * e + 128 * h, 128), 128)] = (o / total).astype(BF)
                r.lse[k, j:j + 1, cols] = most + jnp.log(total)
            return 0

        lax.fori_loop(0, 2, turn, 0)
        r.out[0, cols, :] = self_out(pl.ds(pl.multiple_of(256 * e + 128 * h, 128), 128)).astype(BF)
        give_s1[h].start()

    def self_out(at):
        return mm(r.mix1[0, :, at].T, r.own[0, 576:768, :]) + mm(r.mix1[1, :, at].T, r.own[1, 576:768, :])

    turns = take(2)
    lax.fori_loop(0, 2, self_forward, 0)
    here()
    near_memory()
    for h in range(2):
        here()
        trade_n1[h].wait_recv()
        self_far(h)
    gather_step(2, 0)
    cotangent_load.wait()
    trade_cot.start()
    r.s1[...] = r.s0[...] + self_out(columns(x))
    here()
    project_memory(tx)
    here()
    gather_step(0, 6)
    project_memory(td)
    here()
    for d in give_s1:
        d.wait_recv()
    x1 = r.s1[...] + r.arrived[0].astype(F32)
    r.s1[...] = x1
    r.n2[...] = (x1 * inverse_of(x1) * g_cross).astype(BF)
    gather_step(1, 5)

    def cross_scores(shard, i, b, q):
        at = slice(256 * b, 256 * b + 256)
        return mm(r.kv[shard, at, key_lanes[i]], q, NT) + jnp.concatenate([r.mask2[at, :]] * 2, axis=1)

    def cross_forward(s, _):
        hooks(s, turns_1, {3: lambda: gather_step(1, 6)})
        k = fwd_shard(s)
        r.q2[k] = (mm(r.n2[...], r.cross[k, 384:576, :], NT) * 0.125).astype(BF)
        q = of_keys(r.q2[k])
        for i in range(3):
            ss = [cross_scores(k, i, b, q[i]) for b in range(4)]
            most = jnp.max(jnp.maximum(jnp.maximum(ss[0], ss[1]), jnp.maximum(ss[2], ss[3])), axis=0, keepdims=True)
            total, o = 0.0, 0.0
            for b in range(4):
                p = jnp.exp(ss[b] - most)
                total = total + jnp.sum(p, axis=0, keepdims=True)
                o = o + mm(r.kvT[k, 192 + 64 * i:256 + 64 * i, 256 * b:256 * b + 256], p.astype(BF))
            r.mix2[k, 64 * i:64 * i + 64, :] = (o / total).astype(BF)
            r.lse[4 + k, i:i + 1, :] = most + jnp.log(total)
        return 0

    turns_1 = take(4)
    lax.fori_loop(0, 4, cross_forward, 0)
    here()
    gather_step(2, 5)
    gather_step(2, 6)
    x2 = r.s1[...]
    for k in range(4):
        x2 = x2 + mm(r.mix2[k].T, r.cross[k, 576:768, :])
    r.s2[...] = x2
    r.n3[mine, :] = (x2 * inverse_of(x2) * g_hid).astype(BF)
    start(trade_n3)
    r.sums[mine, :] = x2
    r.sums[other, :] = jnp.zeros_like(x2)
    r.grads[...] = jnp.zeros_like(r.grads)
    core_feed.wait_recv()

    def feed(f, first, n):
        at = rows_of(first, n)
        lanes = pl.ds(pl.multiple_of(first, 128), n)
        rows, cot = r.n3.at[at, :], r.cot.at[at, :]
        for i in range(3):
            cs = slice(256 * i, 256 * i + 256)
            v = mm(rows[...], r.feed[f, 0:768, cs])
            ga = mm(cot[...], r.feed[f, 768 + 256 * i:1024 + 256 * i, :], NT)
            phi = 0.5 * (1.0 + lax.erf(v * np.float32(1 / math.sqrt(2))))
            act = (v * phi).astype(BF)
            slope = phi + v * (jnp.exp(-0.5 * v * v) * np.float32(1 / math.sqrt(2 * math.pi)))
            r.act[0:n, cs] = act
            r.actT[f, cs, lanes] = act.T
            r.gb[f, at, cs] = (slope * ga).astype(BF)
        r.sums[at, :] += mm(r.act[0:n, :], r.feed[f, 768:1536, :])
        r.grads[at, :] += mm(r.gb[f, at, :], r.feed[f, 0:768, :], NT)

    def feed_both(first, n):
        def turn(i, _):
            feed(c + i * (1 - 2 * c), first, n)
            return 0
        lax.fori_loop(0, 2, turn, 0)

    here()
    feed_both(256 * x, 256)
    here()
    trade_cot.wait_recv()
    for h in range(2):
        if h:
            here()
        trade_n3[h].wait_recv()
        feed_both(256 - 256 * x + 128 * h, 128)
        r.out[2, 128 * h:128 * h + 128, :] = r.grads[half(256 - 256 * x, h), :].astype(BF)
        give_gn[h].start()
    r.out[1] = r.sums[other, :].astype(BF)
    give_lo.start()
    here()
    core_feed.wait_send()

    for i in range(3):
        n3T = r.n3[:, 256 * i:256 * i + 256].T
        for f in range(2):
            r.feed[f, 256 * i:256 * i + 256, :] = mm(n3T, r.gb[f]).astype(BF)
        here()
    for i in range(3):
        for f in range(2):
            r.feed[f, 768 + 256 * i:1024 + 256 * i, :] = mm(r.actT[f, 256 * i:256 * i + 256, :], r.cot[...]).astype(BF)
        here()
    for d in give_gn:
        d.wait_recv()
    d, gain = norm_back(x2, inverse_of(x2), g_hid, r.grads[mine, :] + r.arrived[2].astype(F32))

    def put_small(row, value):
        for i in range(3):
            at = 3 * row + i
            r.sm[at // 8, at % 8:at % 8 + 1, :] = value[:, 256 * i:256 * i + 256]

    r.sm[...] = jnp.zeros_like(r.sm)
    put_small(4, gain)
    r.gst[...] = r.cot[mine, :].astype(F32) + d
    gather_sent(range(3), (0, 1, 3, 4, 5, 6, 7, 8, 9, 10))
    here()
    r.rows2[...] = r.gst[...].astype(BF)
    r.acc[...] = jnp.zeros_like(x2)

    def cross_backward(s, _):
        hooks(s, turns_3)
        k = bwd_shard(s)
        rw = r.rows2[...]
        w = r.cross[k, 576:768, :]
        G = mm(rw, w, NT).astype(BF)
        GT = mm(w, rw, NT).astype(BF)
        r.cross[k, 576:768, :] = mm(r.mix2[k], rw).astype(BF)
        q, g = of_keys(r.q2[k]), of_values(G)
        inner = [jnp.sum(r.mix2[k, 64 * i:64 * i + 64, :].astype(F32) * GT[64 * i:64 * i + 64, :].astype(F32), axis=0, keepdims=True)
                 for i in range(3)]
        dqs = [0.0, 0.0, 0.0]
        for b in range(4):
            if b == 2:
                hooks(s, turns_m)
            at = slice(256 * b, 256 * b + 256)
            dks, dvs = [], []
            for i in range(3):
                p = jnp.exp(cross_scores(k, i, b, q[i]) - r.lse[4 + k, i:i + 1, :])
                gs = (p * (mm(r.kv[k, at, value_lanes[i]], g[i], NT) - inner[i])).astype(BF)
                dqs[i] = dqs[i] + mm(r.kvT[k, 64 * i:64 * i + 64, at], gs)
                dks.append(mm(gs, q[i]))
                dvs.append(mm(p.astype(BF), g[i]))
            r.kv[k, at, 0:128] = (dks[0] + dks[1]).astype(BF)
            r.kv[k, at, 128:256] = (dks[2] + dvs[0]).astype(BF)
            r.kv[k, at, 256:384] = (dvs[1] + dvs[2]).astype(BF)
        dqs = [(d * 0.125).astype(BF) for d in dqs]
        r.kvT[k] = r.kv[k].T
        dqT = jnp.concatenate(dqs, axis=0)
        r.acc[...] += mm(dqT.T, r.cross[k, 384:576, :])
        r.cross[k, 384:576, :] = mm(dqT, r.n2[...]).astype(BF)
        return 0

    turns_3, turns_m = take(4), take(4)
    lax.fori_loop(0, 4, cross_backward, 0)
    here()
    x1 = r.s1[...]
    d, gain = norm_back(x1, inverse_of(x1), g_cross, r.acc[...])
    put_small(3, gain)
    x1 = r.gst[...] + d
    r.gst[...] = x1
    r.rows1[mine, :] = x1.astype(BF)
    trade_rows.start()
    here()
    give_lo.wait_recv()
    r.lov[...] = (r.sums[mine, :] + r.arrived[1].astype(F32)).astype(BF)
    stores = [pltpu.make_async_copy(a, b, r.esem.at[i]) for i, (a, b) in enumerate(((r.lov, r.lo), (r.gmv, r.gmem), (r.gtv, r.gtok)))]
    stores[0].start()

    def memory_grad(i, _):
        at = rows_of(i * 256, 256)
        total = 0.0
        for k in range(4):
            total = total + mm(r.kv[k, at, :], r.cross[k, 0:384, :])
        r.gmv[at, :] = total.astype(BF)
        return 0

    lax.fori_loop(0, 4, memory_grad, 0)
    stores[1].start()
    here()

    def memory_weights(s, _):
        hooks(s, turns_4)
        k = bwd_shard(s)

        def block(i, _):
            at = rows_of(i * 192, 192)
            r.cross[k, at, :] = mm(r.kvT[k, at, :], r.mem[...]).astype(BF)
            return 0
        lax.fori_loop(0, 2, block, 0)
        return 0

    turns_4 = take(4)
    lax.fori_loop(0, 4, memory_weights, 0)
    here()
    r.grads[...] = jnp.zeros_like(r.grads)

    def self_backward(s, _):
        hooks(s, turns_5, {2: trade_rows.wait_recv})
        e, f = item_shard(s)
        k = 2 * e + f
        here_rows = rows_of(256 * e, 256)
        rw = r.rows1[here_rows, :]
        w = r.own[f, 576:768, :]
        G = mm(rw, w, NT).astype(BF)
        GT = mm(w, rw, NT).astype(BF)
        flip = (ji + ii == 255).astype(BF)
        q, g = of_keys(r.q1[k]), of_values(G)
        dqs, dks, dvs = [], [], []
        for i in range(3):
            gT = GT[64 * i:64 * i + 64, :]
            inner = jnp.sum(r.mix1[f, 64 * i:64 * i + 64, columns(e)].astype(F32) * gT.astype(F32), axis=0, keepdims=True)
            scores = jnp.where(allowed(e), mm(r.kv1[k, :, key_lanes[i]], q[i], NT) + bias_of(f, i), MASKED)
            p = jnp.exp(scores - r.lse[k, i:i + 1, :])
            gs = (p * (mm(r.kv1[k, :, value_lanes[i]], g[i], NT) - inner)).astype(BF)
            dvs.append(mm(p.astype(BF), g[i]))
            dks.append(mm(gs, q[i]))
            dqs.append((mm(r.kvT1[k, 64 * i:64 * i + 64, :], gs) * 0.125).astype(BF))
            shifted = pltpu.roll(mm(flip, gs), 1, 1, stride=1, stride_axis=0)
            r.sm[2 + 2 * x + f, i:i + 1, :] += jnp.sum(shifted, axis=0, keepdims=True)
        dqT = jnp.concatenate(dqs, axis=0)
        dkv = jnp.concatenate([dks[0] + dks[1], dks[2] + dvs[0], dvs[1] + dvs[2]], axis=1).astype(BF)
        r.gT[f, 0:192, columns(e)] = dqT
        r.gT[f, 192:576, columns(e)] = dkv.T
        r.grads[here_rows, :] += mm(dqT.T, r.own[f, 0:192, :]) + mm(dkv, r.own[f, 192:576, :])
        return 0

    turns_5 = take(4)
    lax.fori_loop(0, 4, self_backward, 0)
    r.out[3] = r.grads[other, :].astype(BF)
    give_gn1.start()
    core_own.wait_send()
    here()
    for f in range(2):
        r.own[f, 0:384, :] = mm(r.gT[f, 0:384, :], r.n1[...]).astype(BF)
    here()
    for f in range(2):
        r.own[f, 384:576, :] = mm(r.gT[f, 384:576, :], r.n1[...]).astype(BF)
        r.own[f, 576:768, :] = mm(r.mix1[f], r.rows1[...]).astype(BF)
    here()
    for d in trade + trade_n1 + trade_n3 + give + give_s1 + give_gn + [core_tab]:
        d.wait_send()
    give_gn1.wait_recv()
    x0 = r.s0[...]
    d, gain = norm_back(x0, inverse_of(x0), g_self, r.grads[mine, :] + r.arrived[3].astype(F32))
    put_small(2, gain)
    g0 = r.gst[...] + d
    r.gtv[...] = g0.astype(BF)
    stores[2].start()
    put_small(0, jnp.sum(jnp.where(tagged(), 0.0, g0), axis=0, keepdims=True))
    put_small(1, jnp.sum(jnp.where(tagged(), g0, 0.0), axis=0, keepdims=True))
    here()
    here()
    for j in range(6, len(to) + 1):
        small_step(j)
    for n, p in enumerate(plans):
        for d in p.back[-1]:
            d.wait_send()
        out_copy(n).wait()
    for d in stores + small_stores:
        d.wait()


def layer(bits, ins):
    S = jax.ShapeDtypeStruct
    V, A, M = (pl.BlockSpec(memory_space=s) for s in (pltpu.VMEM, pl.ANY, pltpu.SMEM))
    vm = pltpu.VMEM
    inputs = dict(tok_in=A, mem_in=A, cot_in=A, lengths=M, mmask_in=A, tags_in=A, emb_in=A, gain1_in=A, gain2_in=A, gain3_in=A, tab_in=A,
                  sq=A, sk=A, sv=A, so=A, cq=A, ck=A, cv=A, co=A, hin=A, hout=A)
    wide, square = (256, 768), (768, 768)
    out = dict(lo=S(wide, BF), gtok=S(wide, BF), gmem=S((1024, 768), BF), smo=S((2, 8, 256), F32), dgo=S((8, 256), F32),
               own_out=S(square, BF), cross_out=S(square, BF), feed_out=S((1536, 768), BF))
    out_specs = [A] * len(out)
    sizes = [n for _, _, n, _ in CHUNKS]

    def parts_of(n, order):
        shards, buffers = 2 if "x" in order else 1, []
        for d in order:
            if d == "x":
                shards = 1
                buffers.append(vm((1, n, 768), BF))
            else:
                n = n // 4 if d == "q" else n // 2
                buffers.append(vm((shards * (3 if d == "q" else 1), n, 768), BF))
        return buffers

    both = (512, 768)
    scratch = dict(
        own=vm((2, 768, 768), BF), cross=vm((4, 768, 768), BF), feed=vm((2, 1536, 768), BF),
        tok=vm(wide, BF), cot=vm(both, BF), mem=vm((1024, 768), BF), n1=vm(both, BF), n3=vm(both, BF), rows1=vm(both, BF),
        out=vm((4, 256, 768), BF), arrived=vm((4, 256, 768), BF),
        s0=vm(wide, F32), s1=vm(wide, F32), s2=vm(wide, F32), gst=vm(wide, F32), acc=vm(wide, F32), sums=vm(both, F32), grads=vm(both, F32),
        n2=vm(wide, BF), rows2=vm(wide, BF), act=vm(wide, BF), actT=vm((2, 768, 512), BF), gb=vm((2, 512, 768), BF),
        q1=vm((4, 256, 192), BF), kv1=vm((4, 256, 384), BF), kvT1=vm((4, 384, 256), BF), q2=vm((4, 256, 192), BF), gT=vm((2, 576, 512), BF),
        kv=vm((4, 1024, 384), BF), kvT=vm((4, 384, 1024), BF), mix1=vm((2, 192, 512), BF), mix2=vm((4, 192, 256), BF),
        lse=vm((8, 8, 256), F32), mask2=vm((1024, 128), F32), tagv=vm((256, 128), F32), btab=vm((2, 8, 256), F32),
        mmask=vm((4, 1024), jnp.int32), tags=vm((1, 256), jnp.int32), emb=vm((2, 768), BF), gain1=vm((768,), BF), gain2=vm((768,), BF),
        gain3=vm((768,), BF), tab=vm((3, 32), BF),
        sm=vm((6, 8, 256), F32), smb=vm((2 + bits, 6, 8, 256), F32), gmv=vm((1024, 768), BF), lov=vm(wide, BF), gtv=vm(wide, BF),
    )
    first = [vm((2 if "x" in order else 1, n, 768), BF) for _, _, n, order in CHUNKS]
    parts = [parts_of(n, order) for _, _, n, order in CHUNKS]
    results = [vm((n, 768), BF) for n in sizes]
    more = [vm((bits - 3, n // 8, 768), BF) for n in sizes] if bits > 3 else []
    dma = pltpu.SemaphoreType.DMA
    copies = 0
    for _, _, _, order in CHUNKS:
        shards = 2 if "x" in order else 1
        copies += shards + bits - 3
        for d in order:
            if d == "x":
                shards, copies = 1, copies + 1
            else:
                copies += (shards + 1) * (3 if d == "q" else 1)
    sems = dict(gsend=dma((3, 11)), grecv=dma((3, 11)), xsend=dma((12,)), xrecv=dma((12,)), csend=dma((3,)), crecv=dma((3,)), rsend=dma((copies,)), rrecv=dma((copies,)), lsem=dma((20,)), osem=dma((len(CHUNKS),)),
                esem=dma((5,)), ssend=dma((2 + bits,)), srecv=dma((2 + bits,)))
    names = list(inputs) + list(out) + list(scratch) + list(sems)

    def kernel(*refs):
        r = SimpleNamespace(**dict(zip(names, refs)))
        rest = iter(refs[len(names):])
        r.parts = [[next(rest) for _ in p] for p in parts]
        r.result = [next(rest) for _ in results]
        r.more = [next(rest) for _ in more]
        r.first = [next(rest) for _ in first]
        layer_kernel(bits, r)

    return pl.pallas_call(
        kernel, out_shape=list(out.values()), in_specs=list(inputs.values()), out_specs=out_specs,
        scratch_shapes=list(scratch.values()) + list(sems.values()) + sum(parts, []) + results + more + first,
        compiler_params=pltpu.CompilerParams(collective_id=0, has_side_effects=True, vmem_limit_bytes=VMEM_LIMIT),
    )(*ins)


def finish_kernel(lo, gtok, gmem, smo, dgo, own, cross, feed,
                  o_lo, o_gtok, o_gmem, o_emb, o_g1, o_g2, o_g3, o_sq, o_sk, o_sv, o_so, o_pb, o_cq, o_ck, o_cv, o_co, o_hin, o_hout):
    o_lo[...] = lo[...]
    o_gtok[...] = gtok[...]
    o_gmem[...] = gmem[...]
    for i, o in enumerate((o_sq, o_sk, o_sv, o_so)):
        o[...] = own[192 * i:192 * i + 192, :].astype(F32)
    for i, o in enumerate((o_ck, o_cv, o_cq, o_co)):
        o[...] = cross[192 * i:192 * i + 192, :].astype(F32)
    o_hin[...] = feed[0:768, :].astype(F32)
    o_hout[...] = feed[768:1536, :].astype(F32)

    @pl.when(pl.program_id(0) == 0)
    def _():
        def small(row):
            return jnp.concatenate([smo[(3 * row + i) // 8, (3 * row + i) % 8:(3 * row + i) % 8 + 1, :] for i in range(3)], axis=1)
        o_emb[0:1, :] = small(0)
        o_emb[1:2, :] = small(1)
        o_g1[...] = small(2).reshape(768)
        o_g2[...] = small(3).reshape(768)
        o_g3[...] = small(4).reshape(768)
        total = lax.dot_general(dgo[...], bucket_onehot().astype(F32), NT, precision=lax.Precision.HIGHEST, preferred_element_type=F32)
        o_pb[...] = total[0:3, :]


def finish(args):
    S = jax.ShapeDtypeStruct
    n = 2
    cut = lambda rows: pl.BlockSpec((rows, 768 // n), lambda i: (0, i))
    full = lambda *s: pl.BlockSpec(s, lambda i: (0,) * len(s))
    flat, square = S((192, 768), F32), S((768, 768), F32)
    shapes = [S((256, 768), BF), S((256, 768), BF), S((1024, 768), BF), S((2, 768), F32)] + [S((768,), F32)] * 3
    shapes += [flat] * 4 + [S((3, 32), F32)] + [flat] * 4 + [square, square]
    ends = [cut(256), cut(256), cut(1024)]
    in_specs = ends + [full(2, 8, 256), full(8, 256), cut(768), cut(768), cut(1536)]
    out_specs = ends + [full(2, 768)] + [full(768)] * 3 + [cut(192)] * 4 + [full(3, 32)] + [cut(192)] * 4
    out_specs += [cut(768), cut(768)]
    return pl.pallas_call(finish_kernel, grid=(n,), out_shape=shapes, in_specs=in_specs, out_specs=out_specs,
                          compiler_params=pltpu.CompilerParams(vmem_limit_bytes=VMEM_LIMIT))(*args)


def per_device(bits, tokens, memory, cotangent, lengths, memory_mask, token_tags, embedding, gain_self, gain_cross, gain_hidden,
               self_query, self_key, self_value, self_output, position_bias, cross_query, cross_key, cross_value,
               cross_output, hidden_in, hidden_out):
    parts = layer(bits, (
        tokens[0], memory[0], cotangent[0], lengths, memory_mask, token_tags, embedding, gain_self, gain_cross, gain_hidden, position_bias.T,
        self_query.T, self_key.T, self_value.T, self_output, cross_query.T, cross_key.T, cross_value.T, cross_output, hidden_in, hidden_out))
    lo, gtok, gmem, g_emb, g1, g2, g3, sq, sk, sv, so, pb, cq, ck, cv, co, hin, hout = finish(parts)
    return (lo[None], gtok[None], gmem[None], g_emb, g1, g2, g3, sq.T, sk.T, sv.T, so, pb.T, cq.T, ck.T, cv.T, co, hin, hout)


def solution(mesh):
    bits = int(math.log2(mesh.shape["dp"]))
    item = P(("dp", "tensor"), None, None)
    col, row, rep = P(None, "tensor"), P("tensor", None), P()
    in_specs = (item, item, item, P("dp"), P("dp", None), P(("dp", "tensor"), None), rep, rep, rep, rep,
                col, col, col, row, col, col, col, col, row, col, row)
    out_specs = (item, item, item, rep, rep, rep, rep, col, col, col, row, col, col, col, col, row, col, row)
    return jax.shard_map(lambda *a: per_device(bits, *a), mesh=mesh, in_specs=in_specs, out_specs=out_specs, check_vma=False)
```

```python
import math
from types import SimpleNamespace

import jax
import jax.numpy as jnp
import numpy as np
from jax import lax
from jax.experimental import pallas as pl
from jax.experimental.pallas import tpu as pltpu
from jax.sharding import PartitionSpec as P

EPSILON = 1e-6
MASKED = -1e9
BUCKETS = 32
MAX_DISTANCE = 128
VMEM_LIMIT = 64 * 1024 * 1024 - 64 * 1024
F32 = jnp.float32
BF = jnp.bfloat16
NN = (((1,), (0,)), ((), ()))
NT = (((1,), (1,)), ((), ()))
MESH = pl.DeviceIdType.MESH

UNITS = ((0, 384), (384, 192), (576, 192))
CHUNKS = (
    (2, 0, 256, 'zyw'),
    (2, 256, 256, 'zwy'),
    (2, 512, 256, 'yzw'),
    (2, 768, 256, 'yzw'),
    (2, 1024, 512, 'yzw'),
    (1, 384, 128, 'xyzw'),
    (1, 512, 256, 'xyzw'),
    (1, 0, 128, 'xyzw'),
    (1, 128, 128, 'xyzw'),
    (1, 256, 128, 'xzyw'),
    (0, 0, 256, 'yzw'),
    (0, 256, 256, 'yzw'),
    (0, 512, 256, 'yzw'),
)
SCHEDULE = (
    (), (), (), (1,), (), (2, 3), (4, 11), (), (12, 13), (14,), (21,), (), (22, 23), (24,), (), (), (), (), (1000,), (1010,),
    (1020,), (1030,), (), (1040, 1001, 1011, 1021, 1031), (1041,), (), (1022,), (1032, 1050, 1060, 1023), (1002, 1033, 1013), (),
    (1012,), (), (1024, 1042), (), (1051, 1052, 1061, 1062, 1003, 1014, 1034), (1015, 1025), (), (), (1070, 1080, 1090), (1004,),
    (), (), (1035,), (1043, 1026), (1016, 1053), (1071, 1072, 1081, 1082, 1091, 1092, 1005, 1036), (1100, 1027),
    (1110, 1120, 1054, 1044, 1101, 1111, 1017, 1063, 1121, 1006, 1055, 1037, 1045, 1007), (200, 1102, 1056),
    (201, 1046, 1112, 1103, 1057, 1113, 1064, 1058, 1104, 1093, 1122, 202, 1114, 1065, 1105, 1073, 1123, 1047, 1083, 1115, 1059, 1094, 203, 1066, 1106, 1074, 1124, 1116, 1084, 204, 1095, 1067, 1107, 1075, 1125, 205, 1085, 1096, 1117, 1068, 1076, 1126, 1086, 1069, 1097, 1077, 1087, 1078, 1127, 1088, 1098, 1079, 1099, 1089),
)


class Remote:
    def __init__(self, *args):
        self.args = args

    def made(self):
        src, dst, send, recv, to = self.args
        return pltpu.make_async_remote_copy(
            src_ref=src, dst_ref=dst, send_sem=send, recv_sem=recv, device_id=to, device_id_type=MESH)

    def start(self):
        self.made().start()

    def wait(self):
        self.made().wait()

    def wait_send(self):
        self.made().wait_send()

    def wait_recv(self):
        self.made().wait_recv()


def mm(a, b, d=NN):
    return lax.dot_general(a, b, d, preferred_element_type=F32)


def inverse_of(h):
    return lax.rsqrt(jnp.mean(h * h, axis=-1, keepdims=True) + EPSILON)


def norm_back(h, inv, g, r):
    s = r * g
    gain = jnp.sum(r * h * inv, axis=0, keepdims=True)
    return inv * s - h * (inv * inv * inv) * jnp.mean(s * h, axis=-1, keepdims=True), gain


def rows_of(start, size):
    return pl.ds(pl.multiple_of(start, 16), size)


def add_into(dst, parts, into=None):
    rows = dst.shape[0]
    into = dst if into is None else into
    step = next(n for n in (64, 48, 32, 16) if rows % n == 0)

    def block(i, _):
        at = rows_of(i * step, step)
        total = dst[at, :].astype(F32)
        for part in parts:
            total = total + part[at, :].astype(F32)
        into[at, :] = total.astype(BF)
        return 0

    lax.fori_loop(0, rows // step, block, 0)


def bucket_of(length=256):
    exact = BUCKETS // 2
    n = np.arange(length)
    far = exact + np.floor(np.log(np.maximum(n, 1) / exact) / math.log(MAX_DISTANCE / exact) * (BUCKETS - exact)).astype(np.int32)
    return np.where(n < exact, n, np.minimum(far, BUCKETS - 1)).astype(np.int32)


def bucket_onehot():
    bucket = bucket_of()
    n = lax.broadcasted_iota(jnp.int32, (BUCKETS, 256), 1)
    chosen = jnp.zeros((BUCKETS, 256), jnp.int32)
    for b in range(1, BUCKETS):
        chosen = chosen + jnp.where(n >= int(np.argmax(bucket >= b)), 1, 0)
    return (chosen == lax.broadcasted_iota(jnp.int32, (BUCKETS, 256), 0)).astype(BF)


def layer_kernel(bits, r):
    dp = lax.axis_index("dp")
    t = lax.axis_index("tensor")
    c = lax.rem(t, 2)
    x = t // 2
    tc = t + 1 - 2 * c
    tx = t + 2 - 4 * x
    td = tc + 2 - 4 * x
    bit = [lax.rem(dp // (1 << b), 2) for b in range(bits)]
    pb = [dp + (1 << b) - (2 << b) * bit[b] for b in range(bits)]
    y, z1, z2 = bit[0], bit[1], bit[2]
    quad, quad_y, quad_z = y + 2 * z1, (1 - y) + 2 * z1, y + 2 * (1 - z1)
    quad_d = 3 - quad
    weights = (r.own, r.cross, r.feed)
    slot_of = lambda a, shard: shard if a == 1 else lax.rem(shard, 2)
    mine, other = rows_of(256 * x, 256), rows_of(256 - 256 * x, 256)

    def fwd_shard(s):
        a, b = lax.rem(s, 2), s // 2
        return 2 * (x + b * (1 - 2 * x)) + c + a * (1 - 2 * c)

    def bwd_shard(s):
        a, b = 1 - s // 2, 1 - lax.rem(s, 2)
        return 2 * (x + b * (1 - 2 * x)) + c + a * (1 - 2 * c)

    def item_shard(s):
        a, b = lax.rem(s, 2), s // 2
        return x + b * (1 - 2 * x), c + a * (1 - 2 * c)

    loads = []

    def load(src, dst):
        loads.append(pltpu.make_async_copy(src, dst, r.lsem.at[len(loads)]))
        loads[-1].start()
        return loads[-1]

    slot = lambda v, k, i: v.at[k, pl.ds(192 * i, 192), :]
    token_load = load(r.tok_in, r.tok)
    key_loads = [load(src, slot(r.cross, t, i)) for i, src in enumerate((r.ck, r.cv))]
    self_loads = [load(src, slot(r.own, c, i)) for i, src in enumerate((r.sq, r.sk, r.sv, r.so))]
    query_loads = [load(src, slot(r.cross, t, 2 + i)) for i, src in enumerate((r.cq, r.co))]
    memory_load = load(r.mem_in, r.mem)
    feed_loads = [load(src, r.feed.at[c, pl.ds(768 * i, 768), :]) for i, src in enumerate((r.hin, r.hout))]
    cotangent_load = load(r.cot_in, r.cot.at[mine, :])

    barrier = pltpu.get_barrier_semaphore()
    partners = [(dp, tc), (dp, tx)] + [(p, t) for p in pb]
    for p in partners:
        pl.semaphore_signal(barrier, inc=1, device_id=p, device_id_type=MESH)

    g_self, g_cross, g_hid = (g[...].astype(F32).reshape(1, 768) for g in (r.gain1, r.gain2, r.gain3))
    ji = lax.broadcasted_iota(jnp.int32, (256, 256), 0)
    ii = lax.broadcasted_iota(jnp.int32, (256, 256), 1)
    r.btab[c, 0:3, :] = mm(r.tab[...], bucket_onehot())
    r.tagv[...] = jnp.broadcast_to((r.tags[...] == 1).astype(F32), (128, 256)).T
    tagged = lambda: jnp.concatenate([r.tagv[...]] * 6, axis=1) > 0.5
    token_load.wait()
    x0 = r.tok[...].astype(F32) + jnp.where(tagged(), r.emb[1:2, :].astype(F32), r.emb[0:1, :].astype(F32))
    r.s0[...] = x0
    r.n1[mine, :] = (x0 * inverse_of(x0) * g_self).astype(BF)
    pl.semaphore_wait(barrier, len(partners))

    def gather_copy(u, j):
        row, size = UNITS[u]
        v, q = r.cross, size // 4
        part = 32 if q == 48 else q // 2
        sems = (r.gsend.at[u, j], r.grecv.at[u, j])
        at = lambda shard, quarter, first=0, n=q: v.at[shard, rows_of(row + quarter * q + first, n), :]
        core, over_x, over_y, over_z = (dp, tc), (dp, tx), (pb[0], t), (pb[1], t)
        if j == 0:
            ref, to = v.at[t, pl.ds(row, size), :], core
        elif j == 1:
            ref, to = at(t, quad), over_x
        elif j == 3:
            ref, to = at(tx, quad), over_y
        elif j == 4:
            ref, to = at(tx, quad), over_z
        elif j == 5:
            ref, to = at(tx, quad), core
        elif j == 6:
            ref, to = at(tx, quad_y, part, q - part), over_z
        elif j == 7:
            ref, to = at(tx, quad_y), core
        elif j == 8:
            ref, to = at(tx, quad_z, 0, part), over_y
        elif j == 9:
            ref, to = at(tx, quad_z), core
        else:
            ref, to = at(tx, quad_d), core
        return Remote(ref, ref, *sems, to)

    GATHER = {0: ((), (1, 0)), 1: ((1,), (3, 4, 5)), 2: ((3,), (6, 7)), 3: ((4,), (8, 9)), 4: ((8, 6), (10,)),
              5: ((0,), ()), 6: ((5, 7, 9, 10), ())}

    def gather_step(u, step):
        arrived, onward = GATHER[step]
        for j in arrived:
            gather_copy(u, j).wait_recv()
        for j in onward:
            gather_copy(u, j).start()

    def gather_sent(us, js):
        for u in us:
            for j in js:
                gather_copy(u, j).wait_send()

    def view(n, shard, first=0, size=None):
        a, row, rows, _ = CHUNKS[n]
        return weights[a].at[slot_of(a, shard), rows_of(row + first, rows if size is None else size), :]

    def place(n, halves):
        first, size = 0, CHUNKS[n][2]
        for b in halves:
            size = size // 2
            first = first + b * size
        return first, size

    def result(n, halves):
        first, size = place(n, halves)
        return r.result[n].at[rows_of(first, size), :]

    flips = ((0, 1), (1, 0), (1, 1))
    turn = lambda b, f: b + f * (1 - 2 * b)
    along_z = [dp + f1 * (2 - 4 * z1) + f2 * (4 - 8 * z2) for f1, f2 in flips]

    count = iter(range(999))

    def plan_of(n):
        order, buffers = CHUNKS[n][3], iter(r.parts[n])
        halves, shards, stages, gathers = [], [tx, t] if "x" in order else [t], [], []

        def copy(src, dst, to):
            j = next(count)
            return Remote(src, dst, r.rsend.at[j], r.rrecv.at[j], to)

        def piece(shard, at):
            return view(n, shard, *place(n, at))

        for d in order:
            buf = next(buffers)
            if d == "x":
                stages.append(([copy(piece(tx, halves), buf.at[0], (dp, tx))], [(piece(t, halves), [buf.at[0]])]))
                shards = [t]
                continue
            if d == "q":
                mine, others = [z1, z2], [([turn(z1, f1), turn(z2, f2)], p) for (f1, f2), p in zip(flips, along_z)]
            else:
                b = "yzw".index(d)
                mine, others = [bit[b]], [([1 - bit[b]], pb[b])]
            m = len(others)
            stages.append((
                [copy(piece(k, halves + o), buf.at[m * i + j], (p, t)) for i, k in enumerate(shards) for j, (o, p) in enumerate(others)],
                [(piece(k, halves + mine), [buf.at[m * i + j] for j in range(m)]) for i, k in enumerate(shards)]))
            halves = halves + mine
            gathers.append((list(halves), [p for _, p in others]))
        back = [[copy(result(n, at), result(n, at), (p, t)) for p in ps] for at, ps in reversed(gathers)]
        more = [(copy(piece(t, halves), r.more[n].at[b - 3], (pb[b], t)), r.more[n].at[b - 3]) for b in range(3, bits)]
        far = [(td, tx)] if "x" in order else []
        core = [(copy(view(n, a), r.first[n].at[i], (dp, tc)), view(n, b), r.first[n].at[i]) for i, (a, b) in enumerate(far + [(tc, t)])]
        return SimpleNamespace(core=core, stages=stages, back=back, more=more, mine=piece(t, halves), result=result(n, halves))

    plans = [plan_of(n) for n in range(len(CHUNKS))]

    def out_copy(n):
        a, row, rows, _ = CHUNKS[n]
        return pltpu.make_async_copy(r.result[n], (r.own_out, r.cross_out, r.feed_out)[a].at[pl.ds(row, rows), :], r.osem.at[n])

    def start(copies):
        for d in copies:
            d.start()

    def sent_of(p):
        return [d for d, _, _ in p.core] + sum([copies for copies, _ in p.stages], []) + sum(p.back, [])

    def reduce_step(n, j):
        p = plans[n]
        m = len(p.core)
        if j == 0:
            start([d for d, _, _ in p.core])
        elif j <= m:
            copy, target, part = p.core[j - 1]
            copy.wait_recv()
            add_into(target, [part])
            if j == (1 if CHUNKS[n][3][0] == "x" else m):
                start(p.stages[0][0])
        elif j - m <= len(p.stages):
            copies, sums = p.stages[j - m - 1]
            for d in copies:
                d.wait_recv()
            last = j - m == len(p.stages)
            for target, parts in sums:
                add_into(target, parts, p.result if last and not p.more else None)
            if not last:
                start(p.stages[j - m][0])
                return
            for i, (copy, part) in enumerate(p.more):
                copy.start()
                copy.wait()
                add_into(p.mine, [part], p.result if i + 1 == len(p.more) else None)
            start(p.back[0])
        else:
            i = j - m - 1 - len(p.stages)
            for d in p.back[i]:
                d.wait_recv()
            if i + 1 < len(p.back):
                start(p.back[i + 1])
            else:
                out_copy(n).start()
                for d in sent_of(p)[:-len(p.back[-1])]:
                    d.wait_send()

    to = [(dp, tc), (dp, tx)] + [(p, t) for p in pb]

    small_stores = [pltpu.make_async_copy(r.sm.at[pl.ds(0, 2)], r.smo, r.esem.at[3]),
                    pltpu.make_async_copy(r.sm.at[2 + t], r.dgo, r.esem.at[4])]

    def small_step(j):
        if j:
            Remote(r.sm, r.smb.at[j - 1], r.ssend.at[j - 1], r.srecv.at[j - 1], to[j - 1]).wait()
            r.sm[...] = r.sm[...] + r.smb[j - 1]
        if j == len(to):
            for d in small_stores:
                d.start()
        if j < len(to):
            Remote(r.sm, r.smb.at[j], r.ssend.at[j], r.srecv.at[j], to[j]).start()

    places = iter(SCHEDULE)

    def run(todo):
        for e in todo:
            if e >= 1000:
                reduce_step((e - 1000) // 10, e % 10)
            elif e >= 200:
                small_step(e - 200)
            else:
                gather_step(e // 10, e % 10)

    def here():
        run(next(places))

    def take(count):
        return [next(places) for _ in range(count)]

    def hooks(s, todos, extra=None):
        for k, todo in enumerate(todos):
            more = (extra or {}).get(k)
            if todo or more:
                @pl.when(s == k)
                def _():
                    run(todo)
                    if more:
                        more()

    def over_x(j, src, dst):
        return Remote(src, dst, r.xsend.at[j], r.xrecv.at[j], (dp, tx))

    def to_core(j, src, dst):
        return Remote(src, dst, r.csend.at[j], r.crecv.at[j], (dp, tc))

    def half(start, h):
        return rows_of(start + 128 * h, 128)

    trade_cot, trade_rows = trade = [over_x(j, v.at[mine, :], v.at[mine, :]) for j, v in enumerate((r.cot, r.rows1))]
    trade_n1, trade_n3 = ([over_x(2 + 2 * j + h, v.at[half(256 * x, h), :], v.at[half(256 * x, h), :]) for h in range(2)]
                          for j, v in enumerate((r.n1, r.n3)))
    give_lo, give_gn1 = give = [over_x(6 + j, r.out.at[i], r.arrived.at[i]) for j, i in enumerate((1, 3))]
    give_s1, give_gn = ([over_x(8 + 2 * j + h, r.out.at[i, half(0, h), :], r.arrived.at[i, half(0, h), :]) for h in range(2)]
                        for j, i in enumerate((0, 2)))
    core_own, core_feed, core_tab = (to_core(j, v.at[c], v.at[c]) for j, v in enumerate((r.own, r.feed, r.btab)))
    for d in key_loads:
        d.wait()
    gather_step(0, 0)
    start(trade_n1)
    for d in self_loads:
        d.wait()
    core_own.start()
    core_tab.start()
    for d in query_loads:
        d.wait()
    gather_step(1, 0)
    for d in feed_loads:
        d.wait()
    core_feed.start()

    def bias_of(f, i):
        return pltpu.roll(jnp.broadcast_to(r.btab[f, i:i + 1, :], (256, 256)), 0, 1, stride=1, stride_axis=0)

    def allowed(e):
        return (ji <= ii) & (ji < r.lengths[2 * e + c])

    lane = lax.broadcasted_iota(jnp.int32, (1, 128), 1)
    low, high = lane < 64, lane >= 64

    def of_keys(a):
        wide = jnp.concatenate([a, jnp.zeros((a.shape[0], 64), a.dtype)], axis=1)
        return [jnp.where(low, wide[:, 0:128], 0), jnp.where(high, wide[:, 0:128], 0), jnp.where(low, wide[:, 128:256], 0)]

    def of_values(a):
        wide = jnp.concatenate([jnp.zeros((a.shape[0], 64), a.dtype), a], axis=1)
        return [jnp.where(high, wide[:, 0:128], 0), jnp.where(low, wide[:, 128:256], 0), jnp.where(high, wide[:, 128:256], 0)]

    key_lanes = (slice(0, 128), slice(0, 128), slice(128, 256))
    value_lanes = (slice(128, 256), slice(256, 384), slice(256, 384))

    def columns(e):
        return pl.ds(pl.multiple_of(256 * e, 256), 256)

    def project_memory(shard):
        w = r.cross.at[shard, pl.ds(0, 384), :]

        def block(i, _):
            at = rows_of(i * 256, 256)
            r.kv[shard, at, :] = mm(r.mem[at, :], w[...], NT).astype(BF)
            return 0
        lax.fori_loop(0, 4, block, 0)
        for i in range(4):
            r.kvT[shard, :, 256 * i:256 * i + 256] = mm(w[...], r.mem[256 * i:256 * i + 256, :], NT).astype(BF)

    def near_self():
        core_own.wait_recv()
        core_tab.wait_recv()

    def near_memory():
        memory_load.wait()
        valid = r.mmask[pl.ds(t, 1), :]
        r.mask2[...] = jnp.broadcast_to(jnp.where(valid == 1, 0.0, MASKED).astype(F32), (128, 1024)).T
        project_memory(t)
        here()
        gather_step(0, 5)
        project_memory(tc)

    def self_forward(s, _):
        hooks(s, turns, {1: near_self})
        e, f = x, c + s * (1 - 2 * c)
        k = 2 * e + f
        rows = r.n1.at[rows_of(256 * e, 256), :]
        r.q1[k] = (mm(rows[...], r.own[f, 0:192, :], NT) * 0.125).astype(BF)
        r.kv1[k] = mm(rows[...], r.own[f, 192:576, :], NT).astype(BF)
        q = of_keys(r.q1[k])
        r.kvT1[k] = mm(r.own[f, 192:576, :], rows[...], NT).astype(BF)
        for i in range(3):
            scores = jnp.where(allowed(e), mm(r.kv1[k, :, key_lanes[i]], q[i], NT) + bias_of(f, i), MASKED)
            most = jnp.max(scores, axis=0, keepdims=True)
            p = jnp.exp(scores - most)
            total = jnp.sum(p, axis=0, keepdims=True)
            o = mm(r.kvT1[k, 192 + 64 * i:256 + 64 * i, :], p.astype(BF))
            r.mix1[f, 64 * i:64 * i + 64, columns(e)] = (o / total).astype(BF)
            r.lse[k, i:i + 1, :] = most + jnp.log(total)
        return 0

    def self_far(h):
        n, e, cols = 128 * (h + 1), 1 - x, slice(128 * h, 128 * h + 128)

        def turn(i, _):
            f = c + i * (1 - 2 * c)
            k = 2 * e + f
            rows = r.n1.at[half(256 * e, h), :]
            r.q1[k, cols, :] = (mm(rows[...], r.own[f, 0:192, :], NT) * 0.125).astype(BF)
            r.kv1[k, cols, :] = mm(rows[...], r.own[f, 192:576, :], NT).astype(BF)
            r.kvT1[k, :, cols] = mm(r.own[f, 192:576, :], rows[...], NT).astype(BF)
            q = of_keys(r.q1[k, cols, :])
            for j in range(3):
                scores = mm(r.kv1[k, 0:n, key_lanes[j]], q[j], NT) + bias_of(f, j)[0:n, cols]
                scores = jnp.where(allowed(e)[0:n, cols], scores, MASKED)
                most = jnp.max(scores, axis=0, keepdims=True)
                p = jnp.exp(scores - most)
                total = jnp.sum(p, axis=0, keepdims=True)
                o = mm(r.kvT1[k, 192 + 64 * j:256 + 64 * j, 0:n], p.astype(BF))
                r.mix1[f, 64 * j:64 * j + 64, pl.ds(pl.multiple_of(256 * e + 128 * h, 128), 128)] = (o / total).astype(BF)
                r.lse[k, j:j + 1, cols] = most + jnp.log(total)
            return 0

        lax.fori_loop(0, 2, turn, 0)
        r.out[0, cols, :] = self_out(pl.ds(pl.multiple_of(256 * e + 128 * h, 128), 128)).astype(BF)
        give_s1[h].start()

    def self_out(at):
        return mm(r.mix1[0, :, at].T, r.own[0, 576:768, :]) + mm(r.mix1[1, :, at].T, r.own[1, 576:768, :])

    turns = take(2)
    lax.fori_loop(0, 2, self_forward, 0)
    here()
    near_memory()
    for h in range(2):
        here()
        trade_n1[h].wait_recv()
        self_far(h)
    gather_step(2, 0)
    cotangent_load.wait()
    trade_cot.start()
    r.s1[...] = r.s0[...] + self_out(columns(x))
    here()
    project_memory(tx)
    here()
    gather_step(0, 6)
    project_memory(td)
    here()
    for d in give_s1:
        d.wait_recv()
    x1 = r.s1[...] + r.arrived[0].astype(F32)
    r.s1[...] = x1
    r.n2[...] = (x1 * inverse_of(x1) * g_cross).astype(BF)
    gather_step(1, 5)

    def cross_scores(shard, i, b, q):
        at = slice(256 * b, 256 * b + 256)
        return mm(r.kv[shard, at, key_lanes[i]], q, NT) + jnp.concatenate([r.mask2[at, :]] * 2, axis=1)

    def cross_forward(s, _):
        hooks(s, turns_1, {3: lambda: gather_step(1, 6)})
        k = fwd_shard(s)
        r.q2[k] = (mm(r.n2[...], r.cross[k, 384:576, :], NT) * 0.125).astype(BF)
        q = of_keys(r.q2[k])
        for i in range(3):
            ss = [cross_scores(k, i, b, q[i]) for b in range(4)]
            most = jnp.max(jnp.maximum(jnp.maximum(ss[0], ss[1]), jnp.maximum(ss[2], ss[3])), axis=0, keepdims=True)
            total, o = 0.0, 0.0
            for b in range(4):
                p = jnp.exp(ss[b] - most)
                total = total + jnp.sum(p, axis=0, keepdims=True)
                o = o + mm(r.kvT[k, 192 + 64 * i:256 + 64 * i, 256 * b:256 * b + 256], p.astype(BF))
            r.mix2[k, 64 * i:64 * i + 64, :] = (o / total).astype(BF)
            r.lse[4 + k, i:i + 1, :] = most + jnp.log(total)
        return 0

    turns_1 = take(4)
    lax.fori_loop(0, 4, cross_forward, 0)
    here()
    gather_step(2, 5)
    gather_step(2, 6)
    x2 = r.s1[...]
    for k in range(4):
        x2 = x2 + mm(r.mix2[k].T, r.cross[k, 576:768, :])
    r.s2[...] = x2
    r.n3[mine, :] = (x2 * inverse_of(x2) * g_hid).astype(BF)
    start(trade_n3)
    r.sums[mine, :] = x2
    r.sums[other, :] = jnp.zeros_like(x2)
    r.grads[...] = jnp.zeros_like(r.grads)
    core_feed.wait_recv()

    def feed(f, first, n):
        at = rows_of(first, n)
        lanes = pl.ds(pl.multiple_of(first, 128), n)
        rows, cot = r.n3.at[at, :], r.cot.at[at, :]
        for i in range(3):
            cs = slice(256 * i, 256 * i + 256)
            v = mm(rows[...], r.feed[f, 0:768, cs])
            ga = mm(cot[...], r.feed[f, 768 + 256 * i:1024 + 256 * i, :], NT)
            phi = 0.5 * (1.0 + lax.erf(v * np.float32(1 / math.sqrt(2))))
            act = (v * phi).astype(BF)
            slope = phi + v * (jnp.exp(-0.5 * v * v) * np.float32(1 / math.sqrt(2 * math.pi)))
            r.act[0:n, cs] = act
            r.actT[f, cs, lanes] = act.T
            r.gb[f, at, cs] = (slope * ga).astype(BF)
        r.sums[at, :] += mm(r.act[0:n, :], r.feed[f, 768:1536, :])
        r.grads[at, :] += mm(r.gb[f, at, :], r.feed[f, 0:768, :], NT)

    def feed_both(first, n):
        def turn(i, _):
            feed(c + i * (1 - 2 * c), first, n)
            return 0
        lax.fori_loop(0, 2, turn, 0)

    here()
    feed_both(256 * x, 256)
    here()
    trade_cot.wait_recv()
    for h in range(2):
        if h:
            here()
        trade_n3[h].wait_recv()
        feed_both(256 - 256 * x + 128 * h, 128)
        r.out[2, 128 * h:128 * h + 128, :] = r.grads[half(256 - 256 * x, h), :].astype(BF)
        give_gn[h].start()
    r.out[1] = r.sums[other, :].astype(BF)
    give_lo.start()
    here()
    core_feed.wait_send()

    for i in range(3):
        n3T = r.n3[:, 256 * i:256 * i + 256].T
        for f in range(2):
            r.feed[f, 256 * i:256 * i + 256, :] = mm(n3T, r.gb[f]).astype(BF)
        here()
    for i in range(3):
        for f in range(2):
            r.feed[f, 768 + 256 * i:1024 + 256 * i, :] = mm(r.actT[f, 256 * i:256 * i + 256, :], r.cot[...]).astype(BF)
        here()
    for d in give_gn:
        d.wait_recv()
    d, gain = norm_back(x2, inverse_of(x2), g_hid, r.grads[mine, :] + r.arrived[2].astype(F32))

    def put_small(row, value):
        for i in range(3):
            at = 3 * row + i
            r.sm[at // 8, at % 8:at % 8 + 1, :] = value[:, 256 * i:256 * i + 256]

    r.sm[...] = jnp.zeros_like(r.sm)
    put_small(4, gain)
    r.gst[...] = r.cot[mine, :].astype(F32) + d
    gather_sent(range(3), (0, 1, 3, 4, 5, 6, 7, 8, 9, 10))
    here()
    r.rows2[...] = r.gst[...].astype(BF)
    r.acc[...] = jnp.zeros_like(x2)

    def cross_backward(s, _):
        hooks(s, turns_3)
        k = bwd_shard(s)
        rw = r.rows2[...]
        w = r.cross[k, 576:768, :]
        G = mm(rw, w, NT).astype(BF)
        GT = mm(w, rw, NT).astype(BF)
        r.cross[k, 576:768, :] = mm(r.mix2[k], rw).astype(BF)
        q, g = of_keys(r.q2[k]), of_values(G)
        inner = [jnp.sum(r.mix2[k, 64 * i:64 * i + 64, :].astype(F32) * GT[64 * i:64 * i + 64, :].astype(F32), axis=0, keepdims=True)
                 for i in range(3)]
        dqs = [0.0, 0.0, 0.0]
        for b in range(4):
            if b == 2:
                hooks(s, turns_m)
            at = slice(256 * b, 256 * b + 256)
            dks, dvs = [], []
            for i in range(3):
                p = jnp.exp(cross_scores(k, i, b, q[i]) - r.lse[4 + k, i:i + 1, :])
                gs = (p * (mm(r.kv[k, at, value_lanes[i]], g[i], NT) - inner[i])).astype(BF)
                dqs[i] = dqs[i] + mm(r.kvT[k, 64 * i:64 * i + 64, at], gs)
                dks.append(mm(gs, q[i]))
                dvs.append(mm(p.astype(BF), g[i]))
            r.kv[k, at, 0:128] = (dks[0] + dks[1]).astype(BF)
            r.kv[k, at, 128:256] = (dks[2] + dvs[0]).astype(BF)
            r.kv[k, at, 256:384] = (dvs[1] + dvs[2]).astype(BF)
        dqs = [(d * 0.125).astype(BF) for d in dqs]
        r.kvT[k] = r.kv[k].T
        dqT = jnp.concatenate(dqs, axis=0)
        r.acc[...] += mm(dqT.T, r.cross[k, 384:576, :])
        r.cross[k, 384:576, :] = mm(dqT, r.n2[...]).astype(BF)
        return 0

    turns_3, turns_m = take(4), take(4)
    lax.fori_loop(0, 4, cross_backward, 0)
    here()
    x1 = r.s1[...]
    d, gain = norm_back(x1, inverse_of(x1), g_cross, r.acc[...])
    put_small(3, gain)
    x1 = r.gst[...] + d
    r.gst[...] = x1
    r.rows1[mine, :] = x1.astype(BF)
    trade_rows.start()
    here()
    give_lo.wait_recv()
    r.lov[...] = (r.sums[mine, :] + r.arrived[1].astype(F32)).astype(BF)
    stores = [pltpu.make_async_copy(a, b, r.esem.at[i]) for i, (a, b) in enumerate(((r.lov, r.lo), (r.gmv, r.gmem), (r.gtv, r.gtok)))]
    stores[0].start()

    def memory_grad(i, _):
        at = rows_of(i * 256, 256)
        total = 0.0
        for k in range(4):
            total = total + mm(r.kv[k, at, :], r.cross[k, 0:384, :])
        r.gmv[at, :] = total.astype(BF)
        return 0

    lax.fori_loop(0, 4, memory_grad, 0)
    stores[1].start()
    here()

    def memory_weights(s, _):
        hooks(s, turns_4)
        k = bwd_shard(s)

        def block(i, _):
            at = rows_of(i * 192, 192)
            r.cross[k, at, :] = mm(r.kvT[k, at, :], r.mem[...]).astype(BF)
            return 0
        lax.fori_loop(0, 2, block, 0)
        return 0

    turns_4 = take(4)
    lax.fori_loop(0, 4, memory_weights, 0)
    here()
    r.grads[...] = jnp.zeros_like(r.grads)

    def self_backward(s, _):
        hooks(s, turns_5, {2: trade_rows.wait_recv})
        e, f = item_shard(s)
        k = 2 * e + f
        here_rows = rows_of(256 * e, 256)
        rw = r.rows1[here_rows, :]
        w = r.own[f, 576:768, :]
        G = mm(rw, w, NT).astype(BF)
        GT = mm(w, rw, NT).astype(BF)
        flip = (ji + ii == 255).astype(BF)
        q, g = of_keys(r.q1[k]), of_values(G)
        dqs, dks, dvs = [], [], []
        for i in range(3):
            gT = GT[64 * i:64 * i + 64, :]
            inner = jnp.sum(r.mix1[f, 64 * i:64 * i + 64, columns(e)].astype(F32) * gT.astype(F32), axis=0, keepdims=True)
            scores = jnp.where(allowed(e), mm(r.kv1[k, :, key_lanes[i]], q[i], NT) + bias_of(f, i), MASKED)
            p = jnp.exp(scores - r.lse[k, i:i + 1, :])
            gs = (p * (mm(r.kv1[k, :, value_lanes[i]], g[i], NT) - inner)).astype(BF)
            dvs.append(mm(p.astype(BF), g[i]))
            dks.append(mm(gs, q[i]))
            dqs.append((mm(r.kvT1[k, 64 * i:64 * i + 64, :], gs) * 0.125).astype(BF))
            shifted = pltpu.roll(mm(flip, gs), 1, 1, stride=1, stride_axis=0)
            r.sm[2 + 2 * x + f, i:i + 1, :] += jnp.sum(shifted, axis=0, keepdims=True)
        dqT = jnp.concatenate(dqs, axis=0)
        dkv = jnp.concatenate([dks[0] + dks[1], dks[2] + dvs[0], dvs[1] + dvs[2]], axis=1).astype(BF)
        r.gT[f, 0:192, columns(e)] = dqT
        r.gT[f, 192:576, columns(e)] = dkv.T
        r.grads[here_rows, :] += mm(dqT.T, r.own[f, 0:192, :]) + mm(dkv, r.own[f, 192:576, :])
        return 0

    turns_5 = take(4)
    lax.fori_loop(0, 4, self_backward, 0)
    r.out[3] = r.grads[other, :].astype(BF)
    give_gn1.start()
    core_own.wait_send()
    here()
    for f in range(2):
        r.own[f, 0:384, :] = mm(r.gT[f, 0:384, :], r.n1[...]).astype(BF)
    here()
    for f in range(2):
        r.own[f, 384:576, :] = mm(r.gT[f, 384:576, :], r.n1[...]).astype(BF)
        r.own[f, 576:768, :] = mm(r.mix1[f], r.rows1[...]).astype(BF)
    here()
    for d in trade + trade_n1 + trade_n3 + give + give_s1 + give_gn + [core_tab]:
        d.wait_send()
    give_gn1.wait_recv()
    x0 = r.s0[...]
    d, gain = norm_back(x0, inverse_of(x0), g_self, r.grads[mine, :] + r.arrived[3].astype(F32))
    put_small(2, gain)
    g0 = r.gst[...] + d
    r.gtv[...] = g0.astype(BF)
    stores[2].start()
    put_small(0, jnp.sum(jnp.where(tagged(), 0.0, g0), axis=0, keepdims=True))
    put_small(1, jnp.sum(jnp.where(tagged(), g0, 0.0), axis=0, keepdims=True))
    here()
    here()
    for j in range(6, len(to) + 1):
        small_step(j)
    for n, p in enumerate(plans):
        for d in p.back[-1]:
            d.wait_send()
        out_copy(n).wait()
    for d in stores + small_stores:
        d.wait()


def layer(bits, ins):
    S = jax.ShapeDtypeStruct
    V, A, M = (pl.BlockSpec(memory_space=s) for s in (pltpu.VMEM, pl.ANY, pltpu.SMEM))
    vm = pltpu.VMEM
    inputs = dict(tok_in=A, mem_in=A, cot_in=A, lengths=M, mmask=V, tags=V, emb=V, gain1=V, gain2=V, gain3=V, tab=V,
                  sq=A, sk=A, sv=A, so=A, cq=A, ck=A, cv=A, co=A, hin=A, hout=A)
    wide, square = (256, 768), (768, 768)
    out = dict(lo=S(wide, BF), gtok=S(wide, BF), gmem=S((1024, 768), BF), smo=S((2, 8, 256), F32), dgo=S((8, 256), F32),
               own_out=S(square, BF), cross_out=S(square, BF), feed_out=S((1536, 768), BF))
    out_specs = [A] * len(out)
    sizes = [n for _, _, n, _ in CHUNKS]

    def parts_of(n, order):
        shards, buffers = 2 if "x" in order else 1, []
        for d in order:
            if d == "x":
                shards = 1
                buffers.append(vm((1, n, 768), BF))
            else:
                n = n // 4 if d == "q" else n // 2
                buffers.append(vm((shards * (3 if d == "q" else 1), n, 768), BF))
        return buffers

    both = (512, 768)
    scratch = dict(
        own=vm((2, 768, 768), BF), cross=vm((4, 768, 768), BF), feed=vm((2, 1536, 768), BF),
        tok=vm(wide, BF), cot=vm(both, BF), mem=vm((1024, 768), BF), n1=vm(both, BF), n3=vm(both, BF), rows1=vm(both, BF),
        out=vm((4, 256, 768), BF), arrived=vm((4, 256, 768), BF),
        s0=vm(wide, F32), s1=vm(wide, F32), s2=vm(wide, F32), gst=vm(wide, F32), acc=vm(wide, F32), sums=vm(both, F32), grads=vm(both, F32),
        n2=vm(wide, BF), rows2=vm(wide, BF), act=vm(wide, BF), actT=vm((2, 768, 512), BF), gb=vm((2, 512, 768), BF),
        q1=vm((4, 256, 192), BF), kv1=vm((4, 256, 384), BF), kvT1=vm((4, 384, 256), BF), q2=vm((4, 256, 192), BF), gT=vm((2, 576, 512), BF),
        kv=vm((4, 1024, 384), BF), kvT=vm((4, 384, 1024), BF), mix1=vm((2, 192, 512), BF), mix2=vm((4, 192, 256), BF),
        lse=vm((8, 8, 256), F32), mask2=vm((1024, 128), F32), tagv=vm((256, 128), F32), btab=vm((2, 8, 256), F32),
        sm=vm((6, 8, 256), F32), smb=vm((2 + bits, 6, 8, 256), F32), gmv=vm((1024, 768), BF), lov=vm(wide, BF), gtv=vm(wide, BF),
    )
    first = [vm((2 if "x" in order else 1, n, 768), BF) for _, _, n, order in CHUNKS]
    parts = [parts_of(n, order) for _, _, n, order in CHUNKS]
    results = [vm((n, 768), BF) for n in sizes]
    more = [vm((bits - 3, n // 8, 768), BF) for n in sizes] if bits > 3 else []
    dma = pltpu.SemaphoreType.DMA
    copies = 0
    for _, _, _, order in CHUNKS:
        shards = 2 if "x" in order else 1
        copies += shards + bits - 3
        for d in order:
            if d == "x":
                shards, copies = 1, copies + 1
            else:
                copies += (shards + 1) * (3 if d == "q" else 1)
    sems = dict(gsend=dma((3, 11)), grecv=dma((3, 11)), xsend=dma((12,)), xrecv=dma((12,)), csend=dma((3,)), crecv=dma((3,)), rsend=dma((copies,)), rrecv=dma((copies,)), lsem=dma((13,)), osem=dma((len(CHUNKS),)),
                esem=dma((5,)), ssend=dma((2 + bits,)), srecv=dma((2 + bits,)))
    names = list(inputs) + list(out) + list(scratch) + list(sems)

    def kernel(*refs):
        r = SimpleNamespace(**dict(zip(names, refs)))
        rest = iter(refs[len(names):])
        r.parts = [[next(rest) for _ in p] for p in parts]
        r.result = [next(rest) for _ in results]
        r.more = [next(rest) for _ in more]
        r.first = [next(rest) for _ in first]
        layer_kernel(bits, r)

    return pl.pallas_call(
        kernel, out_shape=list(out.values()), in_specs=list(inputs.values()), out_specs=out_specs,
        scratch_shapes=list(scratch.values()) + list(sems.values()) + sum(parts, []) + results + more + first,
        compiler_params=pltpu.CompilerParams(collective_id=0, has_side_effects=True, vmem_limit_bytes=VMEM_LIMIT),
    )(*ins)


def finish_kernel(lo, gtok, gmem, smo, dgo, own, cross, feed,
                  o_lo, o_gtok, o_gmem, o_emb, o_g1, o_g2, o_g3, o_sq, o_sk, o_sv, o_so, o_pb, o_cq, o_ck, o_cv, o_co, o_hin, o_hout):
    o_lo[...] = lo[...]
    o_gtok[...] = gtok[...]
    o_gmem[...] = gmem[...]
    for i, o in enumerate((o_sq, o_sk, o_sv, o_so)):
        o[...] = own[192 * i:192 * i + 192, :].astype(F32)
    for i, o in enumerate((o_ck, o_cv, o_cq, o_co)):
        o[...] = cross[192 * i:192 * i + 192, :].astype(F32)
    o_hin[...] = feed[0:768, :].astype(F32)
    o_hout[...] = feed[768:1536, :].astype(F32)

    @pl.when(pl.program_id(0) == 0)
    def _():
        def small(row):
            return jnp.concatenate([smo[(3 * row + i) // 8, (3 * row + i) % 8:(3 * row + i) % 8 + 1, :] for i in range(3)], axis=1)
        o_emb[0:1, :] = small(0)
        o_emb[1:2, :] = small(1)
        o_g1[...] = small(2).reshape(768)
        o_g2[...] = small(3).reshape(768)
        o_g3[...] = small(4).reshape(768)
        total = lax.dot_general(dgo[...], bucket_onehot().astype(F32), NT, precision=lax.Precision.HIGHEST, preferred_element_type=F32)
        o_pb[...] = total[0:3, :]


def finish(args):
    S = jax.ShapeDtypeStruct
    n = 2
    cut = lambda rows: pl.BlockSpec((rows, 768 // n), lambda i: (0, i))
    full = lambda *s: pl.BlockSpec(s, lambda i: (0,) * len(s))
    flat, square = S((192, 768), F32), S((768, 768), F32)
    shapes = [S((256, 768), BF), S((256, 768), BF), S((1024, 768), BF), S((2, 768), F32)] + [S((768,), F32)] * 3
    shapes += [flat] * 4 + [S((3, 32), F32)] + [flat] * 4 + [square, square]
    ends = [cut(256), cut(256), cut(1024)]
    in_specs = ends + [full(2, 8, 256), full(8, 256), cut(768), cut(768), cut(1536)]
    out_specs = ends + [full(2, 768)] + [full(768)] * 3 + [cut(192)] * 4 + [full(3, 32)] + [cut(192)] * 4
    out_specs += [cut(768), cut(768)]
    return pl.pallas_call(finish_kernel, grid=(n,), out_shape=shapes, in_specs=in_specs, out_specs=out_specs,
                          compiler_params=pltpu.CompilerParams(vmem_limit_bytes=VMEM_LIMIT))(*args)


def per_device(bits, tokens, memory, cotangent, lengths, memory_mask, token_tags, embedding, gain_self, gain_cross, gain_hidden,
               self_query, self_key, self_value, self_output, position_bias, cross_query, cross_key, cross_value,
               cross_output, hidden_in, hidden_out):
    parts = layer(bits, (
        tokens[0], memory[0], cotangent[0], lengths, memory_mask, token_tags, embedding, gain_self, gain_cross, gain_hidden, position_bias.T,
        self_query.T, self_key.T, self_value.T, self_output, cross_query.T, cross_key.T, cross_value.T, cross_output, hidden_in, hidden_out))
    lo, gtok, gmem, g_emb, g1, g2, g3, sq, sk, sv, so, pb, cq, ck, cv, co, hin, hout = finish(parts)
    return (lo[None], gtok[None], gmem[None], g_emb, g1, g2, g3, sq.T, sk.T, sv.T, so, pb.T, cq.T, ck.T, cv.T, co, hin, hout)


def solution(mesh):
    bits = int(math.log2(mesh.shape["dp"]))
    item = P(("dp", "tensor"), None, None)
    col, row, rep = P(None, "tensor"), P("tensor", None), P()
    in_specs = (item, item, item, P("dp"), P("dp", None), P(("dp", "tensor"), None), rep, rep, rep, rep,
                col, col, col, row, col, col, col, col, row, col, row)
    out_specs = (item, item, item, rep, rep, rep, rep, col, col, col, row, col, col, col, col, row, col, row)
    return jax.shard_map(lambda *a: per_device(bits, *a), mesh=mesh, in_specs=in_specs, out_specs=out_specs, check_vma=False)
```
